32 devices in a mesh: img: 4 (over x, core), exp: 8 (over z, y).
Axes of the slice: x: 2, y: 2, z: 4, core: 2. Of those that a mesh axis runs over, the one named last changes fastest.
Arguments:
- context: bfloat16 [64, 256, 1024], P(('img', 'exp')), may hold values from -1.5 to 1.5
- residual: bfloat16 [64, 256, 1024], P(('img', 'exp')), may hold values from -1.5 to 1.5
- cotangent: bfloat16 [64, 256, 1024], P(('img', 'exp')), may hold values from -6 to 6
- proj_weight: bfloat16 [1024, 1024], P('img'), may hold values from -0.1875 to 0.1875
- slot_params: bfloat16 [1024, 16], replicated, may hold values from -0.1875 to 0.1875
- expert_in: bfloat16 [16, 1024, 4096], P('exp', None, 'img'), may hold values from -0.1875 to 0.1875
- expert_out: bfloat16 [16, 4096, 1024], P('exp', 'img'), may hold values from -0.09375 to 0.09375
Outputs:
- grad_context: bfloat16 [64, 256, 1024], P(('img', 'exp'))
- grad_residual: bfloat16 [64, 256, 1024], P(('img', 'exp'))
- grad_proj: float32 [1024, 1024], P('img')
- grad_slots: float32 [1024, 16], replicated
- grad_expert_in: bfloat16 [16, 1024, 4096], P('exp', None, 'img')
- grad_expert_out: bfloat16 [16, 4096, 1024], P('exp', 'img')
The draws below stay inside these ranges and needn't reach their ends.
All inputs are finite; a program needn't handle non-finite values.
Results may differ from the reference program's by a relative error of at most 0.025.
Values may be sent and summed in bfloat16 or wider, within the bound.
No kernel may reach another device: no remote copies, remote signals or barrier semaphores. Data moves between devices by JAX's collectives and lax.ppermute only.
A program may use at most 128 MiB of HBM per device.

```python
import math
import jax
import jax.numpy as jnp
from jax import lax

D = 1024
FF = 4096
TOK = 256
EXPERTS = 16
IMAGES = 64


def draw_context(key, part):
    folded = jax.random.fold_in(key, 7101)
    sample = jnp.clip(0.25 * jax.random.normal(folded, (IMAGES, TOK, D), jnp.float32), -1.5, 1.5)
    return sample.astype(jnp.bfloat16)


def draw_residual(key, part):
    folded = jax.random.fold_in(key, 7202)
    sample = jnp.clip(0.25 * jax.random.normal(folded, (IMAGES, TOK, D), jnp.float32), -1.5, 1.5)
    return sample.astype(jnp.bfloat16)


def levels(key, extent, shards, smallest, largest):
    level = 1.0
    for axis_at, shards_of in shards:
        heights = jax.random.uniform(jax.random.fold_in(jax.random.fold_in(key, 6), axis_at), (shards_of,), jnp.float32, smallest / len(shards), largest / len(shards))
        level = level * jnp.repeat(jnp.exp(heights), extent[axis_at] // shards_of).reshape((-1,) + (1,) * (len(extent) - 1 - axis_at))
    return level


def scatter_about(stream_key, shape, deviation, reach, split=(), held_as=jnp.bfloat16):
    gain = levels(stream_key, shape, split, -0.22, 0.18) if split else 1.0
    drawn = jax.random.normal(stream_key, shape, jnp.float32) * deviation * gain
    return jnp.minimum(jnp.maximum(drawn, -reach), reach).astype(held_as)


def setup_inputs(seed: int = 0) -> dict:
    splits = jax.random.split(jax.random.key(seed), 8)
    context = draw_context(jax.random.fold_in(splits[7], 71), 0)
    residual = draw_residual(jax.random.fold_in(splits[7], 71), 0)
    cotangent = scatter_about(splits[2], (IMAGES, TOK, D), 1.0, 6.0, ((0, 32),))
    proj_weight = scatter_about(splits[3], (D, D), D ** -0.5, 0.1875, ((0, 4),))
    slot_params = scatter_about(splits[4], (D, EXPERTS), D ** -0.5, 0.1875)
    expert_in = scatter_about(splits[5], (EXPERTS, D, FF), D ** -0.5, 0.1875, ((0, 8), (2, 4)))
    expert_out = scatter_about(splits[6], (EXPERTS, FF, D), FF ** -0.5, 0.09375, ((0, 8), (1, 4)))
    return dict(context=context, residual=residual, cotangent=cotangent, proj_weight=proj_weight, slot_params=slot_params, expert_in=expert_in, expert_out=expert_out)


logit_scale = 48.0
epsilon = 1e-06

def gelu_back(pre, upstream):
    return jax.vjp(jax.nn.gelu, pre)[1](upstream)[0]

def reference(context, residual, cotangent, proj_weight, slot_params, expert_in, expert_out):
    width = context.shape[2]
    images, tokens = (context.shape[0], context.shape[1])
    factor = logit_scale / math.sqrt(width)
    flat_ctx = context.reshape(images * tokens, width)
    stream = (residual.reshape(-1, width).astype(jnp.float32) + jnp.dot(flat_ctx, proj_weight, preferred_element_type=jnp.float32)).astype(jnp.bfloat16)
    stream32 = stream.astype(jnp.float32)
    inverse = lax.rsqrt(lax.optimization_barrier(jnp.mean(stream32 * stream32, axis=-1, keepdims=True)) + epsilon)
    normed32 = stream32 * inverse
    normed = normed32.astype(jnp.bfloat16)
    params32 = slot_params.astype(jnp.float32)
    slot_norm = jnp.sqrt(lax.optimization_barrier(jnp.sum(params32 * params32, axis=0, keepdims=True)) + epsilon)
    unit32 = params32 / slot_norm
    unit = unit32.astype(jnp.bfloat16)
    logits = factor * jnp.dot(normed, unit, preferred_element_type=jnp.float32)
    logits = logits.reshape(images, tokens, -1)
    expo = jnp.exp(logits)
    dispatch32 = expo / lax.optimization_barrier(jnp.sum(expo, axis=1, keepdims=True))
    combine32 = expo / lax.optimization_barrier(jnp.sum(expo, axis=2, keepdims=True))
    dispatch = dispatch32.astype(jnp.bfloat16)
    combine = combine32.astype(jnp.bfloat16)
    normed3 = normed.reshape(images, tokens, width)
    slot_in = jnp.einsum('bms,bmd->bsd', dispatch.astype(jnp.float32), normed3.astype(jnp.float32)).astype(jnp.bfloat16)
    slot_major = jnp.transpose(slot_in, (1, 0, 2))

    def forward_one(items):
        rows, first, second = items
        pre = jnp.dot(rows, first, preferred_element_type=jnp.float32)
        act = jax.nn.gelu(pre).astype(jnp.bfloat16)
        return jnp.dot(act, second, preferred_element_type=jnp.float32).astype(jnp.bfloat16)
    slot_out = jnp.transpose(lax.map(forward_one, (slot_major, expert_in, expert_out)), (1, 0, 2))
    upstream3 = cotangent.astype(jnp.float32)
    grad_slot_out = jnp.einsum('bms,bmd->bsd', combine.astype(jnp.float32), upstream3).astype(jnp.bfloat16)
    grad_combine = jnp.einsum('bmd,bsd->bms', upstream3, slot_out.astype(jnp.float32))
    grad_major = jnp.transpose(grad_slot_out, (1, 0, 2))

    def backward_one(items):
        rows, first, second, grads = items
        pre = jnp.dot(rows, first, preferred_element_type=jnp.float32)
        act = jax.nn.gelu(pre).astype(jnp.bfloat16)
        grad_act = jnp.dot(grads, second.T, preferred_element_type=jnp.float32)
        grad_pre = gelu_back(pre, grad_act).astype(jnp.bfloat16)
        grad_second = jnp.dot(act.T, grads, preferred_element_type=jnp.float32).astype(jnp.bfloat16)
        grad_first = jnp.dot(rows.T, grad_pre, preferred_element_type=jnp.float32).astype(jnp.bfloat16)
        grad_rows = jnp.dot(grad_pre, first.T, preferred_element_type=jnp.float32).astype(jnp.bfloat16)
        return (grad_first, grad_second, grad_rows)
    grad_expert_in, grad_expert_out, grad_rows = lax.map(backward_one, (slot_major, expert_in, expert_out, grad_major))
    grad_slot_in = jnp.transpose(grad_rows, (1, 0, 2))
    grad_dispatch = jnp.einsum('bmd,bsd->bms', normed3.astype(jnp.float32), grad_slot_in.astype(jnp.float32))
    grad_logits32 = combine32 * (grad_combine - lax.optimization_barrier(jnp.sum(combine32 * grad_combine, axis=2, keepdims=True)))
    grad_logits32 = grad_logits32 + dispatch32 * (grad_dispatch - lax.optimization_barrier(jnp.sum(dispatch32 * grad_dispatch, axis=1, keepdims=True)))
    grad_logits = grad_logits32.astype(jnp.bfloat16).reshape(images * tokens, -1)
    grad_normed = jnp.einsum('bms,bsd->bmd', dispatch.astype(jnp.float32), grad_slot_in.astype(jnp.float32)).reshape(images * tokens, width)
    grad_normed = grad_normed + factor * jnp.dot(grad_logits, unit.T, preferred_element_type=jnp.float32)
    grad_unit = factor * jnp.dot(normed.T, grad_logits, preferred_element_type=jnp.float32)
    grad_slots = (grad_unit - unit32 * lax.optimization_barrier(jnp.sum(unit32 * grad_unit, axis=0, keepdims=True))) / slot_norm
    upstream = cotangent.reshape(-1, width).astype(jnp.float32)
    grad_stream = upstream + inverse * (grad_normed - normed32 * lax.optimization_barrier(jnp.mean(normed32 * grad_normed, axis=-1, keepdims=True)))
    grad_residual = grad_stream.astype(jnp.bfloat16)
    grad_context = jnp.dot(grad_residual, proj_weight.T, preferred_element_type=jnp.float32).astype(jnp.bfloat16)
    grad_proj = jnp.dot(flat_ctx.T, grad_residual, preferred_element_type=jnp.float32)
    return (grad_context.reshape(images, tokens, width), grad_residual.reshape(images, tokens, width), grad_proj, grad_slots, grad_expert_in, grad_expert_out)
```

```python
import math

import jax
import jax.numpy as jnp
from jax import lax
from jax.sharding import PartitionSpec as P

logit_scale = 48.0
epsilon = 1e-06
f32 = jnp.float32
bf16 = jnp.bfloat16


def gelu_back(pre, upstream):
    return jax.vjp(jax.nn.gelu, pre)[1](upstream)[0]


def swap(x, axis, size, bit):
    return lax.ppermute(x, axis, [(i, i ^ bit) for i in range(size)])


def tree(parts):
    while len(parts) > 1:
        parts = [parts[k] + parts[k + 1] for k in range(0, len(parts), 2)]
    return parts[0]


def gather_rows(block, n_img):
    held = [block]
    bit = n_img // 2
    while bit:
        held = held + [swap(h, "img", n_img, bit) for h in held]
        bit //= 2
    return held


def shards(n_img, n_exp, context, residual, cotangent, proj_weight, slot_params, expert_in, expert_out):
    images, tokens, width = context.shape
    rows = images * tokens
    owned = expert_in.shape[0]
    factor = logit_scale / math.sqrt(width)
    me_img = lax.axis_index("img")
    me_exp = lax.axis_index("exp")
    flat_ctx = context.reshape(rows, width)
    flat_cot = cotangent.reshape(rows, width)

    near = swap(proj_weight, "img", n_img, 1)
    far = swap(proj_weight, "img", n_img, 2)
    far_near = swap(far, "img", n_img, 1)
    relative = [proj_weight, near, far, far_near]
    order = jnp.arange(n_img) ^ me_img
    blocks = jnp.stack(relative)
    whole_proj = jnp.take(blocks, order, axis=0).reshape(width, width)

    sub = width // (n_img * n_exp)
    ctx_t = flat_ctx.T.reshape(n_img, n_exp, sub, rows)
    ctx_t = jnp.take(ctx_t, order, axis=0)
    ctx_t = jnp.take(ctx_t, jnp.arange(n_exp) ^ me_exp, axis=1)
    ctx_t = ctx_t.reshape(2, 2, n_exp // 2, 2, sub, rows)
    left_p = ctx_t.transpose(1, 0, 3, 2, 4, 5).reshape(2, -1, rows)
    left_q = ctx_t.transpose(1, 3, 0, 2, 4, 5).reshape(2, -1, rows)

    mixed = jnp.dot(flat_ctx, whole_proj, preferred_element_type=f32)
    stream = (residual.reshape(rows, width).astype(f32) + mixed).astype(bf16)
    stream32 = stream.astype(f32)
    inverse = lax.rsqrt(jnp.mean(stream32 * stream32, axis=-1, keepdims=True) + epsilon)
    normed32 = stream32 * inverse
    normed = normed32.astype(bf16)
    params32 = slot_params.astype(f32)
    slot_norm = jnp.sqrt(jnp.sum(params32 * params32, axis=0, keepdims=True) + epsilon)
    unit32 = params32 / slot_norm
    unit = unit32.astype(bf16)
    logits = factor * jnp.dot(normed, unit, preferred_element_type=f32)
    logits = logits.reshape(images, tokens, -1)
    expo = jnp.exp(logits)
    dispatch32 = expo / jnp.sum(expo, axis=1, keepdims=True)
    combine32 = expo / jnp.sum(expo, axis=2, keepdims=True)
    dispatch = dispatch32.astype(bf16)
    combine = combine32.astype(bf16)
    normed3 = normed.reshape(images, tokens, width)
    slot_in = jnp.einsum("bms,bmd->sbd", dispatch, normed3, preferred_element_type=f32).astype(bf16)
    grad_slot_out = jnp.einsum(
        "bms,bmd->sbd", combine, cotangent, preferred_element_type=f32
    ).astype(bf16)

    out = jnp.stack([slot_in, grad_slot_out], axis=1).reshape(n_exp, owned * 2 * images, width)
    got = lax.all_to_all(out, "exp", split_axis=0, concat_axis=0, tiled=True)
    got = lax.all_gather(got, "img", axis=0, tiled=True)
    got = got.reshape(n_img * n_exp, owned, 2, images, width)
    slot_rows = got[:, :, 0].transpose(1, 0, 2, 3).reshape(owned, -1, width)
    grad_rows = got[:, :, 1].transpose(1, 0, 2, 3).reshape(owned, -1, width)

    pre = jnp.einsum("jgd,jdf->jgf", slot_rows, expert_in, preferred_element_type=f32)
    act = jax.nn.gelu(pre).astype(bf16)
    part_out = jnp.einsum("jgf,jfd->jgd", act, expert_out, preferred_element_type=f32)
    grad_act = jnp.einsum("jgd,jfd->jgf", grad_rows, expert_out, preferred_element_type=f32)
    grad_pre = gelu_back(pre, grad_act).astype(bf16)
    part_in = jnp.einsum("jgf,jdf->jgd", grad_pre, expert_in, preferred_element_type=f32)
    back = jnp.stack([part_out, part_in], axis=0).astype(bf16)
    back = back.reshape(2, owned, n_img * n_exp, images, width).transpose(2, 1, 0, 3, 4)
    back = back.reshape(n_img * n_exp, owned * 2 * images, width)
    back = lax.all_to_all(back, ("img", "exp"), split_axis=0, concat_axis=0, tiled=True)
    back = back.reshape(n_img, n_exp, owned, 2, images, width).astype(f32).sum(axis=0).astype(bf16)
    back = back.transpose(2, 3, 0, 1, 4).reshape(2, images, n_exp * owned, width)
    slot_out, grad_slot_in = back[0], back[1]

    grad_expert_out = jnp.einsum(
        "jgf,jgd->jfd", act, grad_rows, preferred_element_type=f32
    ).astype(bf16)
    grad_expert_in = jnp.einsum(
        "jgd,jgf->jdf", slot_rows, grad_pre, preferred_element_type=f32
    ).astype(bf16)

    grad_combine = jnp.einsum("bmd,bsd->bms", cotangent, slot_out, preferred_element_type=f32)
    grad_dispatch = jnp.einsum("bmd,bsd->bms", normed3, grad_slot_in, preferred_element_type=f32)
    grad_logits32 = combine32 * (
        grad_combine - jnp.sum(combine32 * grad_combine, axis=2, keepdims=True)
    )
    grad_logits32 = grad_logits32 + dispatch32 * (
        grad_dispatch - jnp.sum(dispatch32 * grad_dispatch, axis=1, keepdims=True)
    )
    grad_logits = grad_logits32.astype(bf16).reshape(rows, -1)
    grad_normed = jnp.einsum(
        "bms,bsd->bmd", dispatch, grad_slot_in, preferred_element_type=f32
    ).reshape(rows, width)
    grad_normed = grad_normed + factor * jnp.dot(grad_logits, unit.T, preferred_element_type=f32)
    local_unit = factor * jnp.dot(grad_logits.T, normed, preferred_element_type=f32)
    grad_stream = flat_cot.astype(f32) + inverse * (
        grad_normed - normed32 * jnp.mean(normed32 * grad_normed, axis=-1, keepdims=True)
    )
    grad_residual = grad_stream.astype(bf16)

    half = width // 2
    gr_p, gr_q = grad_residual[:, :half], grad_residual[:, half:]

    def product(k):
        p = jnp.dot(left_p[k], gr_p, preferred_element_type=f32).astype(bf16)
        q = jnp.dot(left_q[k], gr_q, preferred_element_type=f32).astype(bf16)
        return p, q

    def split(x):
        high = x.astype(bf16)
        low = (x - high.astype(f32)).astype(bf16)
        return jnp.concatenate([high, low], axis=0)

    def joined(x):
        n = x.shape[0] // 2
        return x[:n].astype(f32) + x[n:].astype(f32)

    def add(a, b):
        return (a.astype(f32) + b.astype(f32)).astype(bf16)

    def halves(x):
        n = x.shape[0] // 2
        return x[:n], x[n:]

    side = split(local_unit.reshape(-1, half))
    n_side = side.shape[0]
    send_p, send_q = product(1)
    n = send_p.shape[0]
    got = swap(jnp.concatenate([send_p, send_q, side]), "img", n_img, 1)
    keep_p, keep_q = product(0)
    p, q, other = got[:n], got[n : 2 * n], got[2 * n :]
    p0, p1 = halves(add(keep_p, p))
    q0, q1 = halves(add(keep_q, q))
    side = split(joined(side) + joined(other))
    n = p1.shape[0]
    got_p = swap(jnp.concatenate([p1, side]), "img", n_img, 2)
    got_q = swap(q1, "exp", n_exp, 1)
    p0, p1 = halves(add(p0, got_p[:n]))
    q0, q1 = halves(add(q0, got_q))
    side = split(joined(side) + joined(got_p[n:]))
    n = p1.shape[0]
    got_p = swap(jnp.concatenate([p1, side]), "exp", n_exp, 1)
    got_q = swap(q1, "img", n_img, 2)
    p, q = add(p0, got_p[:n]), add(q0, got_q)
    side = split(joined(side) + joined(got_p[n:]))
    groups = n_exp // 2
    p = p.reshape(groups, -1, half)
    q = q.reshape(groups, -1, half)
    n = p.shape[1]
    pq = jnp.concatenate([p, q], axis=1)
    got = [pq[0]]
    sides = [side]
    for m in range(1, groups):
        r = swap(jnp.concatenate([pq[m], side]), "exp", n_exp, 2 * m)
        got.append(r[: 2 * n])
        sides.append(r[2 * n :])
    own = tree([g.astype(f32) for g in got]).astype(bf16)
    grad_unit = tree([joined(s) for s in sides]).reshape(-1, width)
    held = jnp.stack([own] + [swap(own, "exp", n_exp, 2 * m) for m in range(1, groups)])
    held = jnp.stack([held, swap(held, "exp", n_exp, 1)], axis=1)
    held = held.reshape(n_exp, 2, n, half)
    bit = 1
    while bit < n_exp:
        view = held.reshape(n_exp // (2 * bit), 2, bit, 2, n, half)
        held = jnp.where((me_exp & bit) != 0, view[:, ::-1], view).reshape(n_exp, 2, n, half)
        bit *= 2
    grad_proj = held.astype(f32).transpose(0, 2, 1, 3).reshape(-1, width)

    unit_t = unit32.T
    grad_slots = (
        (grad_unit - unit_t * jnp.sum(unit_t * grad_unit, axis=1, keepdims=True)) / slot_norm.T
    ).T
    grad_context = jnp.dot(grad_residual, whole_proj.T, preferred_element_type=f32).astype(bf16)
    return (
        grad_context.reshape(images, tokens, width),
        grad_residual.reshape(images, tokens, width),
        grad_proj,
        grad_slots,
        grad_expert_in,
        grad_expert_out,
    )


def solution(mesh):
    n_img, n_exp = mesh.shape["img"], mesh.shape["exp"]
    placed = (
        P(("img", "exp"), None, None),
        P(("img", "exp"), None, None),
        P(("img", "exp"), None, None),
        P("img", None),
        P(),
        P("exp", None, "img"),
        P("exp", "img", None),
    )

    def run(*args):
        return shards(n_img, n_exp, *args)

    return jax.shard_map(
        run,
        mesh=mesh,
        in_specs=placed,
        out_specs=(
            P(("img", "exp"), None, None),
            P(("img", "exp"), None, None),
            P("img", None),
            P(),
            P("exp", None, "img"),
            P("exp", "img", None),
        ),
        check_vma=False,
    )
```

```python
import functools
import math

import jax
import jax.numpy as jnp
import numpy as np
from jax import lax
from jax.experimental import pallas as pl
from jax.experimental.pallas import tpu as pltpu
from jax.sharding import PartitionSpec as P

logit_scale = 48.0
epsilon = 1e-06
f32 = jnp.float32
bf16 = jnp.bfloat16
vmem = pl.BlockSpec(memory_space=pltpu.VMEM)
smem = pl.BlockSpec(memory_space=pltpu.SMEM)
room = pltpu.CompilerParams(vmem_limit_bytes=48 * 1024 * 1024)


def swap(x, axis, size, bit):
    return lax.ppermute(x, axis, [(i, i ^ bit) for i in range(size)])


def tree(parts):
    while len(parts) > 1:
        parts = [parts[k] + parts[k + 1] for k in range(0, len(parts), 2)]
    return parts[0]


def dot(a, b):
    return jnp.dot(a, b, preferred_element_type=f32)


def dot_last(a, b):
    return lax.dot_general(a, b, (((1,), (1,)), ((), ())), preferred_element_type=f32)


def dot_first(a, b):
    return lax.dot_general(a, b, (((0,), (0,)), ((), ())), preferred_element_type=f32)


def one_hot(order):
    return (jnp.asarray(order, jnp.int32)[:, None] == jnp.arange(order.size)).astype(bf16)


def halves(x):
    n = x.shape[0] // 2
    return x[:n], x[n:]


def high_low(x):
    high = x.astype(bf16).astype(f32)
    return jnp.concatenate([high, (x - high).astype(bf16).astype(f32)], axis=0)


def joined(x):
    high, low = halves(x)
    return high + low


def gelu_both(pre):
    scale = math.sqrt(2.0 / math.pi)
    square = pre * pre
    bent = jnp.tanh(scale * (pre + 0.044715 * (square * pre)))
    cdf = 0.5 * (1.0 + bent)
    slope = 0.5 * (1.0 - bent * bent) * (scale * (1.0 + (3 * 0.044715) * square))
    return pre * cdf, cdf + pre * slope


def forward_kernel(images, factor, n_img, *refs):
    me, ctx, res, cot, unit, perm = refs[:6]
    blocks = refs[6 : 6 + n_img]
    stream_out, inverse_out, dispatch_out, combine_out, slots_out = refs[6 + n_img :]
    tokens = ctx.shape[0] // images
    deep = blocks[0].shape[0]
    slot_in, grad_out = [], []
    for b in range(images):
        at = pl.ds(b * tokens, tokens)
        mixed = res[at, :].astype(f32)
        for r in range(n_img):
            columns = pl.ds(pl.multiple_of((me[0] ^ r) * deep, deep), deep)
            mixed = mixed + dot(ctx[at, columns], blocks[r][...])
        stream = mixed.astype(bf16)
        stream_out[at, :] = stream
        stream32 = stream.astype(f32)
        inverse = lax.rsqrt(jnp.mean(stream32 * stream32, axis=-1, keepdims=True) + epsilon)
        inverse_out[at, :] = inverse
        normed = (stream32 * inverse).astype(bf16)
        expo = jnp.exp(factor * dot(normed, unit[...]))
        dispatch32 = expo / jnp.sum(expo, axis=0, keepdims=True)
        combine32 = expo / jnp.sum(expo, axis=1, keepdims=True)
        dispatch_out[at, :] = dispatch32
        combine_out[at, :] = combine32
        slot_in.append(dot_first(dispatch32.astype(bf16), normed).astype(bf16))
        grad_out.append(dot_first(combine32.astype(bf16), cot[at, :]).astype(bf16))
    parts = jnp.concatenate(slot_in + grad_out, axis=0)
    slots_out[...] = dot_first(perm[...], parts).astype(bf16)


def expert_kernel(got, perm, first, second, rows, act, grad_pre, back, sums, held):
    j, f = pl.program_id(0), pl.program_id(1)
    last = pl.num_programs(1) - 1

    @pl.when((j == 0) & (f == 0))
    def _():
        rows[...] = dot(perm[...], got[...]).astype(bf16).reshape(rows.shape)

    x, g = rows[2 * j], rows[2 * j + 1]
    first_w, second_w = first[0], second[0]
    pre = dot(x, first_w)
    value, slope = gelu_both(pre)
    value = value.astype(bf16)
    act[0] = value
    grad = (dot_last(g, second_w) * slope).astype(bf16)
    grad_pre[0] = grad
    part_out, part_in = dot(value, second_w), dot_last(grad, first_w)

    @pl.when(f == 0)
    def _():
        sums[0], sums[1] = part_out, part_in

    @pl.when(f > 0)
    def _():
        sums[0] += part_out
        sums[1] += part_in

    @pl.when(f == last)
    def _():
        held[2 * j] = sums[0].astype(bf16)
        held[2 * j + 1] = sums[1].astype(bf16)

    @pl.when((f == last) & (j == pl.num_programs(0) - 1))
    def _():
        parts = held[...].reshape(got.shape)
        back[...] = dot_first(perm[...], parts).astype(bf16)


def grads_kernel(rows, act, grad_pre, grad_first, grad_second):
    f = pl.program_id(1)
    deep = grad_second.shape[1]
    at = pl.ds(pl.multiple_of(f * deep, deep), deep)
    grad_second[0] = dot_first(act[0, :, at], rows[1]).astype(bf16)
    deep = grad_first.shape[1]
    at = pl.ds(pl.multiple_of(f * deep, deep), deep)
    grad_first[0] = dot_first(rows[0, :, at], grad_pre[0]).astype(bf16)


def backward_kernel(
    images, factor, me, back, perm, stream, inverse, cot, dispatch, combine, unit_t, left_p, left_q,
    grad_out, send, side_out,
):
    tokens = cot.shape[0] // images
    slots = unit_t.shape[0]
    half = send.shape[1]
    total = tree([back[r].astype(f32) for r in range(back.shape[0])]).astype(bf16)
    parts = dot(perm[...], total).astype(bf16)
    unit_sum = 0.0
    for b in range(images):
        at = pl.ds(b * tokens, tokens)
        slot_out = parts[b * slots : (b + 1) * slots]
        grad_slot_in = parts[(images + b) * slots : (images + b + 1) * slots]
        upstream = cot[at, :]
        inv = inverse[at, :]
        normed32 = stream[at, :].astype(f32) * inv
        normed = normed32.astype(bf16)
        dispatch32, combine32 = dispatch[at, :], combine[at, :]
        grad_combine = dot_last(upstream, slot_out)
        grad_dispatch = dot_last(normed, grad_slot_in)
        logits = combine32 * (
            grad_combine - jnp.sum(combine32 * grad_combine, axis=1, keepdims=True)
        ) + dispatch32 * (
            grad_dispatch - jnp.sum(dispatch32 * grad_dispatch, axis=0, keepdims=True)
        )
        logits = logits.astype(bf16)
        grad_normed = dot(dispatch32.astype(bf16), grad_slot_in) + factor * dot(logits, unit_t[...])
        unit_sum = unit_sum + dot_first(logits, normed)
        grad = upstream.astype(f32) + inv * (
            grad_normed - normed32 * jnp.mean(normed32 * grad_normed, axis=-1, keepdims=True)
        )
        grad_out[at, :] = grad.astype(bf16)
    n = left_p.shape[0]
    send[:n, :] = dot(left_p[...], grad_out[:, :half]).astype(bf16)
    send[n : 2 * n, :] = dot(left_q[...], grad_out[:, half:]).astype(bf16)
    low, high = halves(factor * unit_sum)
    mine = jnp.where((me[0] & 1) == 0, low, high)
    other = jnp.where((me[0] & 1) == 0, high, low)
    side_out[...] = jnp.concatenate([mine[:, :half], mine[:, half:]], axis=0)
    other = jnp.concatenate([other[:, :half], other[:, half:]], axis=0)
    send[2 * n :, :] = high_low(other).astype(bf16)


def keep_kernel(left_p, left_q, grad, out):
    half = out.shape[1]
    n = left_p.shape[0]
    out[:n, :] = dot(left_p[...], grad[:, :half]).astype(bf16)
    out[n:, :] = dot(left_q[...], grad[:, half:]).astype(bf16)


def first_kernel(me, keep, side, got, p_out, q_out, side_out, send_p, send_q):
    n = keep.shape[0] // 2
    p0, p1 = halves(keep[:n, :].astype(f32) + got[:n, :].astype(f32))
    q0, q1 = halves(keep[n:, :].astype(f32) + got[n : 2 * n, :].astype(f32))
    low, high = halves(side[...] + joined(got[2 * n :, :].astype(f32)))
    lower = (me[0] & 2) == 0
    side_out[...] = jnp.where(lower, low, high)
    p_out[...] = p0.astype(bf16)
    q_out[...] = q0.astype(bf16)
    other = high_low(jnp.where(lower, high, low))
    send_p[...] = jnp.concatenate([p1, other], axis=0).astype(bf16)
    send_q[...] = q1.astype(bf16)


def second_kernel(p_in, q_in, side, got_p, got_q, p_out, q_out, side_out, send_p, send_q):
    n = p_in.shape[0]
    got = got_p[...].astype(f32)
    p0, p1 = halves(p_in[...].astype(f32) + got[:n])
    q0, q1 = halves(q_in[...].astype(f32) + got_q[...].astype(f32))
    mine = high_low(side[...] + joined(got[n:]))
    side_out[...] = mine
    p_out[...] = p0.astype(bf16)
    q_out[...] = q0.astype(bf16)
    send_p[...] = jnp.concatenate([p1, mine], axis=0).astype(bf16)
    send_q[...] = q1.astype(bf16)


def third_kernel(p_in, q_in, side, got_p, got_q, keep, side_out, *sends):
    n = p_in.shape[0]
    got = got_p[...].astype(f32)
    p = p_in[...].astype(f32) + got[:n]
    q = q_in[...].astype(f32) + got_q[...].astype(f32)
    mine = high_low(joined(side[...]) + joined(got[n:]))
    side_out[...] = mine
    n = n // (len(sends) + 1)
    keep[...] = jnp.concatenate([p[:n], q[:n]], axis=0)
    for m, send in enumerate(sends, 1):
        at = slice(m * n, (m + 1) * n)
        send[...] = jnp.concatenate([p[at], q[at], mine], axis=0).astype(bf16)


def fourth_kernel(keep, side, *refs):
    gots, (own, side_out) = refs[:-2], refs[-2:]
    n = keep.shape[0]
    gots = [g[...].astype(f32) for g in gots]
    own[...] = tree([keep[...]] + [g[:n] for g in gots]).astype(bf16)
    total = tree([joined(side[...])] + [joined(g[n:]) for g in gots])
    side_out[...] = high_low(total).astype(bf16)


def last_kernel(me, near, far, out):
    n = near.shape[1] // 2
    half = near.shape[2]
    for z in range(near.shape[0]):
        for y, ref in enumerate((near, far)):
            block = ref[z].astype(f32)
            at = me[1] ^ (2 * z + y)
            out[at, :, :half] = block[:n]
            out[at, :, half:] = block[n:]


def shards(n_img, n_exp, context, residual, cotangent, proj_weight, slot_params, expert_in, expert_out):
    images, tokens, width = context.shape
    rows = images * tokens
    owned, _, hidden = expert_in.shape
    slots = slot_params.shape[1]
    half = width // 2
    factor = logit_scale / math.sqrt(width)
    me_img = lax.axis_index("img")
    me_exp = lax.axis_index("exp")
    me = jnp.stack([me_img, me_exp]).astype(jnp.int32)
    flat_ctx = context.reshape(rows, width)
    flat_cot = cotangent.reshape(rows, width)
    shape = jax.ShapeDtypeStruct

    near = swap(proj_weight, "img", n_img, 1)
    far = swap(proj_weight, "img", n_img, 2)
    far_near = swap(far, "img", n_img, 1)
    blocks = [proj_weight, near, far, far_near]
    order = jnp.arange(n_img) ^ me_img

    sub = width // (n_img * n_exp)
    ctx_t = flat_ctx.T.reshape(n_img, n_exp, sub, rows)
    ctx_t = jnp.take(ctx_t, order, axis=0)
    ctx_t = jnp.take(ctx_t, jnp.arange(n_exp) ^ me_exp, axis=1)
    ctx_t = ctx_t.reshape(2, 2, n_exp // 2, 2, sub, rows)
    left_p = ctx_t.transpose(1, 0, 3, 2, 4, 5).reshape(2, -1, rows)
    left_q = ctx_t.transpose(1, 3, 0, 2, 4, 5).reshape(2, -1, rows)

    params32 = slot_params.astype(f32)
    slot_norm = jnp.sqrt(jnp.sum(params32 * params32, axis=0, keepdims=True) + epsilon)
    unit32 = params32 / slot_norm
    unit = unit32.astype(bf16)
    unit_t32 = unit32.T
    unit_t = unit_t32.astype(bf16)

    perm = one_hot(
        np.arange(slots * 2 * images).reshape(slots, 2, images).transpose(1, 2, 0).reshape(-1)
    )
    stream, inverse, dispatch32, combine32, out = pl.pallas_call(
        functools.partial(forward_kernel, images, factor, n_img),
        in_specs=[smem] + [vmem] * (5 + n_img),
        out_specs=[vmem] * 5,
        out_shape=[
            shape((rows, width), bf16),
            shape((rows, 1), f32),
            shape((rows, slots), f32),
            shape((rows, slots), f32),
            shape((slots * 2 * images, width), bf16),
        ],
        compiler_params=room,
        name="forward",
    )(me, flat_ctx, residual.reshape(rows, width), flat_cot, unit, perm, *blocks)

    got = lax.all_to_all(
        out.reshape(n_exp, -1, width), "exp", split_axis=0, concat_axis=0, tiled=True
    )
    got = lax.all_gather(got, "img", axis=0, tiled=True).reshape(-1, width)

    sources = n_img * n_exp
    count = sources * images
    shuffle = one_hot(
        np.arange(count * owned * 2)
        .reshape(sources, owned, 2, images)
        .transpose(1, 2, 0, 3)
        .reshape(-1)
    )
    step = min(hidden, 512)
    whole = lambda s: pl.BlockSpec(s, lambda j, f: (0,) * len(s))
    act_spec = pl.BlockSpec((1, count, step), lambda j, f: (j, 0, f))
    slot_rows, act, grad_pre, back = pl.pallas_call(
        expert_kernel,
        grid=(owned, hidden // step),
        in_specs=[
            whole(got.shape),
            whole(shuffle.shape),
            pl.BlockSpec((1, width, step), lambda j, f: (j, 0, f)),
            pl.BlockSpec((1, step, width), lambda j, f: (j, f, 0)),
        ],
        out_specs=[whole((owned * 2, count, width)), act_spec, act_spec, whole(got.shape)],
        out_shape=[
            shape((owned * 2, count, width), bf16),
            shape((owned, count, hidden), bf16),
            shape((owned, count, hidden), bf16),
            shape(got.shape, bf16),
        ],
        scratch_shapes=[
            pltpu.VMEM((2, count, width), f32),
            pltpu.VMEM((owned * 2, count, width), bf16),
        ],
        compiler_params=room,
        name="experts",
    )(got, shuffle, expert_in, expert_out)

    back = lax.all_to_all(
        back.reshape(sources, -1, width), ("img", "exp"), split_axis=0, concat_axis=0, tiled=True
    )

    cuts = 4
    part = lambda s: pl.BlockSpec((1,) + s, lambda j, f: (j, 0, 0))
    grad_expert_in, grad_expert_out = pl.pallas_call(
        grads_kernel,
        grid=(owned, cuts),
        in_specs=[
            pl.BlockSpec((2, count, width), lambda j, f: (j, 0, 0)),
            part((count, hidden)),
            part((count, hidden)),
        ],
        out_specs=[
            pl.BlockSpec((1, width // cuts, hidden), lambda j, f: (j, f, 0)),
            pl.BlockSpec((1, hidden // cuts, width), lambda j, f: (j, f, 0)),
        ],
        out_shape=[shape(expert_in.shape, bf16), shape(expert_out.shape, bf16)],
        compiler_params=room,
        name="expert_grads",
    )(slot_rows, act, grad_pre)
    back, grad_expert_in, grad_expert_out = lax.optimization_barrier(
        (back, grad_expert_in, grad_expert_out)
    )

    n = left_p.shape[1]
    side_rows = 2 * slots
    grad_residual, send, side = pl.pallas_call(
        functools.partial(backward_kernel, images, factor),
        in_specs=[smem] + [vmem] * 10,
        out_specs=[vmem] * 3,
        out_shape=[
            shape((rows, width), bf16),
            shape((2 * n + side_rows, half), bf16),
            shape((slots, half), f32),
        ],
        compiler_params=room,
        name="backward",
    )(
        me, back.reshape(n_img, -1, width), perm, stream, inverse, flat_cot, dispatch32, combine32,
        unit_t, left_p[1], left_q[1],
    )

    got = swap(send, "img", n_img, 1)
    keep = pl.pallas_call(
        keep_kernel,
        in_specs=[vmem] * 3,
        out_specs=vmem,
        out_shape=shape((2 * n, half), bf16),
        compiler_params=room,
        name="keep",
    )(left_p[0], left_q[0], grad_residual)
    n, side_rows = n // 2, slots
    p, q, side, send_p, send_q = pl.pallas_call(
        first_kernel,
        in_specs=[smem] + [vmem] * 3,
        out_specs=[vmem] * 5,
        out_shape=[
            shape((n, half), bf16),
            shape((n, half), bf16),
            shape((slots // 2, half), f32),
            shape((n + slots, half), bf16),
            shape((n, half), bf16),
        ],
        compiler_params=room,
        name="first",
    )(me, keep, side, got)
    got_p = swap(send_p, "img", n_img, 2)
    got_q = swap(send_q, "exp", n_exp, 1)
    n = n // 2
    p, q, side, send_p, send_q = pl.pallas_call(
        second_kernel,
        in_specs=[vmem] * 5,
        out_specs=[vmem] * 5,
        out_shape=[
            shape((n, half), bf16),
            shape((n, half), bf16),
            shape((slots, half), f32),
            shape((n + slots, half), bf16),
            shape((n, half), bf16),
        ],
        compiler_params=room,
        name="second",
    )(p, q, side, got_p, got_q)
    got_p = swap(send_p, "exp", n_exp, 1)
    got_q = swap(send_q, "img", n_img, 2)
    groups = n_exp // 2
    n = n // groups
    keep, side, *sends = pl.pallas_call(
        third_kernel,
        in_specs=[vmem] * 5,
        out_specs=[vmem] * (1 + groups),
        out_shape=[shape((2 * n, half), f32), shape((slots, half), f32)]
        + [shape((2 * n + slots, half), bf16)] * (groups - 1),
        compiler_params=room,
        name="third",
    )(p, q, side, got_p, got_q)
    gots = [swap(s, "exp", n_exp, 2 * m) for m, s in enumerate(sends, 1)]
    own, side = pl.pallas_call(
        fourth_kernel,
        in_specs=[vmem] * (1 + groups),
        out_specs=[vmem] * 2,
        out_shape=[shape((2 * n, half), bf16), shape((slots, half), bf16)],
        compiler_params=room,
        name="fourth",
    )(keep, side, *gots)
    held = jnp.stack([own] + [swap(own, "exp", n_exp, 2 * m) for m in range(1, groups)])
    side = jnp.stack([side, swap(side, "img", n_img, 2)])
    other = swap(side, "img", n_img, 1)
    grad_proj = pl.pallas_call(
        last_kernel,
        in_specs=[smem, vmem, vmem],
        out_specs=vmem,
        out_shape=shape((n_exp, n, width), f32),
        compiler_params=room,
        name="last",
    )(me, held, swap(held, "exp", n_exp, 1)).reshape(-1, width)

    side = jnp.stack([side, other]).astype(f32).reshape(2, 2, 2, slots // 2, half).sum(axis=2)
    side = jnp.where((me_img & 1) == 0, side, side[::-1])
    side = jnp.where((me_img & 2) == 0, side, side[:, ::-1])
    grad_unit = side.transpose(0, 2, 1, 3).reshape(slots, width)
    grad_slots = (
        (grad_unit - unit_t32 * jnp.sum(unit_t32 * grad_unit, axis=1, keepdims=True)) / slot_norm.T
    ).T

    whole_proj = jnp.take(jnp.stack(blocks), order, axis=0).reshape(width, width)
    grad_context = dot_last(grad_residual, whole_proj).astype(bf16)
    return (
        grad_context.reshape(images, tokens, width),
        grad_residual.reshape(images, tokens, width),
        grad_proj,
        grad_slots,
        grad_expert_in,
        grad_expert_out,
    )


def solution(mesh):
    n_img, n_exp = mesh.shape["img"], mesh.shape["exp"]
    placed = (
        P(("img", "exp"), None, None),
        P(("img", "exp"), None, None),
        P(("img", "exp"), None, None),
        P("img", None),
        P(),
        P("exp", None, "img"),
        P("exp", "img", None),
    )
    return jax.shard_map(
        functools.partial(shards, n_img, n_exp),
        mesh=mesh,
        in_specs=placed,
        out_specs=(
            P(("img", "exp"), None, None),
            P(("img", "exp"), None, None),
            P("img", None),
            P(),
            P("exp", None, "img"),
            P("exp", "img", None),
        ),
        check_vma=False,
    )
```

```python
import functools
import math

import jax
import jax.numpy as jnp
import numpy as np
from jax import lax
from jax.experimental import pallas as pl
from jax.experimental.pallas import tpu as pltpu
from jax.sharding import PartitionSpec as P

logit_scale = 48.0
epsilon = 1e-06
f32 = jnp.float32
bf16 = jnp.bfloat16
spaces = {"vmem": pltpu.VMEM, "hbm": pltpu.HBM, "smem": pltpu.SMEM, "free": pltpu.VMEM}


def call(kernel, name, mib, inputs, outputs, scratch=()):
    def held(where, x):
        fixed = where in ("vmem", "hbm")
        return pltpu.with_memory_space_constraint(x, spaces[where]) if fixed else x

    return pl.pallas_call(
        kernel,
        in_specs=[pl.BlockSpec(memory_space=spaces[where]) for where, _ in inputs],
        out_specs=[pl.BlockSpec(memory_space=spaces[where]) for where, _, _ in outputs],
        out_shape=[spaces[where](s, t) for where, s, t in outputs],
        scratch_shapes=list(scratch),
        compiler_params=pltpu.CompilerParams(vmem_limit_bytes=mib * 1024 * 1024),
        name=name,
    )(*[held(where, x) for where, x in inputs])


def swap(x, axis, size, bit):
    return lax.ppermute(x, axis, [(i, i ^ bit) for i in range(size)])


def tree(parts):
    while len(parts) > 1:
        parts = [parts[k] + parts[k + 1] for k in range(0, len(parts), 2)]
    return parts[0]


def dot(a, b):
    return jnp.dot(a, b, preferred_element_type=f32)


def dot_last(a, b):
    return lax.dot_general(a, b, (((1,), (1,)), ((), ())), preferred_element_type=f32)


def dot_first(a, b):
    return lax.dot_general(a, b, (((0,), (0,)), ((), ())), preferred_element_type=f32)


def one_hot(order):
    return (jnp.asarray(order, jnp.int32)[:, None] == jnp.arange(order.size)).astype(bf16)


def halves(x):
    n = x.shape[0] // 2
    return x[:n], x[n:]


def high_low(x):
    high = x.astype(bf16).astype(f32)
    return jnp.concatenate([high, (x - high).astype(bf16).astype(f32)], axis=0)


def joined(x):
    high, low = halves(x)
    return high + low


def gelu_both(pre):
    scale = math.sqrt(2.0 / math.pi)
    square = pre * pre
    bent = jnp.tanh(scale * (pre + 0.044715 * (square * pre)))
    cdf = 0.5 * (1.0 + bent)
    slope = 0.5 * (1.0 - bent * bent) * (scale * (1.0 + (3 * 0.044715) * square))
    return pre * cdf, cdf + pre * slope


class Mover:
    def __init__(self, sems):
        self.sems, self.used = sems, 0

    def start(self, source, target):
        copy = pltpu.make_async_copy(source, target, self.sems.at[self.used])
        self.used += 1
        copy.start()
        return copy


def prepare_kernel(n_img, n_exp, me, ctx_hbm, res_hbm, own_hbm, near, *refs):
    lefts, near_out, mixed = refs[:4], refs[4], refs[5]
    ctx, res, own, turned, kept, sems = refs[6:]
    mover = Mover(sems)
    get_ctx = mover.start(ctx_hbm, ctx)
    get_own = mover.start(own_hbm, own)
    get_res = mover.start(res_hbm, res)
    out = [mover.start(near, near_out)]
    sub = turned.shape[0] // (n_img * n_exp)
    get_ctx.wait()
    turned[...] = ctx[...].astype(f32).T
    for core in range(2):
        for x in range(2):
            for y in range(2):
                block = []
                for z in range(n_exp // 2):
                    at = ((me[0] ^ (2 * x + core)) * n_exp + (me[1] ^ (2 * z + y))) * sub
                    block.append(turned[pl.ds(pl.multiple_of(at, sub), sub), :])
                block = jnp.concatenate(block, axis=0).astype(bf16)
                n = block.shape[0]
                kept[2 * core, (2 * x + y) * n : (2 * x + y + 1) * n, :] = block
                kept[2 * core + 1, (2 * y + x) * n : (2 * y + x + 1) * n, :] = block
    out += [mover.start(kept.at[k], left) for k, left in enumerate(lefts)]
    get_own.wait()
    get_res.wait()
    deep = own.shape[0]
    first = pl.ds(pl.multiple_of(me[0] * deep, deep), deep)
    second = pl.ds(pl.multiple_of((me[0] ^ 1) * deep, deep), deep)
    mixed[...] = res[...].astype(f32) + dot(ctx[:, first], own[...]) + dot(ctx[:, second], near[...])
    for copy in out:
        copy.wait()


def partial_kernel(taken, me, ctx_hbm, start, block, block_out, total, ctx, sems):
    mover = Mover(sems)
    deep = block.shape[0]
    columns = pl.ds(pl.multiple_of((me[0] ^ taken) * deep, deep), deep)
    get = mover.start(ctx_hbm.at[:, columns], ctx)
    out = mover.start(block, block_out)
    get.wait()
    total[...] = start[...] + dot(ctx[...], block[...])
    out.wait()


def forward_kernel(images, factor, taken, me, ctx_hbm, start, cot_hbm, unit, perm, block, *refs):
    block_out, stream_hbm, inverse_hbm, dispatch_hbm, combine_hbm, slots_hbm = refs[:6]
    ctx, cot, stream_v, inverse_v, dispatch_v, combine_v, slots_v, sems = refs[6:]
    mover = Mover(sems)
    deep = block.shape[0]
    tokens = cot.shape[0] // images
    columns = pl.ds(pl.multiple_of((me[0] ^ taken) * deep, deep), deep)
    get = mover.start(ctx_hbm.at[:, columns], ctx)
    get_cot = mover.start(cot_hbm, cot)
    out = [mover.start(block, block_out)]
    get.wait()
    slot_in, grad_out = [], []
    for b in range(images):
        at = pl.ds(b * tokens, tokens)
        mixed = start[at, :] + dot(ctx[at, :], block[...])
        stream = mixed.astype(bf16)
        stream_v[at, :] = stream
        stream32 = stream.astype(f32)
        inverse = lax.rsqrt(jnp.mean(stream32 * stream32, axis=-1, keepdims=True) + epsilon)
        inverse_v[at, :] = inverse
        normed = (stream32 * inverse).astype(bf16)
        expo = jnp.exp(factor * dot(normed, unit[...]))
        dispatch32 = expo / jnp.sum(expo, axis=0, keepdims=True)
        combine32 = expo / jnp.sum(expo, axis=1, keepdims=True)
        dispatch_v[at, :] = dispatch32
        combine_v[at, :] = combine32
        slot_in.append(dot_first(dispatch32.astype(bf16), normed).astype(bf16))
        if b == 0:
            get_cot.wait()
        grad_out.append(dot_first(combine32.astype(bf16), cot[at, :]).astype(bf16))
    out.append(mover.start(stream_v, stream_hbm))
    out.append(mover.start(inverse_v, inverse_hbm))
    out.append(mover.start(dispatch_v, dispatch_hbm))
    out.append(mover.start(combine_v, combine_hbm))
    parts = jnp.concatenate(slot_in + grad_out, axis=0)
    slots_v[...] = dot_first(perm[...], parts).astype(bf16)
    out += [mover.start(slots_v, slots_hbm.at[r]) for r in range(slots_hbm.shape[0])]
    for copy in out:
        copy.wait()


def expert_kernel(step, got, perm, first_hbm, second_hbm, *refs):
    rows_hbm, act_hbm, grad_hbm, back_hbm = refs[:4]
    first, second, rows, act, grad_pre, held, back, sems = refs[4:]
    mover = Mover(sems)
    owned, _, hidden = first.shape
    cuts = [(j, slice(f, f + step)) for j in range(owned) for f in range(0, hidden, step)]
    gets = [
        (
            mover.start(first_hbm.at[j, :, at], first.at[j, :, at]),
            mover.start(second_hbm.at[j, at, :], second.at[j, at, :]),
        )
        for j, at in cuts
    ]
    rows[...] = dot(perm[...], got[...]).astype(bf16).reshape(rows.shape)
    out = [mover.start(rows, rows_hbm)]
    for j in range(owned):
        x, g = rows[2 * j], rows[2 * j + 1]
        part_out = part_in = 0.0
        for (of, at), get in zip(cuts, gets, strict=True):
            if of != j:
                continue
            get[0].wait()
            first_w = first[j, :, at]
            value, slope = gelu_both(dot(x, first_w))
            value = value.astype(bf16)
            act[j, :, at] = value
            get[1].wait()
            second_w = second[j, at, :]
            grad = (dot_last(g, second_w) * slope).astype(bf16)
            grad_pre[j, :, at] = grad
            part_out = part_out + dot(value, second_w)
            part_in = part_in + dot_last(grad, first_w)
        held[2 * j] = part_out.astype(bf16)
        held[2 * j + 1] = part_in.astype(bf16)
    out.append(mover.start(act, act_hbm))
    out.append(mover.start(grad_pre, grad_hbm))
    back[...] = dot_first(perm[...], held[...].reshape(back.shape)).astype(bf16)
    out.append(mover.start(back, back_hbm))
    for copy in out:
        copy.wait()


def grads_kernel(rows, act, grad_pre, grad_first, grad_second):
    f = pl.program_id(1)
    deep = grad_second.shape[1]
    at = pl.ds(pl.multiple_of(f * deep, deep), deep)
    grad_second[0] = dot_first(act[0, :, at], rows[1]).astype(bf16)
    deep = grad_first.shape[1]
    at = pl.ds(pl.multiple_of(f * deep, deep), deep)
    grad_first[0] = dot_first(rows[0, :, at], grad_pre[0]).astype(bf16)


def backward_kernel(images, factor, back, perm, unit_t, *refs):
    hbm, (grad_hbm, send, side_out), scratch = refs[:7], refs[7:10], refs[10:]
    stream, inverse, dispatch, combine, cot, left_p, left_q, grad_v, sems = scratch
    mover = Mover(sems)
    gets = [mover.start(source, target) for source, target in zip(hbm, scratch[:7], strict=True)]
    tokens = cot.shape[0] // images
    slots = unit_t.shape[0]
    half = send.shape[1]
    total = tree([back[r].astype(f32) for r in range(back.shape[0])]).astype(bf16)
    parts = dot(perm[...], total).astype(bf16)
    for get in gets[:5]:
        get.wait()
    unit_sum = 0.0
    out = []
    for b in range(images):
        at = pl.ds(b * tokens, tokens)
        slot_out = parts[b * slots : (b + 1) * slots]
        grad_slot_in = parts[(images + b) * slots : (images + b + 1) * slots]
        upstream = cot[at, :]
        inv = inverse[at, :]
        normed32 = stream[at, :].astype(f32) * inv
        normed = normed32.astype(bf16)
        dispatch32, combine32 = dispatch[at, :], combine[at, :]
        grad_combine = dot_last(upstream, slot_out)
        grad_dispatch = dot_last(normed, grad_slot_in)
        logits = combine32 * (
            grad_combine - jnp.sum(combine32 * grad_combine, axis=1, keepdims=True)
        ) + dispatch32 * (
            grad_dispatch - jnp.sum(dispatch32 * grad_dispatch, axis=0, keepdims=True)
        )
        logits = logits.astype(bf16)
        grad_normed = dot(dispatch32.astype(bf16), grad_slot_in) + factor * dot(logits, unit_t[...])
        unit_sum = unit_sum + dot_first(logits, normed)
        grad = upstream.astype(f32) + inv * (
            grad_normed - normed32 * jnp.mean(normed32 * grad_normed, axis=-1, keepdims=True)
        )
        grad_v[at, :] = grad.astype(bf16)
        out.append(mover.start(grad_v.at[at, :], grad_hbm.at[at, :]))
    for get in gets[5:]:
        get.wait()
    n = left_p.shape[0]
    send[:n, :] = dot(left_p[...], grad_v[:, :half]).astype(bf16)
    send[n : 2 * n, :] = dot(left_q[...], grad_v[:, half:]).astype(bf16)
    unit_sum = factor * unit_sum
    side = high_low(jnp.concatenate([unit_sum[:, :half], unit_sum[:, half:]], axis=0))
    send[2 * n :, :] = side.astype(bf16)
    side_out[...] = joined(side)
    for copy in out:
        copy.wait()


def keep_kernel(left_p_hbm, left_q_hbm, grad_hbm, out, left_p, left_q, grad, sems):
    mover = Mover(sems)
    gets = [
        mover.start(grad_hbm, grad),
        mover.start(left_p_hbm, left_p),
        mover.start(left_q_hbm, left_q),
    ]
    half = out.shape[1]
    n = left_p.shape[0]
    gets[0].wait()
    gets[1].wait()
    out[:n, :] = dot(left_p[...], grad[:, :half]).astype(bf16)
    gets[2].wait()
    out[n:, :] = dot(left_q[...], grad[:, half:]).astype(bf16)


def chosen(bit, low, high):
    return jnp.where(bit == 0, low, high)


def first_kernel(me, keep, side, got, p_out, q_out, side_out, send_p, send_q):
    n = keep.shape[0] // 2
    p0, p1 = halves(keep[:n, :].astype(f32) + got[:n, :].astype(f32))
    q0, q1 = halves(keep[n:, :].astype(f32) + got[n : 2 * n, :].astype(f32))
    low, high = halves(side[...] + joined(got[2 * n :, :].astype(f32)))
    bit = me[1] & 1
    side_out[...] = chosen(bit, low, high)
    p_out[...] = p0.astype(bf16)
    q_out[...] = q0.astype(bf16)
    send_p[...] = p1.astype(bf16)
    other = high_low(chosen(bit, high, low))
    send_q[...] = jnp.concatenate([q1, other], axis=0).astype(bf16)


def second_kernel(p_in, q_in, side, got_p, got_q, p_out, q_out, side_out, send_p, send_q):
    n = p_in.shape[0]
    got = got_q[...].astype(f32)
    p0, p1 = halves(p_in[...].astype(f32) + got_p[...].astype(f32))
    q0, q1 = halves(q_in[...].astype(f32) + got[:n])
    mine = high_low(side[...] + joined(got[n:]))
    side_out[...] = joined(mine)
    p_out[...] = p0.astype(bf16)
    q_out[...] = q0.astype(bf16)
    send_p[...] = p1.astype(bf16)
    send_q[...] = jnp.concatenate([q1, mine], axis=0).astype(bf16)


def side_rows(piece):
    piece = high_low(piece)
    short = -piece.shape[0] % 16
    if short:
        piece = jnp.concatenate([piece, jnp.zeros((short, piece.shape[1]), f32)], axis=0)
    return piece


def third_kernel(me, p_in, q_in, side, got_p, got_q, keep, side_out, *sends):
    n = p_in.shape[0]
    groups = len(sends) + 1
    got = got_q[...].astype(f32)
    p = p_in[...].astype(f32) + got_p[...].astype(f32)
    q = q_in[...].astype(f32) + got[:n]
    total = side[...] + joined(got[n:])
    deep = total.shape[0] // groups
    pieces = [total[m * deep : (m + 1) * deep] for m in range(groups)]
    bit = 1
    while bit < groups:
        flip = me[1] & (2 * bit)
        pieces = [chosen(flip, pieces[m], pieces[m ^ bit]) for m in range(groups)]
        bit *= 2
    side_out[...] = pieces[0]
    n = n // groups
    keep[...] = jnp.concatenate([p[:n], q[:n]], axis=0)
    for m, send in enumerate(sends, 1):
        at = slice(m * n, (m + 1) * n)
        send[...] = jnp.concatenate([p[at], q[at], side_rows(pieces[m])], axis=0).astype(bf16)


def fourth_kernel(keep, side, *refs):
    gots, own = refs[:-1], refs[-1]
    n, deep = keep.shape[0], side.shape[0]
    gots = [g[...].astype(f32) for g in gots]
    total = tree([side[...]] + [joined(g[n : n + 2 * deep]) for g in gots])
    total = jnp.concatenate([tree([keep[...]] + [g[:n] for g in gots]), side_rows(total)], axis=0)
    own[...] = total.astype(bf16)


def join_kernel(*refs):
    for k, ref in enumerate(refs[:-1]):
        refs[-1][k] = ref[...]


def context_kernel(me, grad_hbm, own_hbm, near_hbm, far_hbm, far_near_hbm, out_hbm, grad, blocks, out, sems):
    mover = Mover(sems)
    deep = blocks.shape[1]
    get = mover.start(grad_hbm, grad)
    sources = (own_hbm, near_hbm, far_hbm, far_near_hbm)
    gets = [mover.start(source, blocks.at[r]) for r, source in enumerate(sources)]
    get.wait()
    puts = []
    for r, get in enumerate(gets):
        get.wait()
        columns = pl.ds(pl.multiple_of((me[0] ^ r) * deep, deep), deep)
        out[r] = dot_last(grad[...], blocks[r]).astype(bf16)
        puts.append(mover.start(out.at[r], out_hbm.at[:, columns]))
    for put in puts:
        put.wait()


def last_kernel(deep, me, near, far, unit_t, slot_norm, grad_hbm, slots_hbm, *scratch):
    grad, side, slots_out, sems = scratch
    mover = Mover(sems)
    n, half = grad.shape[1], near.shape[2]
    puts = []
    for z in range(near.shape[0]):
        for y, ref in enumerate((near, far)):
            block = ref[z].astype(f32)
            at = me[1] ^ (2 * z + y)
            k = 2 * z + y
            grad[k, :, :half] = block[:n]
            grad[k, :, half:] = block[n : 2 * n]
            puts.append(mover.start(grad.at[k], grad_hbm.at[at]))
            side[(at & 1) * near.shape[0] + (at >> 1)] = joined(block[2 * n : 2 * n + 2 * deep])
    total = jnp.concatenate([side[k] for k in range(side.shape[0])], axis=0)
    total = jnp.concatenate(halves(total), axis=1)
    unit = unit_t[...]
    along = jnp.sum(unit * total, axis=1, keepdims=True)
    slots_out[...] = (total - unit * along) / slot_norm[...]
    puts.append(mover.start(slots_out, slots_hbm))
    for put in puts:
        put.wait()


def shards(n_img, n_exp, context, residual, cotangent, proj_weight, slot_params, expert_in, expert_out):
    images, tokens, width = context.shape
    rows = images * tokens
    owned, _, hidden = expert_in.shape
    slots = slot_params.shape[1]
    half = width // 2
    factor = logit_scale / math.sqrt(width)
    me_img = lax.axis_index("img")
    me_exp = lax.axis_index("exp")
    me = jnp.stack([me_img, me_exp]).astype(jnp.int32)
    flat_ctx = context.reshape(rows, width)
    flat_cot = cotangent.reshape(rows, width)
    flat_res = residual.reshape(rows, width)
    dma = pltpu.SemaphoreType.DMA
    own = ("smem", me)

    far = swap(proj_weight, "img", n_img, 2)
    near = swap(proj_weight, "img", n_img, 1)
    deep = proj_weight.shape[0]
    block = (deep, width)
    left = (width // 2, rows)
    *lefts, near_copy, mixed = call(
        functools.partial(prepare_kernel, n_img, n_exp),
        "prepare",
        16,
        [own, ("hbm", flat_ctx), ("hbm", flat_res), ("hbm", proj_weight), ("vmem", near)],
        [("hbm", left, bf16)] * 4 + [("hbm", block, bf16), ("vmem", (rows, width), f32)],
        [
            pltpu.VMEM((rows, width), bf16),
            pltpu.VMEM((rows, width), bf16),
            pltpu.VMEM(block, bf16),
            pltpu.VMEM((width, rows), f32),
            pltpu.VMEM((4,) + left, bf16),
            dma((8,)),
        ],
    )
    params32 = slot_params.astype(f32).T
    slot_norm = jnp.sqrt(jnp.sum(params32 * params32, axis=1, keepdims=True) + epsilon)
    unit_t32 = params32 / slot_norm
    unit_t = unit_t32.astype(bf16)
    unit = unit_t.T
    perm = one_hot(
        np.arange(slots * 2 * images).reshape(slots, 2, images).transpose(1, 2, 0).reshape(-1)
    )
    sources = n_img * n_exp
    count = sources * images
    shuffle = one_hot(
        np.arange(count * owned * 2)
        .reshape(sources, owned, 2, images)
        .transpose(1, 2, 0, 3)
        .reshape(-1)
    )
    far, mixed, unit, unit_t, perm, shuffle = lax.optimization_barrier(
        (far, mixed, unit, unit_t, perm, shuffle)
    )
    keep_left, send_left = lefts[:2], lefts[2:]
    far_near = swap(far, "img", n_img, 1)
    far_copy, mixed = call(
        functools.partial(partial_kernel, 2),
        "partial",
        6,
        [own, ("hbm", flat_ctx), ("vmem", mixed), ("vmem", far)],
        [("hbm", block, bf16), ("vmem", (rows, width), f32)],
        [pltpu.VMEM((rows, deep), bf16), dma((2,))],
    )
    stats = [((rows, width), bf16), ((rows, 1), f32), ((rows, slots), f32), ((rows, slots), f32)]
    message = slots * 2 * images
    far_near_copy, *stats_hbm, out = call(
        functools.partial(forward_kernel, images, factor, 3),
        "forward",
        20,
        [
            own, ("hbm", flat_ctx), ("vmem", mixed), ("hbm", flat_cot), ("free", unit),
            ("free", perm), ("vmem", far_near),
        ],
        [("hbm", block, bf16)]
        + [("hbm", *s) for s in stats]
        + [("hbm", (n_img, message, width), bf16)],
        [
            pltpu.VMEM((rows, deep), bf16),
            pltpu.VMEM((rows, width), bf16),
            *[pltpu.VMEM(*s) for s in stats],
            pltpu.VMEM((message, width), bf16),
            dma((7 + n_img,)),
        ],
    )

    both = ("img", "exp")
    got = out.reshape(sources, -1, width)
    got = lax.all_to_all(got, both, split_axis=0, concat_axis=0, tiled=True).reshape(-1, width)

    step = min(hidden, 512)
    kept = [((owned * 2, count, width), bf16)] + [((owned, count, hidden), bf16)] * 2
    slot_rows, act, grad_pre, back = call(
        functools.partial(expert_kernel, step),
        "experts",
        28,
        [("vmem", got), ("free", shuffle), ("hbm", expert_in), ("hbm", expert_out)],
        [("hbm", *s) for s in kept] + [("hbm", got.shape, bf16)],
        [
            pltpu.VMEM(expert_in.shape, bf16),
            pltpu.VMEM(expert_out.shape, bf16),
            *[pltpu.VMEM(*s) for s in kept],
            pltpu.VMEM((owned * 2, count, width), bf16),
            pltpu.VMEM(got.shape, bf16),
            dma((2 * owned * (hidden // step) + 4,)),
        ],
    )
    back = back.reshape(sources, -1, width)
    back = lax.all_to_all(back, both, split_axis=0, concat_axis=0, tiled=True)

    cuts = 4
    fixed = lambda x: pltpu.with_memory_space_constraint(x, pltpu.HBM)
    part = lambda s: pl.BlockSpec((1,) + s, lambda j, f: (j, 0, 0))
    grad_expert_in, grad_expert_out = pl.pallas_call(
        grads_kernel,
        grid=(owned, cuts),
        in_specs=[
            pl.BlockSpec((2, count, width), lambda j, f: (j, 0, 0)),
            part((count, hidden)),
            part((count, hidden)),
        ],
        out_specs=[
            pl.BlockSpec((1, width // cuts, hidden), lambda j, f: (j, f, 0)),
            pl.BlockSpec((1, hidden // cuts, width), lambda j, f: (j, f, 0)),
        ],
        out_shape=[pltpu.HBM(expert_in.shape, bf16), pltpu.HBM(expert_out.shape, bf16)],
        compiler_params=pltpu.CompilerParams(vmem_limit_bytes=14 * 1024 * 1024),
        name="expert_grads",
    )(fixed(slot_rows), fixed(act), fixed(grad_pre))
    back, grad_expert_in, grad_expert_out = lax.optimization_barrier(
        (back, grad_expert_in, grad_expert_out)
    )

    n = width // 2
    grad_residual, send, side = call(
        functools.partial(backward_kernel, images, factor),
        "backward",
        24,
        [("vmem", back.reshape(n_img, -1, width)), ("free", perm), ("free", unit_t)]
        + [("hbm", x) for x in (*stats_hbm, flat_cot, *send_left)],
        [
            ("hbm", (rows, width), bf16),
            ("vmem", (2 * n + 4 * slots, half), bf16),
            ("vmem", (2 * slots, half), f32),
        ],
        [
            *[pltpu.VMEM(*s) for s in stats],
            pltpu.VMEM((rows, width), bf16),
            pltpu.VMEM(left, bf16),
            pltpu.VMEM(left, bf16),
            pltpu.VMEM((rows, width), bf16),
            dma((7 + images,)),
        ],
    )

    got = swap(send, "img", n_img, 1)
    (keep,) = call(
        keep_kernel,
        "keep",
        8,
        [("hbm", x) for x in (*keep_left, grad_residual)],
        [("vmem", (2 * n, half), bf16)],
        [pltpu.VMEM(left, bf16), pltpu.VMEM(left, bf16), pltpu.VMEM((rows, width), bf16), dma((3,))],
    )

    def after(n):
        rest = (("vmem", (n, half), bf16),) * 2 + (("vmem", (slots, half), f32),)
        return [*rest, ("vmem", (n, half), bf16), ("vmem", (n + 2 * slots, half), bf16)]

    n = n // 2
    p, q, side, send_p, send_q = call(
        first_kernel,
        "first",
        6,
        [own, ("vmem", keep), ("vmem", side), ("vmem", got)],
        after(n),
    )
    got_p = swap(send_p, "img", n_img, 2)
    got_q = swap(send_q, "exp", n_exp, 1)
    projection = (proj_weight, near_copy, far_copy, far_near_copy)
    (grad_context,) = call(
        context_kernel,
        "context",
        12,
        [own] + [("hbm", x) for x in (grad_residual, *projection)],
        [("hbm", (rows, width), bf16)],
        [
            pltpu.VMEM((rows, width), bf16),
            pltpu.VMEM((n_img,) + block, bf16),
            pltpu.VMEM((n_img, rows, deep), bf16),
            dma((1 + 2 * n_img,)),
        ],
    )
    got_p, got_q, grad_context = lax.optimization_barrier((got_p, got_q, grad_context))
    n = n // 2
    p, q, side, send_p, send_q = call(
        second_kernel, "second", 4, [("vmem", x) for x in (p, q, side, got_p, got_q)], after(n)
    )
    got_p = swap(send_p, "exp", n_exp, 1)
    got_q = swap(send_q, "img", n_img, 2)
    groups = n_exp // 2
    n = n // groups
    piece = slots // groups
    tail = -(-2 * piece // 16) * 16
    block = (2 * n + tail, half)
    keep, side, *sends = call(
        third_kernel,
        "third",
        4,
        [own] + [("vmem", x) for x in (p, q, side, got_p, got_q)],
        [("vmem", (2 * n, half), f32), ("vmem", (piece, half), f32)]
        + [("vmem", block, bf16)] * (groups - 1),
    )
    gots = [swap(s, "exp", n_exp, 2 * m) for m, s in enumerate(sends, 1)]
    (held,) = call(
        fourth_kernel,
        "fourth",
        4,
        [("vmem", x) for x in (keep, side, *gots)],
        [("vmem", block, bf16)],
    )
    held = [held] + [swap(held, "exp", n_exp, 2 * m) for m in range(1, groups)]
    (held,) = call(
        join_kernel, "join", 4, [("vmem", x) for x in held], [("vmem", (groups,) + block, bf16)]
    )
    others = swap(held, "exp", n_exp, 1)
    grad_proj, grad_slots = call(
        functools.partial(last_kernel, piece),
        "last",
        6,
        [own, ("vmem", held), ("vmem", others), ("free", unit_t32), ("free", slot_norm)],
        [("hbm", (n_exp, n, width), f32), ("hbm", (slots, width), f32)],
        [
            pltpu.VMEM((n_exp, n, width), f32),
            pltpu.VMEM((n_exp, piece, half), f32),
            pltpu.VMEM((slots, width), f32),
            dma((n_exp + 1,)),
        ],
    )
    return (
        grad_context.reshape(images, tokens, width),
        grad_residual.reshape(images, tokens, width),
        grad_proj.reshape(-1, width),
        grad_slots.T,
        grad_expert_in,
        grad_expert_out,
    )


def solution(mesh):
    n_img, n_exp = mesh.shape["img"], mesh.shape["exp"]
    placed = (
        P(("img", "exp"), None, None),
        P(("img", "exp"), None, None),
        P(("img", "exp"), None, None),
        P("img", None),
        P(),
        P("exp", None, "img"),
        P("exp", "img", None),
    )
    return jax.shard_map(
        functools.partial(shards, n_img, n_exp),
        mesh=mesh,
        in_specs=placed,
        out_specs=(
            P(("img", "exp"), None, None),
            P(("img", "exp"), None, None),
            P("img", None),
            P(),
            P("exp", None, "img"),
            P("exp", "img", None),
        ),
        check_vma=False,
    )
```

```python
import functools
import math

import jax
import jax.numpy as jnp
import numpy as np
from jax import lax
from jax.experimental import pallas as pl
from jax.experimental.pallas import tpu as pltpu
from jax.sharding import PartitionSpec as P

logit_scale = 48.0
epsilon = 1e-06
f32 = jnp.float32
bf16 = jnp.bfloat16
spaces = {"vmem": pltpu.VMEM, "hbm": pltpu.HBM, "free": pltpu.VMEM}


def call(kernel, name, mib, inputs, outputs, scratch=()):
    def held(where, x):
        fixed = where in ("vmem", "hbm")
        return pltpu.with_memory_space_constraint(x, spaces[where]) if fixed else x

    return pl.pallas_call(
        kernel,
        in_specs=[pl.BlockSpec(memory_space=spaces[where]) for where, _ in inputs],
        out_specs=[pl.BlockSpec(memory_space=spaces[where]) for where, _, _ in outputs],
        out_shape=[spaces[where](s, t) for where, s, t in outputs],
        scratch_shapes=list(scratch),
        compiler_params=pltpu.CompilerParams(vmem_limit_bytes=mib * 1024 * 1024),
        name=name,
    )(*[held(where, x) for where, x in inputs])


def swap(x, axis, size, bit):
    return lax.ppermute(x, axis, [(i, i ^ bit) for i in range(size)])


def tree(parts):
    while len(parts) > 1:
        parts = [parts[k] + parts[k + 1] for k in range(0, len(parts), 2)]
    return parts[0]


def dot(a, b):
    return jnp.dot(a, b, preferred_element_type=f32)


def dot_last(a, b):
    return lax.dot_general(a, b, (((1,), (1,)), ((), ())), preferred_element_type=f32)


def dot_first(a, b):
    return lax.dot_general(a, b, (((0,), (0,)), ((), ())), preferred_element_type=f32)


def one_hot(order):
    return (jnp.asarray(order, jnp.int32)[:, None] == jnp.arange(order.size)).astype(bf16)


def halves(x):
    n = x.shape[0] // 2
    return x[:n], x[n:]


def high_low(x):
    high = x.astype(bf16).astype(f32)
    return jnp.concatenate([high, (x - high).astype(bf16).astype(f32)], axis=0)


def joined(x):
    high, low = halves(x)
    return high + low


def gelu_both(pre):
    scale = math.sqrt(2.0 / math.pi)
    square = pre * pre
    bent = jnp.tanh(scale * (pre + 0.044715 * (square * pre)))
    cdf = 0.5 * (1.0 + bent)
    slope = 0.5 * (1.0 - bent * bent) * (scale * (1.0 + (3 * 0.044715) * square))
    return pre * cdf, cdf + pre * slope


class Mover:
    def __init__(self, sems):
        self.sems, self.used = sems, 0

    def start(self, source, target):
        copy = pltpu.make_async_copy(source, target, self.sems.at[self.used])
        self.used += 1
        copy.start()
        return copy


def prepare_kernel(n_img, n_exp, ctx_hbm, res_hbm, cot_hbm, own_hbm, near, *refs):
    lefts, near_out, mixed, ctx, cot = refs[:4], *refs[4:8]
    res, own, turned, kept, sems = refs[8:]
    mover = Mover(sems)
    get_ctx = mover.start(ctx_hbm, ctx)
    get_own = mover.start(own_hbm, own)
    get_res = mover.start(res_hbm, res)
    out = [mover.start(near, near_out), mover.start(cot_hbm, cot)]
    sub = turned.shape[0] // (n_img * n_exp)
    get_ctx.wait()
    turned[...] = ctx[...].astype(f32).T
    for core in range(2):
        for x in range(2):
            for y in range(2):
                block = []
                for z in range(n_exp // 2):
                    at = ((lax.axis_index("img") ^ (2 * x + core)) * n_exp + (lax.axis_index("exp") ^ (2 * z + y))) * sub
                    block.append(turned[pl.ds(pl.multiple_of(at, sub), sub), :])
                block = jnp.concatenate(block, axis=0).astype(bf16)
                n = block.shape[0]
                kept[2 * core, (2 * x + y) * n : (2 * x + y + 1) * n, :] = block
                kept[2 * core + 1, (2 * y + x) * n : (2 * y + x + 1) * n, :] = block
    out += [mover.start(kept.at[k], left) for k, left in enumerate(lefts)]
    get_own.wait()
    get_res.wait()
    deep = own.shape[0]
    first = pl.ds(pl.multiple_of(lax.axis_index("img") * deep, deep), deep)
    second = pl.ds(pl.multiple_of((lax.axis_index("img") ^ 1) * deep, deep), deep)
    mixed[...] = res[...].astype(f32) + dot(ctx[:, first], own[...]) + dot(ctx[:, second], near[...])
    for copy in out:
        copy.wait()


def partial_kernel(taken, ctx, start, block, block_out, total, sems):
    deep = block.shape[0]
    columns = pl.ds(pl.multiple_of((lax.axis_index("img") ^ taken) * deep, deep), deep)
    out = Mover(sems).start(block, block_out)
    total[...] = start[...] + dot(ctx[:, columns], block[...])
    out.wait()


def forward_kernel(images, factor, taken, ctx, start, cot, unit, perm, block, *refs):
    block_out, stream_v, stats_v, slots_hbm, slots_v, sems = refs
    mover = Mover(sems)
    deep = block.shape[0]
    tokens = cot.shape[0] // images
    columns = pl.ds(pl.multiple_of((lax.axis_index("img") ^ taken) * deep, deep), deep)
    out = [mover.start(block, block_out)]
    slot_in, grad_out = [], []
    for b in range(images):
        at = pl.ds(b * tokens, tokens)
        mixed = start[at, :] + dot(ctx[at, columns], block[...])
        stream = mixed.astype(bf16)
        stream_v[at, :] = stream
        stream32 = stream.astype(f32)
        inverse = lax.rsqrt(jnp.mean(stream32 * stream32, axis=-1, keepdims=True) + epsilon)
        normed = (stream32 * inverse).astype(bf16)
        expo = jnp.exp(factor * dot_last(normed, unit[...]))
        dispatch32 = expo / jnp.sum(expo, axis=0, keepdims=True)
        combine32 = expo / jnp.sum(expo, axis=1, keepdims=True)
        slots = dispatch32.shape[1]
        stats_v[at, :slots] = dispatch32
        stats_v[at, slots : 2 * slots] = combine32
        stats_v[at, 2 * slots : 2 * slots + 1] = inverse
        slot_in.append(dot_first(dispatch32.astype(bf16), normed).astype(bf16))
        grad_out.append(dot_first(combine32.astype(bf16), cot[at, :]).astype(bf16))
    parts = jnp.concatenate(slot_in + grad_out, axis=0)
    slots_v[...] = dot_first(perm[...], parts).astype(bf16)
    out.append(mover.start(slots_v, slots_hbm))
    for copy in out:
        copy.wait()


def expert_kernel(step, ahead, got, perm, first_hbm, second_hbm, *refs):
    rows_hbm, act_hbm, grad_hbm, back_hbm = refs[:4]
    first, second, rows, act, grad_pre, held, back, sems = refs[4:]
    mover = Mover(sems)
    owned, _, hidden = first.shape
    steps = [(j, slice(f, f + step)) for j in range(owned) for f in range(0, hidden, step)]
    pieces = []
    for j, at in steps:
        pieces.append((first_hbm.at[j, :, at], first.at[j, :, at]))
        pieces.append((second_hbm.at[j, at, :], second.at[j, at, :]))
    coming = [mover.start(*piece) for piece in pieces[:ahead]]

    def arrive():
        if len(coming) < len(pieces):
            coming.append(mover.start(*pieces[len(coming)]))

    rows[...] = dot(perm[...], got[...]).astype(bf16).reshape(rows.shape)
    out = [mover.start(rows, rows_hbm)]
    part_out = part_in = None
    for k, (j, at) in enumerate(steps):
        x, g = rows[2 * j], rows[2 * j + 1]
        coming[2 * k].wait()
        arrive()
        first_w = first[j, :, at]
        value, slope = gelu_both(dot(x, first_w))
        value = value.astype(bf16)
        act[j, :, at] = value
        coming[2 * k + 1].wait()
        arrive()
        second_w = second[j, at, :]
        grad = (dot_last(g, second_w) * slope).astype(bf16)
        grad_pre[j, :, at] = grad
        more_out, more_in = dot(value, second_w), dot_last(grad, first_w)
        if at.start == 0:
            part_out, part_in = more_out, more_in
        else:
            part_out, part_in = part_out + more_out, part_in + more_in
        if at.stop == hidden:
            held[2 * j] = part_out.astype(bf16)
            held[2 * j + 1] = part_in.astype(bf16)
    out.append(mover.start(act, act_hbm))
    out.append(mover.start(grad_pre, grad_hbm))
    back[...] = dot_first(perm[...], held[...].reshape(back.shape)).astype(bf16)
    out.append(mover.start(back, back_hbm))
    for copy in out:
        copy.wait()


def grads_kernel(rows, act, grad_pre, grad_first, grad_second):
    f = pl.program_id(1)
    deep = grad_second.shape[1]
    at = pl.ds(pl.multiple_of(f * deep, deep), deep)
    grad_second[0] = dot_first(act[0, :, at], rows[1]).astype(bf16)
    deep = grad_first.shape[1]
    at = pl.ds(pl.multiple_of(f * deep, deep), deep)
    grad_first[0] = dot_first(rows[0, :, at], grad_pre[0]).astype(bf16)


def backward_kernel(images, factor, back, perm, unit_t, *refs):
    stream, stats, cot, left_p_hbm, left_q_hbm, grad_hbm, send, side_out = refs[:8]
    left_p, left_q, grad_v, sems = refs[8:]
    mover = Mover(sems)
    gets = [mover.start(left_p_hbm, left_p), mover.start(left_q_hbm, left_q)]
    tokens = cot.shape[0] // images
    slots = unit_t.shape[0]
    half = send.shape[1]
    total = tree([back[r].astype(f32) for r in range(back.shape[0])]).astype(bf16)
    parts = dot(perm[...], total).astype(bf16)
    unit_sum = 0.0
    out = []
    for b in range(images):
        at = pl.ds(b * tokens, tokens)
        slot_out = parts[b * slots : (b + 1) * slots]
        grad_slot_in = parts[(images + b) * slots : (images + b + 1) * slots]
        upstream = cot[at, :]
        inv = stats[at, 2 * slots : 2 * slots + 1]
        normed32 = stream[at, :].astype(f32) * inv
        normed = normed32.astype(bf16)
        dispatch32, combine32 = stats[at, :slots], stats[at, slots : 2 * slots]
        grad_combine = dot_last(upstream, slot_out)
        grad_dispatch = dot_last(normed, grad_slot_in)
        logits = combine32 * (
            grad_combine - jnp.sum(combine32 * grad_combine, axis=1, keepdims=True)
        ) + dispatch32 * (
            grad_dispatch - jnp.sum(dispatch32 * grad_dispatch, axis=0, keepdims=True)
        )
        logits = logits.astype(bf16)
        grad_normed = dot(dispatch32.astype(bf16), grad_slot_in) + factor * dot(logits, unit_t[...])
        unit_sum = unit_sum + dot_first(logits, normed)
        grad = upstream.astype(f32) + inv * (
            grad_normed - normed32 * jnp.mean(normed32 * grad_normed, axis=-1, keepdims=True)
        )
        grad_v[at, :] = grad.astype(bf16)
        out.append(mover.start(grad_v.at[at, :], grad_hbm.at[at, :]))
    for get in gets:
        get.wait()
    n = left_p.shape[0]
    send[:n, :] = dot(left_p[...], grad_v[:, :half]).astype(bf16)
    send[n : 2 * n, :] = dot(left_q[...], grad_v[:, half:]).astype(bf16)
    unit_sum = factor * unit_sum
    side = high_low(jnp.concatenate([unit_sum[:, :half], unit_sum[:, half:]], axis=0))
    send[2 * n :, :] = side.astype(bf16)
    side_out[...] = joined(side)
    for copy in out:
        copy.wait()


def keep_kernel(left_p_hbm, left_q_hbm, grad_hbm, out, left_p, left_q, grad, sems):
    mover = Mover(sems)
    gets = [
        mover.start(grad_hbm, grad),
        mover.start(left_p_hbm, left_p),
        mover.start(left_q_hbm, left_q),
    ]
    half = out.shape[1]
    n = left_p.shape[0]
    gets[0].wait()
    gets[1].wait()
    out[:n, :] = dot(left_p[...], grad[:, :half]).astype(bf16)
    gets[2].wait()
    out[n:, :] = dot(left_q[...], grad[:, half:]).astype(bf16)


def chosen(bit, low, high):
    return jnp.where(bit == 0, low, high)


def first_kernel(keep, side, got, p_out, q_out, side_out, send_p, send_q):
    n = keep.shape[0] // 2
    p0, p1 = halves(keep[:n, :].astype(f32) + got[:n, :].astype(f32))
    q0, q1 = halves(keep[n:, :].astype(f32) + got[n : 2 * n, :].astype(f32))
    low, high = halves(side[...] + joined(got[2 * n :, :].astype(f32)))
    bit = lax.axis_index("exp") & 1
    side_out[...] = chosen(bit, low, high)
    p_out[...] = p0.astype(bf16)
    q_out[...] = q0.astype(bf16)
    send_p[...] = p1.astype(bf16)
    other = high_low(chosen(bit, high, low))
    send_q[...] = jnp.concatenate([q1, other], axis=0).astype(bf16)


def second_kernel(p_in, q_in, side, got_p, got_q, p_out, q_out, side_out, send_p, send_q):
    n = p_in.shape[0]
    got = got_q[...].astype(f32)
    p0, p1 = halves(p_in[...].astype(f32) + got_p[...].astype(f32))
    q0, q1 = halves(q_in[...].astype(f32) + got[:n])
    mine = high_low(side[...] + joined(got[n:]))
    side_out[...] = joined(mine)
    p_out[...] = p0.astype(bf16)
    q_out[...] = q0.astype(bf16)
    send_p[...] = p1.astype(bf16)
    send_q[...] = jnp.concatenate([q1, mine], axis=0).astype(bf16)


def side_rows(piece):
    piece = high_low(piece)
    short = -piece.shape[0] % 8
    if short:
        piece = jnp.concatenate([piece, jnp.zeros((short, piece.shape[1]), f32)], axis=0)
    return piece


def third_kernel(p_in, q_in, side, got_p, got_q, keep, side_out, *sends):
    n = p_in.shape[0]
    groups = len(sends) + 1
    got = got_q[...].astype(f32)
    p = p_in[...].astype(f32) + got_p[...].astype(f32)
    q = q_in[...].astype(f32) + got[:n]
    total = side[...] + joined(got[n:])
    deep = total.shape[0] // groups
    pieces = [total[m * deep : (m + 1) * deep] for m in range(groups)]
    bit = 1
    while bit < groups:
        flip = lax.axis_index("exp") & (2 * bit)
        pieces = [chosen(flip, pieces[m], pieces[m ^ bit]) for m in range(groups)]
        bit *= 2
    side_out[...] = pieces[0]
    n = n // groups
    keep[...] = jnp.concatenate([p[:n], q[:n]], axis=0)
    for m, send in enumerate(sends, 1):
        at = slice(m * n, (m + 1) * n)
        send[...] = jnp.concatenate([p[at], q[at], side_rows(pieces[m])], axis=0).astype(bf16)


def fourth_kernel(keep, side, *refs):
    gots, own = refs[:-1], refs[-1]
    n, deep = keep.shape[0], side.shape[0]
    gots = [g[...].astype(f32) for g in gots]
    total = tree([side[...]] + [joined(g[n : n + 2 * deep]) for g in gots])
    total = jnp.concatenate([tree([keep[...]] + [g[:n] for g in gots]), side_rows(total)], axis=0)
    own[...] = total.astype(bf16)


def context_kernel(grad_hbm, own_hbm, near_hbm, far_hbm, far_near_hbm, out_hbm, grad, blocks, out, sems):
    mover = Mover(sems)
    deep = blocks.shape[1]
    get = mover.start(grad_hbm, grad)
    sources = (own_hbm, near_hbm, far_hbm, far_near_hbm)
    gets = [mover.start(source, blocks.at[r]) for r, source in enumerate(sources)]
    get.wait()
    puts = []
    for r, get in enumerate(gets):
        get.wait()
        columns = pl.ds(pl.multiple_of((lax.axis_index("img") ^ r) * deep, deep), deep)
        out[r] = dot_last(grad[...], blocks[r]).astype(bf16)
        puts.append(mover.start(out.at[r], out_hbm.at[:, columns]))
    for put in puts:
        put.wait()


def last_kernel(deep, *refs):
    blocks, refs = refs[:-8], refs[-8:]
    unit_t, slot_norm, grad_hbm, slots_hbm, grad, side, slots_out, sems = refs
    mover = Mover(sems)
    groups = len(blocks) // 2
    n, half = grad.shape[1], blocks[0].shape[1]
    puts = []
    for y in range(2):
        for z in range(groups):
            block = blocks[y * groups + z][...].astype(f32)
            at = lax.axis_index("exp") ^ (2 * z + y)
            k = 2 * z + y
            grad[k, :, :half] = block[:n]
            grad[k, :, half:] = block[n : 2 * n]
            puts.append(mover.start(grad.at[k], grad_hbm.at[at]))
            side[(at & 1) * groups + (at >> 1)] = joined(block[2 * n : 2 * n + 2 * deep])
    total = jnp.concatenate([side[k] for k in range(side.shape[0])], axis=0)
    total = jnp.concatenate(halves(total), axis=1)
    unit = unit_t[...]
    along = jnp.sum(unit * total, axis=1, keepdims=True)
    slots_out[...] = (total - unit * along) / slot_norm[...]
    puts.append(mover.start(slots_out, slots_hbm))
    for put in puts:
        put.wait()


def shards(n_img, n_exp, context, residual, cotangent, proj_weight, slot_params, expert_in, expert_out):
    images, tokens, width = context.shape
    rows = images * tokens
    owned, _, hidden = expert_in.shape
    slots = slot_params.shape[1]
    half = width // 2
    factor = logit_scale / math.sqrt(width)
    flat_ctx = context.reshape(rows, width)
    flat_cot = cotangent.reshape(rows, width)
    flat_res = residual.reshape(rows, width)
    dma = pltpu.SemaphoreType.DMA

    far = swap(proj_weight, "img", n_img, 2)
    near = swap(proj_weight, "img", n_img, 1)
    deep = proj_weight.shape[0]
    block = (deep, width)
    left = (width // 2, rows)
    *lefts, near_copy, mixed, ctx, cot = call(
        functools.partial(prepare_kernel, n_img, n_exp),
        "prepare",
        16,
        [("hbm", x) for x in (flat_ctx, flat_res, flat_cot, proj_weight)] + [("vmem", near)],
        [("hbm", left, bf16)] * 4
        + [("hbm", block, bf16), ("vmem", (rows, width), f32)]
        + [("vmem", (rows, width), bf16)] * 2,
        [
            pltpu.VMEM((rows, width), bf16),
            pltpu.VMEM(block, bf16),
            pltpu.VMEM((width, rows), f32),
            pltpu.VMEM((4,) + left, bf16),
            dma((9,)),
        ],
    )
    params32 = slot_params.astype(f32).T
    slot_norm = jnp.sqrt(jnp.sum(params32 * params32, axis=1, keepdims=True) + epsilon)
    unit_t32 = params32 / slot_norm
    unit_t = unit_t32.astype(bf16)
    perm = one_hot(
        np.arange(slots * 2 * images).reshape(slots, 2, images).transpose(1, 2, 0).reshape(-1)
    )
    sources = n_img * n_exp
    count = sources * images
    shuffle = one_hot(
        np.arange(count * owned * 2)
        .reshape(sources, owned, 2, images)
        .transpose(1, 2, 0, 3)
        .reshape(-1)
    )
    far, mixed, unit_t, perm, shuffle = lax.optimization_barrier(
        (far, mixed, unit_t, perm, shuffle)
    )
    keep_left, send_left = lefts[:2], lefts[2:]
    far_near = swap(far, "img", n_img, 1)
    far_copy, mixed = call(
        functools.partial(partial_kernel, 2),
        "partial",
        6,
        [("vmem", ctx), ("vmem", mixed), ("vmem", far)],
        [("hbm", block, bf16), ("vmem", (rows, width), f32)],
        [dma((1,))],
    )
    stats = [((rows, width), bf16), ((rows, -(-(2 * slots + 1) // 128) * 128), f32)]
    message = slots * 2 * images
    far_near_copy, *kept_stats, out = call(
        functools.partial(forward_kernel, images, factor, 3),
        "forward",
        20,
        [
            ("vmem", ctx), ("vmem", mixed), ("vmem", cot), ("free", unit_t), ("free", perm),
            ("vmem", far_near),
        ],
        [("hbm", block, bf16)]
        + [("vmem", *s) for s in stats]
        + [("hbm", (message, width), bf16)],
        [
            pltpu.VMEM((message, width), bf16),
            dma((2,)),
        ],
    )

    both = ("img", "exp")
    got = out.reshape(n_exp, -1, width)
    got = lax.all_to_all(got, "exp", split_axis=0, concat_axis=0, tiled=True)
    got = lax.all_gather(got, "img", axis=0, tiled=True).reshape(-1, width)

    step = min(hidden, 512)
    kept = [((owned * 2, count, width), bf16)] + [((owned, count, hidden), bf16)] * 2
    slot_rows, act, grad_pre, back = call(
        functools.partial(expert_kernel, step, 3),
        "experts",
        28,
        [("vmem", got), ("free", shuffle), ("hbm", expert_in), ("hbm", expert_out)],
        [("hbm", *s) for s in kept] + [("hbm", got.shape, bf16)],
        [
            pltpu.VMEM(expert_in.shape, bf16),
            pltpu.VMEM(expert_out.shape, bf16),
            *[pltpu.VMEM(*s) for s in kept],
            pltpu.VMEM((owned * 2, count, width), bf16),
            pltpu.VMEM(got.shape, bf16),
            dma((2 * owned * (hidden // step) + 4,)),
        ],
    )
    back = back.reshape(sources, -1, width)
    back = lax.all_to_all(back, both, split_axis=0, concat_axis=0, tiled=True)

    cuts = 4
    fixed = lambda x: pltpu.with_memory_space_constraint(x, pltpu.HBM)
    part = lambda s: pl.BlockSpec((1,) + s, lambda j, f: (j, 0, 0))
    grad_expert_in, grad_expert_out = pl.pallas_call(
        grads_kernel,
        grid=(owned, cuts),
        in_specs=[
            pl.BlockSpec((2, count, width), lambda j, f: (j, 0, 0)),
            part((count, hidden)),
            part((count, hidden)),
        ],
        out_specs=[
            pl.BlockSpec((1, width // cuts, hidden), lambda j, f: (j, f, 0)),
            pl.BlockSpec((1, hidden // cuts, width), lambda j, f: (j, f, 0)),
        ],
        out_shape=[pltpu.HBM(expert_in.shape, bf16), pltpu.HBM(expert_out.shape, bf16)],
        compiler_params=pltpu.CompilerParams(vmem_limit_bytes=14 * 1024 * 1024),
        name="expert_grads",
    )(fixed(slot_rows), fixed(act), fixed(grad_pre))
    back, grad_expert_in, grad_expert_out = lax.optimization_barrier(
        (back, grad_expert_in, grad_expert_out)
    )

    n = width // 2
    grad_residual, send, side = call(
        functools.partial(backward_kernel, images, factor),
        "backward",
        24,
        [("vmem", back.reshape(n_img, -1, width)), ("free", perm), ("free", unit_t)]
        + [("vmem", x) for x in (*kept_stats, cot)]
        + [("hbm", x) for x in send_left],
        [
            ("hbm", (rows, width), bf16),
            ("vmem", (2 * n + 4 * slots, half), bf16),
            ("vmem", (2 * slots, half), f32),
        ],
        [
            pltpu.VMEM(left, bf16),
            pltpu.VMEM(left, bf16),
            pltpu.VMEM((rows, width), bf16),
            dma((2 + images,)),
        ],
    )

    got = swap(send, "img", n_img, 1)
    (keep,) = call(
        keep_kernel,
        "keep",
        8,
        [("hbm", x) for x in (*keep_left, grad_residual)],
        [("vmem", (2 * n, half), bf16)],
        [pltpu.VMEM(left, bf16), pltpu.VMEM(left, bf16), pltpu.VMEM((rows, width), bf16), dma((3,))],
    )

    def after(n):
        rest = (("vmem", (n, half), bf16),) * 2 + (("vmem", (slots, half), f32),)
        return [*rest, ("vmem", (n, half), bf16), ("vmem", (n + 2 * slots, half), bf16)]

    n = n // 2
    p, q, side, send_p, send_q = call(
        first_kernel,
        "first",
        6,
        [("vmem", keep), ("vmem", side), ("vmem", got)],
        after(n),
    )
    got_p = swap(send_p, "img", n_img, 2)
    got_q = swap(send_q, "exp", n_exp, 1)
    projection = (proj_weight, near_copy, far_copy, far_near_copy)
    (grad_context,) = call(
        context_kernel,
        "context",
        12,
        [("hbm", x) for x in (grad_residual, *projection)],
        [("hbm", (rows, width), bf16)],
        [
            pltpu.VMEM((rows, width), bf16),
            pltpu.VMEM((n_img,) + block, bf16),
            pltpu.VMEM((n_img, rows, deep), bf16),
            dma((1 + 2 * n_img,)),
        ],
    )
    got_p, got_q, grad_context = lax.optimization_barrier((got_p, got_q, grad_context))
    n = n // 2
    p, q, side, send_p, send_q = call(
        second_kernel, "second", 4, [("vmem", x) for x in (p, q, side, got_p, got_q)], after(n)
    )
    got_p = swap(send_p, "exp", n_exp, 1)
    got_q = swap(send_q, "img", n_img, 2)
    groups = n_exp // 2
    n = n // groups
    piece = slots // groups
    tail = -(-2 * piece // 8) * 8
    block = (2 * n + tail, half)
    keep, side, *sends = call(
        third_kernel,
        "third",
        4,
        [("vmem", x) for x in (p, q, side, got_p, got_q)],
        [("vmem", (2 * n, half), f32), ("vmem", (piece, half), f32)]
        + [("vmem", block, bf16)] * (groups - 1),
    )
    gots = [swap(s, "exp", n_exp, 2 * m) for m, s in enumerate(sends, 1)]
    (held,) = call(
        fourth_kernel,
        "fourth",
        4,
        [("vmem", x) for x in (keep, side, *gots)],
        [("vmem", block, bf16)],
    )
    held = [held] + [swap(held, "exp", n_exp, 2 * m) for m in range(1, groups)]
    others = [swap(x, "exp", n_exp, 1) for x in held]
    grad_proj, grad_slots = call(
        functools.partial(last_kernel, piece),
        "last",
        6,
        [("vmem", x) for x in (*held, *others)] + [("free", unit_t32), ("free", slot_norm)],
        [("hbm", (n_exp, n, width), f32), ("hbm", (slots, width), f32)],
        [
            pltpu.VMEM((n_exp, n, width), f32),
            pltpu.VMEM((n_exp, piece, half), f32),
            pltpu.VMEM((slots, width), f32),
            dma((n_exp + 1,)),
        ],
    )
    return (
        grad_context.reshape(images, tokens, width),
        grad_residual.reshape(images, tokens, width),
        grad_proj.reshape(-1, width),
        grad_slots.T,
        grad_expert_in,
        grad_expert_out,
    )


def solution(mesh):
    n_img, n_exp = mesh.shape["img"], mesh.shape["exp"]
    placed = (
        P(("img", "exp"), None, None),
        P(("img", "exp"), None, None),
        P(("img", "exp"), None, None),
        P("img", None),
        P(),
        P("exp", None, "img"),
        P("exp", "img", None),
    )
    return jax.shard_map(
        functools.partial(shards, n_img, n_exp),
        mesh=mesh,
        in_specs=placed,
        out_specs=(
            P(("img", "exp"), None, None),
            P(("img", "exp"), None, None),
            P("img", None),
            P(),
            P("exp", None, "img"),
            P("exp", "img", None),
        ),
        check_vma=False,
    )
```

```python
import functools
import math

import jax
import jax.numpy as jnp
import numpy as np
from jax import lax
from jax.experimental import pallas as pl
from jax.experimental.pallas import tpu as pltpu
from jax.sharding import PartitionSpec as P

logit_scale = 48.0
epsilon = 1e-06
f32 = jnp.float32
bf16 = jnp.bfloat16
spaces = {"vmem": pltpu.VMEM, "hbm": pltpu.HBM, "free": pltpu.VMEM}


def call(kernel, name, mib, inputs, outputs, scratch=()):
    def held(where, x):
        fixed = where in ("vmem", "hbm")
        return pltpu.with_memory_space_constraint(x, spaces[where]) if fixed else x

    return pl.pallas_call(
        kernel,
        in_specs=[pl.BlockSpec(memory_space=spaces[where]) for where, _ in inputs],
        out_specs=[pl.BlockSpec(memory_space=spaces[where]) for where, _, _ in outputs],
        out_shape=[spaces[where](s, t) for where, s, t in outputs],
        scratch_shapes=list(scratch),
        compiler_params=pltpu.CompilerParams(vmem_limit_bytes=mib * 1024 * 1024),
        name=name,
    )(*[held(where, x) for where, x in inputs])


def fetch_kernel(*refs):
    n = len(refs) // 2
    mover = Mover(refs[-1])
    pairs = zip(refs[:n], refs[n : 2 * n], strict=True)
    for copy in [mover.start(x.at[pl.ds(0, y.shape[0])], y) for x, y in pairs]:
        copy.wait()


def swap(x, axis, size, bit):
    return lax.ppermute(x, axis, [(i, i ^ bit) for i in range(size)])


def tree(parts):
    while len(parts) > 1:
        parts = [parts[k] + parts[k + 1] for k in range(0, len(parts), 2)]
    return parts[0]


def dot(a, b):
    return jnp.dot(a, b, preferred_element_type=f32)


def dot_last(a, b):
    return lax.dot_general(a, b, (((1,), (1,)), ((), ())), preferred_element_type=f32)


def dot_first(a, b):
    return lax.dot_general(a, b, (((0,), (0,)), ((), ())), preferred_element_type=f32)


def one_hot(order):
    return (jnp.asarray(order, jnp.int32)[:, None] == jnp.arange(order.size)).astype(bf16)


def halves(x):
    n = x.shape[0] // 2
    return x[:n], x[n:]


def high_low(x):
    high = x.astype(bf16).astype(f32)
    return jnp.concatenate([high, (x - high).astype(bf16).astype(f32)], axis=0)


def joined(x):
    high, low = halves(x)
    return high + low


def gelu_both(pre):
    scale = math.sqrt(2.0 / math.pi)
    square = pre * pre
    bent = jnp.tanh(scale * (pre + 0.044715 * (square * pre)))
    cdf = 0.5 * (1.0 + bent)
    slope = 0.5 * (1.0 - bent * bent) * (scale * (1.0 + (3 * 0.044715) * square))
    return pre * cdf, cdf + pre * slope


class Mover:
    def __init__(self, sems):
        self.sems, self.used = sems, 0

    def start(self, source, target):
        copy = pltpu.make_async_copy(source, target, self.sems.at[self.used])
        self.used += 1
        copy.start()
        return copy


def prepare_kernel(n_img, n_exp, ctx_hbm, res_hbm, cot_hbm, own_hbm, near, *refs):
    lefts, near_out, mixed, ctx, cot = refs[:4], *refs[4:8]
    res, own, turned, kept, sems = refs[8:]
    mover = Mover(sems)
    get_ctx = mover.start(ctx_hbm, ctx)
    get_own = mover.start(own_hbm, own)
    get_res = mover.start(res_hbm, res)
    out = [mover.start(near, near_out), mover.start(cot_hbm, cot)]
    sub = turned.shape[0] // (n_img * n_exp)
    get_ctx.wait()
    turned[...] = ctx[...].astype(f32).T
    for core in range(2):
        for x in range(2):
            for y in range(2):
                block = []
                for z in range(n_exp // 2):
                    at = ((lax.axis_index("img") ^ (2 * x + core)) * n_exp + (lax.axis_index("exp") ^ (2 * z + y))) * sub
                    block.append(turned[pl.ds(pl.multiple_of(at, sub), sub), :])
                block = jnp.concatenate(block, axis=0).astype(bf16)
                n = block.shape[0]
                kept[2 * core, (2 * x + y) * n : (2 * x + y + 1) * n, :] = block
                kept[2 * core + 1, (2 * y + x) * n : (2 * y + x + 1) * n, :] = block
    out += [mover.start(kept.at[k], left) for k, left in enumerate(lefts)]
    get_own.wait()
    get_res.wait()
    deep = own.shape[0]
    first = pl.ds(pl.multiple_of(lax.axis_index("img") * deep, deep), deep)
    second = pl.ds(pl.multiple_of((lax.axis_index("img") ^ 1) * deep, deep), deep)
    mixed[...] = res[...].astype(f32) + dot(ctx[:, first], own[...]) + dot(ctx[:, second], near[...])
    for copy in out:
        copy.wait()


def partial_kernel(taken, ctx, start, block, block_out, total, sems):
    deep = block.shape[0]
    columns = pl.ds(pl.multiple_of((lax.axis_index("img") ^ taken) * deep, deep), deep)
    out = Mover(sems).start(block, block_out)
    total[...] = start[...] + dot(ctx[:, columns], block[...])
    out.wait()


def inverse_of(stream32):
    return lax.rsqrt(jnp.mean(stream32 * stream32, axis=-1, keepdims=True) + epsilon)


def softmaxes(expo):
    dispatch32 = expo / jnp.sum(expo, axis=0, keepdims=True)
    return dispatch32, expo / jnp.sum(expo, axis=1, keepdims=True)


def forward_kernel(images, factor, taken, ctx, start, cot, unit, perm, block, *refs):
    block_out, stream_v, expo_v, slots_hbm, slots_v, sems = refs
    mover = Mover(sems)
    deep = block.shape[0]
    tokens = cot.shape[0] // images
    columns = pl.ds(pl.multiple_of((lax.axis_index("img") ^ taken) * deep, deep), deep)
    out = [mover.start(block, block_out)]
    slot_in, grad_out = [], []
    for b in range(images):
        at = pl.ds(b * tokens, tokens)
        mixed = start[at, :] + dot(ctx[at, columns], block[...])
        stream = mixed.astype(bf16)
        stream_v[at, :] = stream
        stream32 = stream.astype(f32)
        inverse = inverse_of(stream32)
        normed = (stream32 * inverse).astype(bf16)
        expo = jnp.exp(factor * dot_last(normed, unit[...]))
        dispatch32, combine32 = softmaxes(expo)
        expo_v[at, :] = expo
        slot_in.append(dot_first(dispatch32.astype(bf16), normed).astype(bf16))
        grad_out.append(dot_first(combine32.astype(bf16), cot[at, :]).astype(bf16))
    parts = jnp.concatenate(slot_in + grad_out, axis=0)
    slots_v[...] = dot_first(perm[...], parts).astype(bf16)
    out.append(mover.start(slots_v, slots_hbm))
    for copy in out:
        copy.wait()


def expert_kernel(own, near, across, diagonal, perm, first, second, *refs):
    rows_hbm, act_hbm, grad_hbm, keep, send = refs[:5]
    rows, act, grad_pre, held, sems = refs[5:]
    mover = Mover(sems)
    owned = first.shape[0]
    got = jnp.concatenate([own[...], across[...], near[...], diagonal[...]], axis=0)
    rows[...] = dot(perm[...], got).astype(bf16).reshape(rows.shape)
    out = [mover.start(rows, rows_hbm)]
    for j in range(owned):
        first_w, second_w = first[j], second[j]
        value, slope = gelu_both(dot(rows[2 * j], first_w))
        value = value.astype(bf16)
        act[j] = value
        grad = (dot_last(rows[2 * j + 1], second_w) * slope).astype(bf16)
        grad_pre[j] = grad
        held[2 * j] = dot(value, second_w).astype(bf16)
        held[2 * j + 1] = dot_last(grad, first_w).astype(bf16)
    out.append(mover.start(act, act_hbm))
    out.append(mover.start(grad_pre, grad_hbm))
    back = dot_first(perm[...], held[...].reshape(got.shape)).astype(bf16)
    keep[...], send[...] = halves(back)
    for copy in out:
        copy.wait()


def pair_kernel(keep, got, out_hbm, out, sems):
    mover = Mover(sems)
    total = (keep[...].astype(f32) + got[...].astype(f32)).astype(bf16)
    puts = []
    for x, block in enumerate(halves(total)):
        out[x] = block
        puts.append(mover.start(out.at[x], out_hbm.at[(lax.axis_index("img") >> 1) ^ x]))
    for put in puts:
        put.wait()


def grads_kernel(rows, act, grad_pre, grad_first, grad_second):
    f = pl.program_id(1)
    deep = grad_second.shape[1]
    at = pl.ds(pl.multiple_of(f * deep, deep), deep)
    grad_second[0] = dot_first(act[0, :, at], rows[1]).astype(bf16)
    deep = grad_first.shape[1]
    at = pl.ds(pl.multiple_of(f * deep, deep), deep)
    grad_first[0] = dot_first(rows[0, :, at], grad_pre[0]).astype(bf16)


def backward_kernel(images, factor, back, perm, unit_t, *refs):
    stream, expo, cot, left_p, left_q_hbm, grad_hbm, send, side_out, left_q, grad_v, sems = refs
    mover = Mover(sems)
    get = mover.start(left_q_hbm, left_q)
    tokens = cot.shape[0] // images
    slots = unit_t.shape[0]
    half = send.shape[1]
    total = tree([back[r].astype(f32) for r in range(back.shape[0])]).astype(bf16)
    parts = dot(perm[...], total).astype(bf16)
    unit_sum = 0.0
    out = []
    for b in range(images):
        at = pl.ds(b * tokens, tokens)
        slot_out = parts[b * slots : (b + 1) * slots]
        grad_slot_in = parts[(images + b) * slots : (images + b + 1) * slots]
        upstream = cot[at, :]
        stream32 = stream[at, :].astype(f32)
        inv = inverse_of(stream32)
        normed32 = stream32 * inv
        normed = normed32.astype(bf16)
        dispatch32, combine32 = softmaxes(expo[at, :])
        grad_combine = dot_last(upstream, slot_out)
        grad_dispatch = dot_last(normed, grad_slot_in)
        logits = combine32 * (
            grad_combine - jnp.sum(combine32 * grad_combine, axis=1, keepdims=True)
        ) + dispatch32 * (
            grad_dispatch - jnp.sum(dispatch32 * grad_dispatch, axis=0, keepdims=True)
        )
        logits = logits.astype(bf16)
        grad_normed = dot(dispatch32.astype(bf16), grad_slot_in) + factor * dot(logits, unit_t[...])
        unit_sum = unit_sum + dot_first(logits, normed)
        grad = upstream.astype(f32) + inv * (
            grad_normed - normed32 * jnp.mean(normed32 * grad_normed, axis=-1, keepdims=True)
        )
        grad_v[at, :] = grad.astype(bf16)
        out.append(mover.start(grad_v.at[at, :], grad_hbm.at[at, :]))
    n = left_p.shape[0]
    send[:n, :] = dot(left_p[...], grad_v[:, :half]).astype(bf16)
    get.wait()
    send[n : 2 * n, :] = dot(left_q[...], grad_v[:, half:]).astype(bf16)
    unit_sum = factor * unit_sum
    side = high_low(jnp.concatenate([unit_sum[:, :half], unit_sum[:, half:]], axis=0))
    send[2 * n :, :] = side.astype(bf16)
    side_out[...] = joined(side)
    for copy in out:
        copy.wait()


def keep_kernel(left_p_hbm, left_q_hbm, grad_hbm, out, left_p, left_q, grad, sems):
    mover = Mover(sems)
    gets = [
        mover.start(grad_hbm, grad),
        mover.start(left_p_hbm, left_p),
        mover.start(left_q_hbm, left_q),
    ]
    half = out.shape[1]
    n = left_p.shape[0]
    gets[0].wait()
    gets[1].wait()
    out[:n, :] = dot(left_p[...], grad[:, :half]).astype(bf16)
    gets[2].wait()
    out[n:, :] = dot(left_q[...], grad[:, half:]).astype(bf16)


def chosen(bit, low, high):
    return jnp.where(bit == 0, low, high)


def first_kernel(keep, side, got, p_out, q_out, side_out, send_p, send_q):
    n = keep.shape[0] // 2
    p0, p1 = halves(keep[:n, :].astype(f32) + got[:n, :].astype(f32))
    q0, q1 = halves(keep[n:, :].astype(f32) + got[n : 2 * n, :].astype(f32))
    low, high = halves(side[...] + joined(got[2 * n :, :].astype(f32)))
    bit = lax.axis_index("exp") & 1
    side_out[...] = chosen(bit, low, high)
    p_out[...] = p0.astype(bf16)
    q_out[...] = q0.astype(bf16)
    send_p[...] = p1.astype(bf16)
    other = high_low(chosen(bit, high, low))
    send_q[...] = jnp.concatenate([q1, other], axis=0).astype(bf16)


def second_kernel(p_in, q_in, side, got_p, got_q, p_out, q_out, side_out, send_p, send_q):
    n = p_in.shape[0]
    got = got_q[...].astype(f32)
    p0, p1 = halves(p_in[...].astype(f32) + got_p[...].astype(f32))
    q0, q1 = halves(q_in[...].astype(f32) + got[:n])
    mine = high_low(side[...] + joined(got[n:]))
    side_out[...] = joined(mine)
    p_out[...] = p0.astype(bf16)
    q_out[...] = q0.astype(bf16)
    send_p[...] = p1.astype(bf16)
    send_q[...] = jnp.concatenate([q1, mine], axis=0).astype(bf16)


def side_rows(piece):
    piece = high_low(piece)
    short = -piece.shape[0] % 8
    if short:
        piece = jnp.concatenate([piece, jnp.zeros((short, piece.shape[1]), f32)], axis=0)
    return piece


def third_kernel(p_in, q_in, side, got_p, got_q, keep, side_out, *sends):
    n = p_in.shape[0]
    groups = len(sends) + 1
    got = got_q[...].astype(f32)
    p = p_in[...].astype(f32) + got_p[...].astype(f32)
    q = q_in[...].astype(f32) + got[:n]
    total = side[...] + joined(got[n:])
    deep = total.shape[0] // groups
    pieces = [total[m * deep : (m + 1) * deep] for m in range(groups)]
    bit = 1
    while bit < groups:
        flip = lax.axis_index("exp") & (2 * bit)
        pieces = [chosen(flip, pieces[m], pieces[m ^ bit]) for m in range(groups)]
        bit *= 2
    side_out[...] = pieces[0]
    n = n // groups
    keep[...] = jnp.concatenate([p[:n], q[:n]], axis=0)
    for m, send in enumerate(sends, 1):
        at = slice(m * n, (m + 1) * n)
        send[...] = jnp.concatenate([p[at], q[at], side_rows(pieces[m])], axis=0).astype(bf16)


def fourth_kernel(keep, side, *refs):
    gots, own = refs[:-1], refs[-1]
    n, deep = keep.shape[0], side.shape[0]
    gots = [g[...].astype(f32) for g in gots]
    total = tree([side[...]] + [joined(g[n : n + 2 * deep]) for g in gots])
    total = jnp.concatenate([tree([keep[...]] + [g[:n] for g in gots]), side_rows(total)], axis=0)
    own[...] = total.astype(bf16)


def context_kernel(grad_hbm, own_hbm, near_hbm, far_hbm, far_near_hbm, out_hbm, grad, blocks, out, sems):
    mover = Mover(sems)
    deep = blocks.shape[1]
    get = mover.start(grad_hbm, grad)
    sources = (own_hbm, near_hbm, far_hbm, far_near_hbm)
    gets = [mover.start(source, blocks.at[r]) for r, source in enumerate(sources)]
    get.wait()
    puts = []
    for r, get in enumerate(gets):
        get.wait()
        columns = pl.ds(pl.multiple_of((lax.axis_index("img") ^ r) * deep, deep), deep)
        out[r] = dot_last(grad[...], blocks[r]).astype(bf16)
        puts.append(mover.start(out.at[r], out_hbm.at[:, columns]))
    for put in puts:
        put.wait()


def last_kernel(deep, *refs):
    blocks, refs = refs[:-8], refs[-8:]
    unit_t, slot_norm, grad_hbm, slots_hbm, grad, side, slots_out, sems = refs
    mover = Mover(sems)
    groups = len(blocks) // 2
    n, half = grad.shape[1], blocks[0].shape[1]
    puts = []
    for y in range(2):
        for z in range(groups):
            block = blocks[y * groups + z][...].astype(f32)
            at = lax.axis_index("exp") ^ (2 * z + y)
            k = 2 * z + y
            grad[k, :, :half] = block[:n]
            grad[k, :, half:] = block[n : 2 * n]
            puts.append(mover.start(grad.at[k], grad_hbm.at[at]))
            side[(at & 1) * groups + (at >> 1)] = joined(block[2 * n : 2 * n + 2 * deep])
    total = jnp.concatenate([side[k] for k in range(side.shape[0])], axis=0)
    total = jnp.concatenate(halves(total), axis=1)
    unit = unit_t[...]
    along = jnp.sum(unit * total, axis=1, keepdims=True)
    slots_out[...] = (total - unit * along) / slot_norm[...]
    puts.append(mover.start(slots_out, slots_hbm))
    for put in puts:
        put.wait()


def shards(n_img, n_exp, context, residual, cotangent, proj_weight, slot_params, expert_in, expert_out):
    images, tokens, width = context.shape
    rows = images * tokens
    owned, _, hidden = expert_in.shape
    slots = slot_params.shape[1]
    half = width // 2
    factor = logit_scale / math.sqrt(width)
    flat_ctx = context.reshape(rows, width)
    flat_cot = cotangent.reshape(rows, width)
    flat_res = residual.reshape(rows, width)
    dma = pltpu.SemaphoreType.DMA

    far = swap(proj_weight, "img", n_img, 2)
    perm = one_hot(
        np.arange(slots * 2 * images).reshape(slots, 2, images).transpose(1, 2, 0).reshape(-1)
    )
    proj_again, perm = lax.optimization_barrier((proj_weight, perm))
    near = swap(proj_again, "img", n_img, 1)
    deep = proj_weight.shape[0]
    block = (deep, width)
    left = (width // 2, rows)
    *lefts, near_copy, mixed, ctx, cot = call(
        functools.partial(prepare_kernel, n_img, n_exp),
        "prepare",
        16,
        [("hbm", x) for x in (flat_ctx, flat_res, flat_cot, proj_weight)] + [("vmem", near)],
        [("hbm", left, bf16)] * 4
        + [("hbm", block, bf16), ("vmem", (rows, width), f32)]
        + [("vmem", (rows, width), bf16)] * 2,
        [
            pltpu.VMEM((rows, width), bf16),
            pltpu.VMEM(block, bf16),
            pltpu.VMEM((width, rows), f32),
            pltpu.VMEM((4,) + left, bf16),
            dma((9,)),
        ],
    )
    params32 = slot_params.astype(f32).T
    slot_norm = jnp.sqrt(jnp.sum(params32 * params32, axis=1, keepdims=True) + epsilon)
    unit_t32 = params32 / slot_norm
    unit_t = unit_t32.astype(bf16)
    sources = n_img * n_exp
    far_img = n_img // 2
    count = sources * images
    shuffle = one_hot(
        np.arange(count * owned * 2)
        .reshape(sources, owned, 2, images)
        .transpose(1, 2, 0, 3)
        .reshape(-1)
    )
    far, mixed, unit_t, perm, shuffle = lax.optimization_barrier(
        (far, mixed, unit_t, perm, shuffle)
    )
    keep_left, send_left = lefts[:2], lefts[2:]
    far_near = swap(far, "img", n_img, 1)
    far_copy, mixed = call(
        functools.partial(partial_kernel, 2),
        "partial",
        6,
        [("vmem", ctx), ("vmem", mixed), ("vmem", far)],
        [("hbm", block, bf16), ("vmem", (rows, width), f32)],
        [dma((1,))],
    )
    stats = [((rows, width), bf16), ((rows, slots), f32)]
    message = slots * 2 * images
    far_near_copy, *kept_stats, out = call(
        functools.partial(forward_kernel, images, factor, 3),
        "forward",
        20,
        [
            ("vmem", ctx), ("vmem", mixed), ("vmem", cot), ("free", unit_t), ("free", perm),
            ("vmem", far_near),
        ],
        [("hbm", block, bf16)]
        + [("vmem", *s) for s in stats]
        + [("hbm", (message, width), bf16)],
        [
            pltpu.VMEM((message, width), bf16),
            dma((2,)),
        ],
    )

    got = lax.all_to_all(out.reshape(n_exp, -1, width), "exp", 0, 0, tiled=True)
    got = got.reshape(-1, width)
    got, first, second = lax.optimization_barrier((got, expert_in, expert_out))
    across = swap(got, "img", n_img, 2)
    near = swap(got, "img", n_img, 1)
    first, second = call(
        fetch_kernel,
        "weights",
        4,
        [("hbm", first), ("hbm", second)],
        [("vmem", first.shape, bf16), ("vmem", second.shape, bf16)],
        [dma((2,))],
    )
    across, first, second = lax.optimization_barrier((across, first, second))
    diagonal = swap(across, "img", n_img, 1)

    kept = [((owned * 2, count, width), bf16)] + [((owned, count, hidden), bf16)] * 2
    returned = (far_img * got.shape[0], width)
    slot_rows, act, grad_pre, keep, send = call(
        expert_kernel,
        "experts",
        16,
        [("vmem", x) for x in (got, near, across, diagonal)]
        + [("free", shuffle), ("vmem", first), ("vmem", second)],
        [("hbm", *s) for s in kept] + [("vmem", returned, bf16)] * 2,
        [
            *[pltpu.VMEM(*s) for s in kept],
            pltpu.VMEM((owned * 2, count, width), bf16),
            dma((3,)),
        ],
    )
    groups = [
        [(2 * x + c) * n_exp + e for x in range(far_img) for e in range(n_exp)] for c in range(2)
    ]
    near = swap(send, "img", n_img, 1)
    (back,) = call(
        pair_kernel,
        "pair",
        4,
        [("vmem", keep), ("vmem", near)],
        [("hbm", (far_img,) + got.shape, bf16)],
        [pltpu.VMEM((far_img,) + got.shape, bf16), dma((far_img,))],
    )
    back = back.reshape(far_img * n_exp, -1, width)
    back = lax.all_to_all(
        back, ("img", "exp"), 0, 0, axis_index_groups=groups, tiled=True
    )

    cuts = 4
    fixed = lambda x: pltpu.with_memory_space_constraint(x, pltpu.HBM)
    part = lambda s: pl.BlockSpec((1,) + s, lambda j, f: (j, 0, 0))
    grad_expert_in, grad_expert_out = pl.pallas_call(
        grads_kernel,
        grid=(owned, cuts),
        in_specs=[
            pl.BlockSpec((2, count, width), lambda j, f: (j, 0, 0)),
            part((count, hidden)),
            part((count, hidden)),
        ],
        out_specs=[
            pl.BlockSpec((1, width // cuts, hidden), lambda j, f: (j, f, 0)),
            pl.BlockSpec((1, hidden // cuts, width), lambda j, f: (j, f, 0)),
        ],
        out_shape=[pltpu.HBM(expert_in.shape, bf16), pltpu.HBM(expert_out.shape, bf16)],
        compiler_params=pltpu.CompilerParams(vmem_limit_bytes=14 * 1024 * 1024),
        name="expert_grads",
    )(fixed(slot_rows), fixed(act), fixed(grad_pre))
    (left_p,) = call(
        fetch_kernel, "left", 4, [("hbm", send_left[0])], [("vmem", left, bf16)], [dma((1,))]
    )
    back, grad_expert_in, grad_expert_out, left_p = lax.optimization_barrier(
        (back, grad_expert_in, grad_expert_out, left_p)
    )

    n = width // 2
    grad_residual, send, side = call(
        functools.partial(backward_kernel, images, factor),
        "backward",
        24,
        [("vmem", back.reshape(far_img, -1, width)), ("free", perm), ("free", unit_t)]
        + [("vmem", x) for x in (*kept_stats, cot, left_p)]
        + [("hbm", send_left[1])],
        [
            ("hbm", (rows, width), bf16),
            ("vmem", (2 * n + 4 * slots, half), bf16),
            ("vmem", (2 * slots, half), f32),
        ],
        [
            pltpu.VMEM(left, bf16),
            pltpu.VMEM((rows, width), bf16),
            dma((1 + images,)),
        ],
    )

    got = swap(send, "img", n_img, 1)
    (keep,) = call(
        keep_kernel,
        "keep",
        8,
        [("hbm", x) for x in (*keep_left, grad_residual)],
        [("vmem", (2 * n, half), bf16)],
        [pltpu.VMEM(left, bf16), pltpu.VMEM(left, bf16), pltpu.VMEM((rows, width), bf16), dma((3,))],
    )

    def after(n):
        rest = (("vmem", (n, half), bf16),) * 2 + (("vmem", (slots, half), f32),)
        return [*rest, ("vmem", (n, half), bf16), ("vmem", (n + 2 * slots, half), bf16)]

    n = n // 2
    p, q, side, send_p, send_q = call(
        first_kernel,
        "first",
        6,
        [("vmem", keep), ("vmem", side), ("vmem", got)],
        after(n),
    )
    got_p = swap(send_p, "img", n_img, 2)
    got_q = swap(send_q, "exp", n_exp, 1)
    projection = (proj_weight, near_copy, far_copy, far_near_copy)
    (grad_context,) = call(
        context_kernel,
        "context",
        12,
        [("hbm", x) for x in (grad_residual, *projection)],
        [("hbm", (rows, width), bf16)],
        [
            pltpu.VMEM((rows, width), bf16),
            pltpu.VMEM((n_img,) + block, bf16),
            pltpu.VMEM((n_img, rows, deep), bf16),
            dma((1 + 2 * n_img,)),
        ],
    )
    got_p, got_q, grad_context = lax.optimization_barrier((got_p, got_q, grad_context))
    n = n // 2
    p, q, side, send_p, send_q = call(
        second_kernel, "second", 4, [("vmem", x) for x in (p, q, side, got_p, got_q)], after(n)
    )
    got_p = swap(send_p, "exp", n_exp, 1)
    got_q = swap(send_q, "img", n_img, 2)
    groups = n_exp // 2
    n = n // groups
    piece = slots // groups
    tail = -(-2 * piece // 8) * 8
    block = (2 * n + tail, half)
    keep, side, *sends = call(
        third_kernel,
        "third",
        4,
        [("vmem", x) for x in (p, q, side, got_p, got_q)],
        [("vmem", (2 * n, half), f32), ("vmem", (piece, half), f32)]
        + [("vmem", block, bf16)] * (groups - 1),
    )
    gots = [swap(s, "exp", n_exp, 2 * m) for m, s in enumerate(sends, 1)]
    (held,) = call(
        fourth_kernel,
        "fourth",
        4,
        [("vmem", x) for x in (keep, side, *gots)],
        [("vmem", block, bf16)],
    )
    held = [held] + [swap(held, "exp", n_exp, 2 * m) for m in range(1, groups)]
    others = [swap(x, "exp", n_exp, 1) for x in held]
    grad_proj, grad_slots = call(
        functools.partial(last_kernel, piece),
        "last",
        6,
        [("vmem", x) for x in (*held, *others)] + [("free", unit_t32), ("free", slot_norm)],
        [("hbm", (n_exp, n, width), f32), ("hbm", (slots, width), f32)],
        [
            pltpu.VMEM((n_exp, n, width), f32),
            pltpu.VMEM((n_exp, piece, half), f32),
            pltpu.VMEM((slots, width), f32),
            dma((n_exp + 1,)),
        ],
    )
    return (
        grad_context.reshape(images, tokens, width),
        grad_residual.reshape(images, tokens, width),
        grad_proj.reshape(-1, width),
        grad_slots.T,
        grad_expert_in,
        grad_expert_out,
    )


def solution(mesh):
    n_img, n_exp = mesh.shape["img"], mesh.shape["exp"]
    placed = (
        P(("img", "exp"), None, None),
        P(("img", "exp"), None, None),
        P(("img", "exp"), None, None),
        P("img", None),
        P(),
        P("exp", None, "img"),
        P("exp", "img", None),
    )
    return jax.shard_map(
        functools.partial(shards, n_img, n_exp),
        mesh=mesh,
        in_specs=placed,
        out_specs=(
            P(("img", "exp"), None, None),
            P(("img", "exp"), None, None),
            P("img", None),
            P(),
            P("exp", None, "img"),
            P("exp", "img", None),
        ),
        check_vma=False,
    )
```

```python
import functools
import math

import jax
import jax.numpy as jnp
import numpy as np
from jax import lax
from jax.experimental import pallas as pl
from jax.experimental.pallas import tpu as pltpu
from jax.sharding import PartitionSpec as P

logit_scale = 48.0
epsilon = 1e-06
f32 = jnp.float32
bf16 = jnp.bfloat16
spaces = {"vmem": pltpu.VMEM, "hbm": pltpu.HBM, "free": pltpu.VMEM}


def call(kernel, name, mib, inputs, outputs, scratch=(), aliases=()):
    def held(where, x):
        fixed = where in ("vmem", "hbm")
        return pltpu.with_memory_space_constraint(x, spaces[where]) if fixed else x

    return pl.pallas_call(
        kernel,
        in_specs=[pl.BlockSpec(memory_space=spaces[where]) for where, _ in inputs],
        out_specs=[pl.BlockSpec(memory_space=spaces[where]) for where, _, _ in outputs],
        out_shape=[spaces[where](s, t) for where, s, t in outputs],
        scratch_shapes=list(scratch),
        input_output_aliases=dict(aliases),
        compiler_params=pltpu.CompilerParams(vmem_limit_bytes=mib * 1024 * 1024),
        name=name,
    )(*[held(where, x) for where, x in inputs])


def fetch_kernel(*refs):
    n = len(refs) // 2
    mover = Mover(refs[-1])
    pairs = zip(refs[:n], refs[n : 2 * n], strict=True)
    tails = [(x.at[pl.ds(x.shape[0] - y.shape[0], y.shape[0])], y) for x, y in pairs]
    for copy in [mover.start(x, y) for x, y in tails]:
        copy.wait()


def swap(x, axis, size, bit):
    return lax.ppermute(x, axis, [(i, i ^ bit) for i in range(size)])


def tree(parts):
    while len(parts) > 1:
        parts = [parts[k] + parts[k + 1] for k in range(0, len(parts), 2)]
    return parts[0]


def dot(a, b):
    return jnp.dot(a, b, preferred_element_type=f32)


def dot_last(a, b):
    return lax.dot_general(a, b, (((1,), (1,)), ((), ())), preferred_element_type=f32)


def dot_first(a, b):
    return lax.dot_general(a, b, (((0,), (0,)), ((), ())), preferred_element_type=f32)


def one_hot(order):
    return (jnp.asarray(order, jnp.int32)[:, None] == jnp.arange(order.size)).astype(bf16)


def halves(x):
    n = x.shape[0] // 2
    return x[:n], x[n:]


def high_low(x):
    high = x.astype(bf16).astype(f32)
    return jnp.concatenate([high, (x - high).astype(bf16).astype(f32)], axis=0)


def joined(x):
    high, low = halves(x)
    return high + low


def gelu_both(pre):
    scale = math.sqrt(2.0 / math.pi)
    square = pre * pre
    bent = jnp.tanh(scale * (pre + 0.044715 * (square * pre)))
    cdf = 0.5 * (1.0 + bent)
    slope = 0.5 * (1.0 - bent * bent) * (scale * (1.0 + (3 * 0.044715) * square))
    return pre * cdf, cdf + pre * slope


class Mover:
    def __init__(self, sems):
        self.sems, self.used = sems, 0

    def start(self, source, target):
        copy = pltpu.make_async_copy(source, target, self.sems.at[self.used])
        self.used += 1
        copy.start()
        return copy


def prepare_kernel(n_img, n_exp, ctx_hbm, res_hbm, cot_hbm, own_hbm, first_hbm, near, *refs):
    lefts, near_out, mixed, ctx, cot, early = refs[:4], *refs[4:9]
    res, own, turned, kept, sems = refs[9:]
    mover = Mover(sems)
    get_ctx = mover.start(ctx_hbm, ctx)
    get_own = mover.start(own_hbm, own)
    get_res = mover.start(res_hbm, res)
    out = [mover.start(near, near_out), mover.start(cot_hbm, cot)]
    sub = turned.shape[0] // (n_img * n_exp)
    get_ctx.wait()
    turned[...] = ctx[...].astype(f32).T
    for core in range(2):
        for x in range(2):
            for y in range(2):
                block = []
                for z in range(n_exp // 2):
                    at = ((lax.axis_index("img") ^ (2 * x + core)) * n_exp + (lax.axis_index("exp") ^ (2 * z + y))) * sub
                    block.append(turned[pl.ds(pl.multiple_of(at, sub), sub), :])
                block = jnp.concatenate(block, axis=0).astype(bf16)
                n = block.shape[0]
                kept[2 * core, (2 * x + y) * n : (2 * x + y + 1) * n, :] = block
                kept[2 * core + 1, (2 * y + x) * n : (2 * y + x + 1) * n, :] = block
    out += [mover.start(kept.at[k], left) for k, left in enumerate(lefts)]
    get_own.wait()
    get_res.wait()
    deep = own.shape[0]
    first = pl.ds(pl.multiple_of(lax.axis_index("img") * deep, deep), deep)
    second = pl.ds(pl.multiple_of((lax.axis_index("img") ^ 1) * deep, deep), deep)
    mixed[...] = res[...].astype(f32) + dot(ctx[:, first], own[...]) + dot(ctx[:, second], near[...])
    out.append(mover.start(first_hbm.at[pl.ds(0, early.shape[0])], early))
    for copy in out:
        copy.wait()


def partial_kernel(taken, ctx, start, block, block_out, total, sems):
    deep = block.shape[0]
    columns = pl.ds(pl.multiple_of((lax.axis_index("img") ^ taken) * deep, deep), deep)
    out = Mover(sems).start(block, block_out)
    total[...] = start[...] + dot(ctx[:, columns], block[...])
    out.wait()


def inverse_of(stream32):
    return lax.rsqrt(jnp.mean(stream32 * stream32, axis=-1, keepdims=True) + epsilon)


def softmaxes(expo):
    dispatch32 = expo / jnp.sum(expo, axis=0, keepdims=True)
    return dispatch32, expo / jnp.sum(expo, axis=1, keepdims=True)


def forward_kernel(images, factor, taken, ctx, start, cot, unit, perm, block, *refs):
    block_out, stream_v, expo_v, slots_v, sems = refs
    mover = Mover(sems)
    deep = block.shape[0]
    tokens = cot.shape[0] // images
    columns = pl.ds(pl.multiple_of((lax.axis_index("img") ^ taken) * deep, deep), deep)
    out = [mover.start(block, block_out)]
    slot_in, grad_out = [], []
    for b in range(images):
        at = pl.ds(b * tokens, tokens)
        mixed = start[at, :] + dot(ctx[at, columns], block[...])
        stream = mixed.astype(bf16)
        stream_v[at, :] = stream
        stream32 = stream.astype(f32)
        inverse = inverse_of(stream32)
        normed = (stream32 * inverse).astype(bf16)
        expo = jnp.exp(factor * dot_last(normed, unit[...]))
        dispatch32, combine32 = softmaxes(expo)
        expo_v[at, :] = expo
        slot_in.append(dot_first(dispatch32.astype(bf16), normed).astype(bf16))
        grad_out.append(dot_first(combine32.astype(bf16), cot[at, :]).astype(bf16))
    parts = jnp.concatenate(slot_in + grad_out, axis=0)
    slots_v[...] = dot_first(perm[...], parts).astype(bf16)
    for copy in out:
        copy.wait()


def expert_kernel(own, near, across, diagonal, perm, early, first, second, *refs):
    rows_hbm, act_hbm, grad_hbm, keep, send = refs[:5]
    rows, act, grad_pre, held, sems = refs[5:]
    mover = Mover(sems)
    owned = second.shape[0]
    early_count = early.shape[0]
    got = jnp.concatenate([own[...], across[...], near[...], diagonal[...]], axis=0)
    rows[...] = dot(perm[...], got).astype(bf16).reshape(rows.shape)
    out = [mover.start(rows, rows_hbm)]
    for j in range(owned):
        first_w = early[j] if j < early_count else first[j - early_count]
        second_w = second[j]
        value, slope = gelu_both(dot(rows[2 * j], first_w))
        value = value.astype(bf16)
        act[j] = value
        grad = (dot_last(rows[2 * j + 1], second_w) * slope).astype(bf16)
        grad_pre[j] = grad
        held[2 * j] = dot(value, second_w).astype(bf16)
        held[2 * j + 1] = dot_last(grad, first_w).astype(bf16)
    out.append(mover.start(act, act_hbm))
    out.append(mover.start(grad_pre, grad_hbm))
    back = dot_first(perm[...], held[...].reshape(got.shape)).astype(bf16)
    keep[...], send[...] = halves(back)
    for copy in out:
        copy.wait()


def pair_kernel(keep, got, out):
    n = out.shape[1]
    for x in range(out.shape[0]):
        at = pl.ds(x * n, n)
        total = keep[at, :].astype(f32) + got[at, :].astype(f32)
        out[(lax.axis_index("img") >> 1) ^ x] = total.astype(bf16)


def grads_kernel(cuts, rows_hbm, act_hbm, grad_hbm, left_hbm, cot_hbm, *refs):
    first_hbm, second_hbm, left, cot = refs[:4]
    refs = refs[4:]
    rows, act, grad_pre, first, second, sems = refs
    mover = Mover(sems)
    sources = (rows_hbm, act_hbm, grad_hbm)
    gets = [mover.start(x, y) for x, y in zip(sources, refs[:3], strict=True)]
    out = [mover.start(left_hbm, left), mover.start(cot_hbm, cot)]
    for get in gets:
        get.wait()
    for j in range(first.shape[0]):
        pairs = ((second, second_hbm, act[j], rows[2 * j + 1]), (first, first_hbm, rows[2 * j], grad_pre[j]))
        for made, made_hbm, a, b in pairs:
            deep = made.shape[1] // cuts
            for k in range(cuts):
                at = slice(k * deep, (k + 1) * deep)
                made[j, at, :] = dot_first(a[:, at], b).astype(bf16)
                out.append(mover.start(made.at[j, at, :], made_hbm.at[j, at, :]))
    for copy in out:
        copy.wait()


def backward_kernel(images, factor, back, perm, unit_t, *refs):
    stream, expo, cot, left_p, left_q_hbm, grad_hbm, send, side_out, left_q, grad_v, sems = refs
    mover = Mover(sems)
    get = mover.start(left_q_hbm, left_q)
    tokens = cot.shape[0] // images
    slots = unit_t.shape[0]
    half = send.shape[1]
    total = tree([back[r].astype(f32) for r in range(back.shape[0])]).astype(bf16)
    parts = dot(perm[...], total).astype(bf16)
    unit_sum = 0.0
    out = []
    for b in range(images):
        at = pl.ds(b * tokens, tokens)
        slot_out = parts[b * slots : (b + 1) * slots]
        grad_slot_in = parts[(images + b) * slots : (images + b + 1) * slots]
        upstream = cot[at, :]
        stream32 = stream[at, :].astype(f32)
        inv = inverse_of(stream32)
        normed32 = stream32 * inv
        normed = normed32.astype(bf16)
        dispatch32, combine32 = softmaxes(expo[at, :])
        grad_combine = dot_last(upstream, slot_out)
        grad_dispatch = dot_last(normed, grad_slot_in)
        logits = combine32 * (
            grad_combine - jnp.sum(combine32 * grad_combine, axis=1, keepdims=True)
        ) + dispatch32 * (
            grad_dispatch - jnp.sum(dispatch32 * grad_dispatch, axis=0, keepdims=True)
        )
        logits = logits.astype(bf16)
        grad_normed = dot(dispatch32.astype(bf16), grad_slot_in) + factor * dot(logits, unit_t[...])
        unit_sum = unit_sum + dot_first(logits, normed)
        grad = upstream.astype(f32) + inv * (
            grad_normed - normed32 * jnp.mean(normed32 * grad_normed, axis=-1, keepdims=True)
        )
        grad_v[at, :] = grad.astype(bf16)
        out.append(mover.start(grad_v.at[at, :], grad_hbm.at[at, :]))
    n = left_p.shape[0]
    send[:n, :] = dot(left_p[...], grad_v[:, :half]).astype(bf16)
    get.wait()
    send[n : 2 * n, :] = dot(left_q[...], grad_v[:, half:]).astype(bf16)
    unit_sum = factor * unit_sum
    side = high_low(jnp.concatenate([unit_sum[:, :half], unit_sum[:, half:]], axis=0))
    send[2 * n :, :] = side.astype(bf16)
    side_out[...] = joined(side)
    for copy in out:
        copy.wait()


def keep_kernel(left_p_hbm, left_q_hbm, grad_hbm, out, left_p, left_q, grad, sems):
    mover = Mover(sems)
    gets = [
        mover.start(grad_hbm, grad),
        mover.start(left_p_hbm, left_p),
        mover.start(left_q_hbm, left_q),
    ]
    half = out.shape[1]
    n = left_p.shape[0]
    gets[0].wait()
    gets[1].wait()
    out[:n, :] = dot(left_p[...], grad[:, :half]).astype(bf16)
    gets[2].wait()
    out[n:, :] = dot(left_q[...], grad[:, half:]).astype(bf16)


def chosen(bit, low, high):
    return jnp.where(bit == 0, low, high)


def first_kernel(keep, side, got, p_out, q_out, side_out, send_p, send_q):
    n = keep.shape[0] // 2
    p0, p1 = halves(keep[:n, :].astype(f32) + got[:n, :].astype(f32))
    q0, q1 = halves(keep[n:, :].astype(f32) + got[n : 2 * n, :].astype(f32))
    low, high = halves(side[...] + joined(got[2 * n :, :].astype(f32)))
    bit = lax.axis_index("exp") & 1
    side_out[...] = chosen(bit, low, high)
    p_out[...] = p0.astype(bf16)
    q_out[...] = q0.astype(bf16)
    send_p[...] = p1.astype(bf16)
    other = high_low(chosen(bit, high, low))
    send_q[...] = jnp.concatenate([q1, other], axis=0).astype(bf16)


def second_kernel(p_in, q_in, side, got_p, got_q, p_out, q_out, side_out, send_p, send_q):
    n = p_in.shape[0]
    got = got_q[...].astype(f32)
    p0, p1 = halves(p_in[...].astype(f32) + got_p[...].astype(f32))
    q0, q1 = halves(q_in[...].astype(f32) + got[:n])
    mine = high_low(side[...] + joined(got[n:]))
    side_out[...] = joined(mine)
    p_out[...] = p0.astype(bf16)
    q_out[...] = q0.astype(bf16)
    send_p[...] = p1.astype(bf16)
    send_q[...] = jnp.concatenate([q1, mine], axis=0).astype(bf16)


def side_rows(piece):
    piece = high_low(piece)
    short = -piece.shape[0] % 8
    if short:
        piece = jnp.concatenate([piece, jnp.zeros((short, piece.shape[1]), f32)], axis=0)
    return piece


def third_kernel(p_in, q_in, side, got_p, got_q, keep, side_out, *sends):
    n = p_in.shape[0]
    groups = len(sends) + 1
    got = got_q[...].astype(f32)
    p = p_in[...].astype(f32) + got_p[...].astype(f32)
    q = q_in[...].astype(f32) + got[:n]
    total = side[...] + joined(got[n:])
    deep = total.shape[0] // groups
    pieces = [total[m * deep : (m + 1) * deep] for m in range(groups)]
    bit = 1
    while bit < groups:
        flip = lax.axis_index("exp") & (2 * bit)
        pieces = [chosen(flip, pieces[m], pieces[m ^ bit]) for m in range(groups)]
        bit *= 2
    side_out[...] = pieces[0]
    n = n // groups
    keep[...] = jnp.concatenate([p[:n], q[:n]], axis=0)
    for m, send in enumerate(sends, 1):
        at = slice(m * n, (m + 1) * n)
        send[...] = jnp.concatenate([p[at], q[at], side_rows(pieces[m])], axis=0).astype(bf16)


def fourth_kernel(keep, side, *refs):
    gots, own = refs[:-1], refs[-1]
    n, deep = keep.shape[0], side.shape[0]
    gots = [g[...].astype(f32) for g in gots]
    total = tree([side[...]] + [joined(g[n : n + 2 * deep]) for g in gots])
    total = jnp.concatenate([tree([keep[...]] + [g[:n] for g in gots]), side_rows(total)], axis=0)
    own[...] = total.astype(bf16)


def context_kernel(grad_hbm, own_hbm, near_hbm, far_hbm, far_near_hbm, out_hbm, grad, blocks, out, sems):
    mover = Mover(sems)
    deep = blocks.shape[1]
    get = mover.start(grad_hbm, grad)
    sources = (own_hbm, near_hbm, far_hbm, far_near_hbm)
    gets = [mover.start(source, blocks.at[r]) for r, source in enumerate(sources)]
    get.wait()
    puts = []
    for r, get in enumerate(gets):
        get.wait()
        columns = pl.ds(pl.multiple_of((lax.axis_index("img") ^ r) * deep, deep), deep)
        out[r] = dot_last(grad[...], blocks[r]).astype(bf16)
        puts.append(mover.start(out.at[r], out_hbm.at[:, columns]))
    for put in puts:
        put.wait()


def settle(y, blocks, grad_hbm, side, grad, mover, deep):
    groups = len(blocks)
    n, half = grad.shape[1], blocks[0].shape[1]
    puts = []
    for z in range(groups):
        block = blocks[z][...].astype(f32)
        at = lax.axis_index("exp") ^ (2 * z + y)
        grad[z, :, :half] = block[:n]
        grad[z, :, half:] = block[n : 2 * n]
        puts.append(mover.start(grad.at[z], grad_hbm.at[at]))
        side[(at & 1) * groups + (at >> 1)] = joined(block[2 * n : 2 * n + 2 * deep])
    return puts


def settle_kernel(deep, *refs):
    blocks, (grad_hbm, side, grad, sems) = refs[:-4], refs[-4:]
    for put in settle(0, blocks, grad_hbm, side, grad, Mover(sems), deep):
        put.wait()


def last_kernel(deep, early, *refs):
    blocks, refs = refs[:-9], refs[-9:]
    unit_t, slot_norm, _, grad_hbm, slots_hbm, side, grad, slots_out, sems = refs
    mover = Mover(sems)
    side[...] = early[...]
    puts = settle(1, blocks, grad_hbm, side, grad, mover, deep)
    total = jnp.concatenate([side[k] for k in range(side.shape[0])], axis=0)
    total = jnp.concatenate(halves(total), axis=1)
    unit = unit_t[...]
    along = jnp.sum(unit * total, axis=1, keepdims=True)
    slots_out[...] = (total - unit * along) / slot_norm[...]
    puts.append(mover.start(slots_out, slots_hbm))
    for put in puts:
        put.wait()


def shards(n_img, n_exp, context, residual, cotangent, proj_weight, slot_params, expert_in, expert_out):
    images, tokens, width = context.shape
    rows = images * tokens
    owned, _, hidden = expert_in.shape
    slots = slot_params.shape[1]
    half = width // 2
    factor = logit_scale / math.sqrt(width)
    flat_ctx = context.reshape(rows, width)
    flat_cot = cotangent.reshape(rows, width)
    flat_res = residual.reshape(rows, width)
    dma = pltpu.SemaphoreType.DMA

    far = swap(proj_weight, "img", n_img, 2)
    perm = one_hot(
        np.arange(slots * 2 * images).reshape(slots, 2, images).transpose(1, 2, 0).reshape(-1)
    )
    proj_again, perm = lax.optimization_barrier((proj_weight, perm))
    near = swap(proj_again, "img", n_img, 1)
    deep = proj_weight.shape[0]
    block = (deep, width)
    left = (width // 2, rows)
    early = (1,) + expert_in.shape[1:]
    *lefts, near_copy, mixed, ctx, cot, early = call(
        functools.partial(prepare_kernel, n_img, n_exp),
        "prepare",
        16,
        [("hbm", x) for x in (flat_ctx, flat_res, flat_cot, proj_weight, expert_in)]
        + [("vmem", near)],
        [("hbm", left, bf16)] * 4
        + [("hbm", block, bf16), ("vmem", (rows, width), f32)]
        + [("vmem", (rows, width), bf16)] * 2
        + [("vmem", early, bf16)],
        [
            pltpu.VMEM((rows, width), bf16),
            pltpu.VMEM(block, bf16),
            pltpu.VMEM((width, rows), f32),
            pltpu.VMEM((4,) + left, bf16),
            dma((10,)),
        ],
    )
    params32 = slot_params.astype(f32).T
    slot_norm = jnp.sqrt(jnp.sum(params32 * params32, axis=1, keepdims=True) + epsilon)
    unit_t32 = params32 / slot_norm
    unit_t = unit_t32.astype(bf16)
    sources = n_img * n_exp
    far_img = n_img // 2
    count = sources * images
    shuffle = one_hot(
        np.arange(count * owned * 2)
        .reshape(sources, owned, 2, images)
        .transpose(1, 2, 0, 3)
        .reshape(-1)
    )
    far, mixed, unit_t, perm, shuffle = lax.optimization_barrier(
        (far, mixed, unit_t, perm, shuffle)
    )
    keep_left, send_left = lefts[:2], lefts[2:]
    far_near = swap(far, "img", n_img, 1)
    far_copy, mixed = call(
        functools.partial(partial_kernel, 2),
        "partial",
        6,
        [("vmem", ctx), ("vmem", mixed), ("vmem", far)],
        [("hbm", block, bf16), ("vmem", (rows, width), f32)],
        [dma((1,))],
    )
    stats = [((rows, width), bf16), ((rows, slots), f32)]
    message = slots * 2 * images
    far_near_copy, *kept_stats, out = call(
        functools.partial(forward_kernel, images, factor, 3),
        "forward",
        20,
        [
            ("vmem", ctx), ("vmem", mixed), ("vmem", cot), ("free", unit_t), ("free", perm),
            ("vmem", far_near),
        ],
        [("hbm", block, bf16)]
        + [("vmem", *s) for s in stats]
        + [("vmem", (message, width), bf16)],
        [dma((1,))],
    )

    got = lax.all_to_all(out.reshape(n_exp, -1, width), "exp", 0, 0, tiled=True)
    got = got.reshape(-1, width)
    got, first, second = lax.optimization_barrier((got, expert_in, expert_out))
    across = swap(got, "img", n_img, 2)
    first, second = call(
        fetch_kernel,
        "weights",
        4,
        [("hbm", first), ("hbm", second)],
        [("vmem", (owned - 1,) + first.shape[1:], bf16), ("vmem", second.shape, bf16)],
        [dma((2,))],
    )
    got, across, first, second = lax.optimization_barrier((got, across, first, second))
    near = swap(got, "img", n_img, 1)
    diagonal = swap(across, "img", n_img, 1)

    kept = [((owned * 2, count, width), bf16)] + [((owned, count, hidden), bf16)] * 2
    returned = (far_img * got.shape[0], width)
    slot_rows, act, grad_pre, keep, send = call(
        expert_kernel,
        "experts",
        16,
        [("vmem", x) for x in (got, near, across, diagonal)]
        + [("free", shuffle), ("vmem", early), ("vmem", first), ("vmem", second)],
        [("hbm", *s) for s in kept] + [("vmem", returned, bf16)] * 2,
        [
            *[pltpu.VMEM(*s) for s in kept],
            pltpu.VMEM((owned * 2, count, width), bf16),
            dma((3,)),
        ],
    )
    groups = [
        [(2 * x + c) * n_exp + e for x in range(far_img) for e in range(n_exp)] for c in range(2)
    ]
    near = swap(send, "img", n_img, 1)
    (back,) = call(
        pair_kernel,
        "pair",
        4,
        [("vmem", keep), ("vmem", near)],
        [("vmem", (far_img,) + got.shape, bf16)],
    )
    back = back.reshape(far_img * n_exp, -1, width)
    back = lax.all_to_all(
        back, ("img", "exp"), 0, 0, axis_index_groups=groups, tiled=True
    )

    cuts = 2
    grad_expert_in, grad_expert_out, left_p, cot = call(
        functools.partial(grads_kernel, cuts),
        "expert_grads",
        20,
        [("hbm", x) for x in (slot_rows, act, grad_pre, send_left[0], flat_cot)],
        [("hbm", expert_in.shape, bf16), ("hbm", expert_out.shape, bf16), ("vmem", left, bf16)]
        + [("vmem", (rows, width), bf16)],
        [
            *[pltpu.VMEM(*s) for s in kept],
            pltpu.VMEM(expert_in.shape, bf16),
            pltpu.VMEM(expert_out.shape, bf16),
            dma((5 + 2 * owned * cuts,)),
        ],
    )
    back, grad_expert_in, grad_expert_out, left_p, cot = lax.optimization_barrier(
        (back, grad_expert_in, grad_expert_out, left_p, cot)
    )

    n = width // 2
    grad_residual, send, side = call(
        functools.partial(backward_kernel, images, factor),
        "backward",
        24,
        [("vmem", back.reshape(far_img, -1, width)), ("free", perm), ("free", unit_t)]
        + [("vmem", x) for x in (*kept_stats, cot, left_p)]
        + [("hbm", send_left[1])],
        [
            ("hbm", (rows, width), bf16),
            ("vmem", (2 * n + 4 * slots, half), bf16),
            ("vmem", (2 * slots, half), f32),
        ],
        [
            pltpu.VMEM(left, bf16),
            pltpu.VMEM((rows, width), bf16),
            dma((1 + images,)),
        ],
    )

    got = swap(send, "img", n_img, 1)
    (keep,) = call(
        keep_kernel,
        "keep",
        8,
        [("hbm", x) for x in (*keep_left, grad_residual)],
        [("vmem", (2 * n, half), bf16)],
        [pltpu.VMEM(left, bf16), pltpu.VMEM(left, bf16), pltpu.VMEM((rows, width), bf16), dma((3,))],
    )

    def after(n):
        rest = (("vmem", (n, half), bf16),) * 2 + (("vmem", (slots, half), f32),)
        return [*rest, ("vmem", (n, half), bf16), ("vmem", (n + 2 * slots, half), bf16)]

    n = n // 2
    p, q, side, send_p, send_q = call(
        first_kernel,
        "first",
        6,
        [("vmem", keep), ("vmem", side), ("vmem", got)],
        after(n),
    )
    got_p = swap(send_p, "img", n_img, 2)
    got_q = swap(send_q, "exp", n_exp, 1)
    projection = (proj_weight, near_copy, far_copy, far_near_copy)
    (grad_context,) = call(
        context_kernel,
        "context",
        12,
        [("hbm", x) for x in (grad_residual, *projection)],
        [("hbm", (rows, width), bf16)],
        [
            pltpu.VMEM((rows, width), bf16),
            pltpu.VMEM((n_img,) + block, bf16),
            pltpu.VMEM((n_img, rows, deep), bf16),
            dma((1 + 2 * n_img,)),
        ],
    )
    got_p, got_q, grad_context = lax.optimization_barrier((got_p, got_q, grad_context))
    n = n // 2
    p, q, side, send_p, send_q = call(
        second_kernel, "second", 4, [("vmem", x) for x in (p, q, side, got_p, got_q)], after(n)
    )
    got_p = swap(send_p, "exp", n_exp, 1)
    got_q = swap(send_q, "img", n_img, 2)
    groups = n_exp // 2
    n = n // groups
    piece = slots // groups
    tail = -(-2 * piece // 8) * 8
    block = (2 * n + tail, half)
    keep, side, *sends = call(
        third_kernel,
        "third",
        4,
        [("vmem", x) for x in (p, q, side, got_p, got_q)],
        [("vmem", (2 * n, half), f32), ("vmem", (piece, half), f32)]
        + [("vmem", block, bf16)] * (groups - 1),
    )
    gots = [swap(s, "exp", n_exp, 2 * m) for m, s in enumerate(sends, 1)]
    (held,) = call(
        fourth_kernel,
        "fourth",
        4,
        [("vmem", x) for x in (keep, side, *gots)],
        [("vmem", block, bf16)],
    )
    held = [held] + [swap(held, "exp", n_exp, 2 * m) for m in range(1, groups)]
    others = [swap(x, "exp", n_exp, 1) for x in held]
    grad_proj, side = call(
        functools.partial(settle_kernel, piece),
        "settle",
        6,
        [("vmem", x) for x in held],
        [("hbm", (n_exp, n, width), f32), ("vmem", (n_exp, piece, half), f32)],
        [pltpu.VMEM((groups, n, width), f32), dma((groups,))],
    )
    grad_proj, grad_slots = call(
        functools.partial(last_kernel, piece),
        "last",
        6,
        [("vmem", x) for x in (side, *others)]
        + [("free", unit_t32), ("free", slot_norm), ("hbm", grad_proj)],
        [("hbm", (n_exp, n, width), f32), ("hbm", (slots, width), f32)],
        [
            pltpu.VMEM((n_exp, piece, half), f32),
            pltpu.VMEM((groups, n, width), f32),
            pltpu.VMEM((slots, width), f32),
            dma((groups + 1,)),
        ],
        {groups + 3: 0},
    )
    return (
        grad_context.reshape(images, tokens, width),
        grad_residual.reshape(images, tokens, width),
        grad_proj.reshape(-1, width),
        grad_slots.T,
        grad_expert_in,
        grad_expert_out,
    )


def solution(mesh):
    n_img, n_exp = mesh.shape["img"], mesh.shape["exp"]
    placed = (
        P(("img", "exp"), None, None),
        P(("img", "exp"), None, None),
        P(("img", "exp"), None, None),
        P("img", None),
        P(),
        P("exp", None, "img"),
        P("exp", "img", None),
    )
    return jax.shard_map(
        functools.partial(shards, n_img, n_exp),
        mesh=mesh,
        in_specs=placed,
        out_specs=(
            P(("img", "exp"), None, None),
            P(("img", "exp"), None, None),
            P("img", None),
            P(),
            P("exp", None, "img"),
            P("exp", "img", None),
        ),
        check_vma=False,
    )
```

```python
import functools
import math

import jax
import jax.numpy as jnp
import numpy as np
from jax import lax
from jax.experimental import pallas as pl
from jax.experimental.pallas import tpu as pltpu
from jax.sharding import PartitionSpec as P

logit_scale = 48.0
epsilon = 1e-06
f32 = jnp.float32
bf16 = jnp.bfloat16
spaces = {"vmem": pltpu.VMEM, "hbm": pltpu.HBM, "free": pltpu.VMEM}


def call(kernel, name, mib, inputs, outputs, scratch=(), aliases=()):
    def held(where, x):
        fixed = where in ("vmem", "hbm")
        return pltpu.with_memory_space_constraint(x, spaces[where]) if fixed else x

    return pl.pallas_call(
        kernel,
        in_specs=[pl.BlockSpec(memory_space=spaces[where]) for where, _ in inputs],
        out_specs=[pl.BlockSpec(memory_space=spaces[where]) for where, _, _ in outputs],
        out_shape=[spaces[where](s, t) for where, s, t in outputs],
        scratch_shapes=list(scratch),
        input_output_aliases=dict(aliases),
        compiler_params=pltpu.CompilerParams(vmem_limit_bytes=mib * 1024 * 1024),
        name=name,
    )(*[held(where, x) for where, x in inputs])


def fetch_kernel(*refs):
    n = len(refs) // 2
    mover = Mover(refs[-1])
    pairs = zip(refs[:n], refs[n : 2 * n], strict=True)
    tails = [(x.at[pl.ds(x.shape[0] - y.shape[0], y.shape[0])], y) for x, y in pairs]
    for copy in [mover.start(x, y) for x, y in tails]:
        copy.wait()


def swap(x, axis, size, bit):
    return lax.ppermute(x, axis, [(i, i ^ bit) for i in range(size)])


def tree(parts):
    while len(parts) > 1:
        parts = [parts[k] + parts[k + 1] for k in range(0, len(parts), 2)]
    return parts[0]


def dot(a, b):
    return jnp.dot(a, b, preferred_element_type=f32)


def dot_last(a, b):
    return lax.dot_general(a, b, (((1,), (1,)), ((), ())), preferred_element_type=f32)


def dot_first(a, b):
    return lax.dot_general(a, b, (((0,), (0,)), ((), ())), preferred_element_type=f32)


def one_hot(order):
    return (jnp.asarray(order, jnp.int32)[:, None] == jnp.arange(order.size)).astype(bf16)


def halves(x):
    n = x.shape[0] // 2
    return x[:n], x[n:]


def high_low(x):
    high = x.astype(bf16).astype(f32)
    return jnp.concatenate([high, (x - high).astype(bf16).astype(f32)], axis=0)


def joined(x):
    high, low = halves(x)
    return high + low


def gelu_both(pre):
    scale = math.sqrt(2.0 / math.pi)
    square = pre * pre
    bent = jnp.tanh(scale * (pre + 0.044715 * (square * pre)))
    cdf = 0.5 * (1.0 + bent)
    slope = 0.5 * (1.0 - bent * bent) * (scale * (1.0 + (3 * 0.044715) * square))
    return pre * cdf, cdf + pre * slope


class Mover:
    def __init__(self, sems):
        self.sems, self.used = sems, 0

    def start(self, source, target):
        copy = pltpu.make_async_copy(source, target, self.sems.at[self.used])
        self.used += 1
        copy.start()
        return copy


def prepare_kernel(n_img, n_exp, ctx_hbm, res_hbm, cot_hbm, own_hbm, first_hbm, near, *refs):
    lefts, near_out, mixed, ctx, cot, early = refs[:4], *refs[4:9]
    res, own, turned, kept, sems = refs[9:]
    mover = Mover(sems)
    get_ctx = mover.start(ctx_hbm, ctx)
    get_own = mover.start(own_hbm, own)
    get_res = mover.start(res_hbm, res)
    out = [mover.start(near, near_out), mover.start(cot_hbm, cot)]
    sub = turned.shape[0] // (n_img * n_exp)
    get_ctx.wait()
    turned[...] = ctx[...].astype(f32).T
    for core in range(2):
        for x in range(2):
            for y in range(2):
                block = []
                for z in range(n_exp // 2):
                    at = ((lax.axis_index("img") ^ (2 * x + core)) * n_exp + (lax.axis_index("exp") ^ (2 * z + y))) * sub
                    block.append(turned[pl.ds(pl.multiple_of(at, sub), sub), :])
                block = jnp.concatenate(block, axis=0).astype(bf16)
                n = block.shape[0]
                kept[2 * core, (2 * x + y) * n : (2 * x + y + 1) * n, :] = block
                kept[2 * core + 1, (2 * y + x) * n : (2 * y + x + 1) * n, :] = block
    out += [mover.start(kept.at[k], left) for k, left in enumerate(lefts)]
    get_own.wait()
    get_res.wait()
    deep = own.shape[0]
    first = pl.ds(pl.multiple_of(lax.axis_index("img") * deep, deep), deep)
    second = pl.ds(pl.multiple_of((lax.axis_index("img") ^ 1) * deep, deep), deep)
    mixed[...] = res[...].astype(f32) + dot(ctx[:, first], own[...]) + dot(ctx[:, second], near[...])
    out.append(mover.start(first_hbm.at[pl.ds(0, early.shape[0])], early))
    for copy in out:
        copy.wait()


def partial_kernel(taken, ctx, start, block, block_out, total, sems):
    deep = block.shape[0]
    columns = pl.ds(pl.multiple_of((lax.axis_index("img") ^ taken) * deep, deep), deep)
    out = Mover(sems).start(block, block_out)
    total[...] = start[...] + dot(ctx[:, columns], block[...])
    out.wait()


def inverse_of(stream32):
    return lax.rsqrt(jnp.mean(stream32 * stream32, axis=-1, keepdims=True) + epsilon)


def softmaxes(expo):
    dispatch32 = expo / jnp.sum(expo, axis=0, keepdims=True)
    return dispatch32, expo / jnp.sum(expo, axis=1, keepdims=True)


def forward_kernel(images, factor, taken, ctx, start, cot, unit, perm, block, *refs):
    block_out, stream_v, expo_v, slots_v, sems = refs
    mover = Mover(sems)
    deep = block.shape[0]
    tokens = cot.shape[0] // images
    columns = pl.ds(pl.multiple_of((lax.axis_index("img") ^ taken) * deep, deep), deep)
    out = [mover.start(block, block_out)]
    slot_in, grad_out = [], []
    for b in range(images):
        at = pl.ds(b * tokens, tokens)
        mixed = start[at, :] + dot(ctx[at, columns], block[...])
        stream = mixed.astype(bf16)
        stream_v[at, :] = stream
        stream32 = stream.astype(f32)
        inverse = inverse_of(stream32)
        normed = (stream32 * inverse).astype(bf16)
        expo = jnp.exp(factor * dot_last(normed, unit[...]))
        dispatch32, combine32 = softmaxes(expo)
        expo_v[at, :] = expo
        slot_in.append(dot_first(dispatch32.astype(bf16), normed).astype(bf16))
        grad_out.append(dot_first(combine32.astype(bf16), cot[at, :]).astype(bf16))
    parts = jnp.concatenate(slot_in + grad_out, axis=0)
    slots_v[...] = dot_first(perm[...], parts).astype(bf16)
    for copy in out:
        copy.wait()


def expert_kernel(own, near, across, diagonal, perm, early, first, second, *refs):
    rows_hbm, act_hbm, grad_hbm, keep, send = refs[:5]
    rows, act, grad_pre, held, sems = refs[5:]
    mover = Mover(sems)
    owned = second.shape[0]
    early_count = early.shape[0]
    got = jnp.concatenate([own[...], across[...], near[...], diagonal[...]], axis=0)
    rows[...] = dot(perm[...], got).astype(bf16).reshape(rows.shape)
    out = [mover.start(rows, rows_hbm)]
    for j in range(owned):
        first_w = early[j] if j < early_count else first[j - early_count]
        second_w = second[j]
        value, slope = gelu_both(dot(rows[2 * j], first_w))
        value = value.astype(bf16)
        act[j] = value
        grad = (dot_last(rows[2 * j + 1], second_w) * slope).astype(bf16)
        grad_pre[j] = grad
        held[2 * j] = dot(value, second_w).astype(bf16)
        held[2 * j + 1] = dot_last(grad, first_w).astype(bf16)
    out.append(mover.start(act, act_hbm))
    out.append(mover.start(grad_pre, grad_hbm))
    back = dot_first(perm[...], held[...].reshape(got.shape)).astype(bf16)
    keep[...], send[...] = halves(back)
    for copy in out:
        copy.wait()


def pair_kernel(keep, got, out):
    n = out.shape[1]
    for x in range(out.shape[0]):
        at = pl.ds(x * n, n)
        total = keep[at, :].astype(f32) + got[at, :].astype(f32)
        out[(lax.axis_index("img") >> 1) ^ x] = total.astype(bf16)


def grads_kernel(cuts, rows_hbm, act_hbm, grad_hbm, left_hbm, cot_hbm, *refs):
    first_hbm, second_hbm, left, cot = refs[:4]
    refs = refs[4:]
    rows, act, grad_pre, first, second, sems = refs
    mover = Mover(sems)
    sources = (rows_hbm, act_hbm, grad_hbm)
    gets = [mover.start(x, y) for x, y in zip(sources, refs[:3], strict=True)]
    out = [mover.start(left_hbm, left), mover.start(cot_hbm, cot)]
    for get in gets:
        get.wait()
    for j in range(first.shape[0]):
        pairs = ((second, second_hbm, act[j], rows[2 * j + 1]), (first, first_hbm, rows[2 * j], grad_pre[j]))
        for made, made_hbm, a, b in pairs:
            deep = made.shape[1] // cuts
            for k in range(cuts):
                at = slice(k * deep, (k + 1) * deep)
                made[j, at, :] = dot_first(a[:, at], b).astype(bf16)
                out.append(mover.start(made.at[j, at, :], made_hbm.at[j, at, :]))
    for copy in out:
        copy.wait()


def backward_kernel(images, factor, back, perm, unit_t, *refs):
    stream, expo, cot, left_p, left_q_hbm, *keep_hbm = refs[:7]
    grad_v, send_p, send_q, side_out, *keep_left = refs[7:13]
    left_q, sems = refs[13:]
    mover = Mover(sems)
    get = mover.start(left_q_hbm, left_q)
    gets = [mover.start(*pair) for pair in zip(keep_hbm, keep_left, strict=True)]
    tokens = cot.shape[0] // images
    slots = unit_t.shape[0]
    half = send_p.shape[1]
    total = tree([back[r].astype(f32) for r in range(back.shape[0])]).astype(bf16)
    parts = dot(perm[...], total).astype(bf16)
    unit_sum = 0.0
    for b in range(images):
        at = pl.ds(b * tokens, tokens)
        slot_out = parts[b * slots : (b + 1) * slots]
        grad_slot_in = parts[(images + b) * slots : (images + b + 1) * slots]
        upstream = cot[at, :]
        stream32 = stream[at, :].astype(f32)
        inv = inverse_of(stream32)
        normed32 = stream32 * inv
        normed = normed32.astype(bf16)
        dispatch32, combine32 = softmaxes(expo[at, :])
        grad_combine = dot_last(upstream, slot_out)
        grad_dispatch = dot_last(normed, grad_slot_in)
        logits = combine32 * (
            grad_combine - jnp.sum(combine32 * grad_combine, axis=1, keepdims=True)
        ) + dispatch32 * (
            grad_dispatch - jnp.sum(dispatch32 * grad_dispatch, axis=0, keepdims=True)
        )
        logits = logits.astype(bf16)
        grad_normed = dot(dispatch32.astype(bf16), grad_slot_in) + factor * dot(logits, unit_t[...])
        unit_sum = unit_sum + dot_first(logits, normed)
        grad = upstream.astype(f32) + inv * (
            grad_normed - normed32 * jnp.mean(normed32 * grad_normed, axis=-1, keepdims=True)
        )
        grad_v[at, :] = grad.astype(bf16)
    n = left_p.shape[0]
    send_p[...] = dot(left_p[...], grad_v[:, :half]).astype(bf16)
    get.wait()
    send_q[:n, :] = dot(left_q[...], grad_v[:, half:]).astype(bf16)
    unit_sum = factor * unit_sum
    side = high_low(jnp.concatenate([unit_sum[:, :half], unit_sum[:, half:]], axis=0))
    send_q[n:, :] = side.astype(bf16)
    for get in gets:
        get.wait()
    side_out[...] = joined(side)


def keep_kernel(left_p, left_q, grad, out_p, out_q):
    half = out_p.shape[1]
    out_p[...] = dot(left_p[...], grad[:, :half]).astype(bf16)
    out_q[...] = dot(left_q[...], grad[:, half:]).astype(bf16)


def chosen(bit, low, high):
    return jnp.where(bit == 0, low, high)


def first_p_kernel(keep, got, out, send):
    kept, sent = halves(keep[...].astype(f32) + got[...].astype(f32))
    out[...], send[...] = kept.astype(bf16), sent.astype(bf16)


def first_q_kernel(keep, side, got, out, side_out, send):
    n = keep.shape[0]
    got = got[...].astype(f32)
    kept, sent = halves(keep[...].astype(f32) + got[:n])
    low, high = halves(side[...] + joined(got[n:]))
    bit = lax.axis_index("exp") & 1
    side_out[...] = chosen(bit, low, high)
    out[...] = kept.astype(bf16)
    other = high_low(chosen(bit, high, low))
    send[...] = jnp.concatenate([sent, other], axis=0).astype(bf16)


def second_kernel(p_in, q_in, side, got_p, got_q, p_out, q_out, side_out, send_p, send_q):
    n = p_in.shape[0]
    got = got_q[...].astype(f32)
    p0, p1 = halves(p_in[...].astype(f32) + got_p[...].astype(f32))
    q0, q1 = halves(q_in[...].astype(f32) + got[:n])
    mine = high_low(side[...] + joined(got[n:]))
    side_out[...] = joined(mine)
    p_out[...] = p0.astype(bf16)
    q_out[...] = q0.astype(bf16)
    send_p[...] = p1.astype(bf16)
    send_q[...] = jnp.concatenate([q1, mine], axis=0).astype(bf16)


def side_rows(piece):
    piece = high_low(piece)
    short = -piece.shape[0] % 8
    if short:
        piece = jnp.concatenate([piece, jnp.zeros((short, piece.shape[1]), f32)], axis=0)
    return piece


def third_kernel(p_in, q_in, side, got_p, got_q, keep, side_out, *sends):
    n = p_in.shape[0]
    groups = len(sends) + 1
    got = got_q[...].astype(f32)
    p = p_in[...].astype(f32) + got_p[...].astype(f32)
    q = q_in[...].astype(f32) + got[:n]
    total = side[...] + joined(got[n:])
    deep = total.shape[0] // groups
    pieces = [total[m * deep : (m + 1) * deep] for m in range(groups)]
    bit = 1
    while bit < groups:
        flip = lax.axis_index("exp") & (2 * bit)
        pieces = [chosen(flip, pieces[m], pieces[m ^ bit]) for m in range(groups)]
        bit *= 2
    side_out[...] = pieces[0]
    n = n // groups
    keep[...] = jnp.concatenate([p[:n], q[:n]], axis=0)
    for m, send in enumerate(sends, 1):
        at = slice(m * n, (m + 1) * n)
        send[...] = jnp.concatenate([p[at], q[at], side_rows(pieces[m])], axis=0).astype(bf16)


def fourth_kernel(keep, side, *refs):
    gots, own = refs[:-1], refs[-1]
    n, deep = keep.shape[0], side.shape[0]
    gots = [g[...].astype(f32) for g in gots]
    total = tree([side[...]] + [joined(g[n : n + 2 * deep]) for g in gots])
    total = jnp.concatenate([tree([keep[...]] + [g[:n] for g in gots]), side_rows(total)], axis=0)
    own[...] = total.astype(bf16)


def context_kernel(grad, own_hbm, near_hbm, far_hbm, far_near_hbm, *refs):
    out_hbm, grad_hbm, blocks, out, sems = refs
    mover = Mover(sems)
    deep = blocks.shape[1]
    sources = (own_hbm, near_hbm, far_hbm, far_near_hbm)
    gets = [mover.start(source, blocks.at[r]) for r, source in enumerate(sources)]
    puts = [mover.start(grad, grad_hbm)]
    for r, get in enumerate(gets):
        get.wait()
        columns = pl.ds(pl.multiple_of((lax.axis_index("img") ^ r) * deep, deep), deep)
        out[r] = dot_last(grad[...], blocks[r]).astype(bf16)
        puts.append(mover.start(out.at[r], out_hbm.at[:, columns]))
    for put in puts:
        put.wait()


def settle(y, blocks, grad_hbm, side, grad, mover, deep):
    groups = len(blocks)
    n, half = grad.shape[1], blocks[0].shape[1]
    puts = []
    for z in range(groups):
        block = blocks[z][...].astype(f32)
        at = lax.axis_index("exp") ^ (2 * z + y)
        grad[z, :, :half] = block[:n]
        grad[z, :, half:] = block[n : 2 * n]
        puts.append(mover.start(grad.at[z], grad_hbm.at[at]))
        side[(at & 1) * groups + (at >> 1)] = joined(block[2 * n : 2 * n + 2 * deep])
    return puts


def settle_kernel(deep, *refs):
    blocks, (grad_hbm, side, grad, sems) = refs[:-4], refs[-4:]
    for put in settle(0, blocks, grad_hbm, side, grad, Mover(sems), deep):
        put.wait()


def last_kernel(deep, early, *refs):
    blocks, refs = refs[:-9], refs[-9:]
    unit_t, slot_norm, _, grad_hbm, slots_hbm, side, grad, slots_out, sems = refs
    mover = Mover(sems)
    side[...] = early[...]
    puts = settle(1, blocks, grad_hbm, side, grad, mover, deep)
    total = jnp.concatenate([side[k] for k in range(side.shape[0])], axis=0)
    total = jnp.concatenate(halves(total), axis=1)
    unit = unit_t[...]
    along = jnp.sum(unit * total, axis=1, keepdims=True)
    slots_out[...] = (total - unit * along) / slot_norm[...]
    puts.append(mover.start(slots_out, slots_hbm))
    for put in puts:
        put.wait()


def shards(n_img, n_exp, context, residual, cotangent, proj_weight, slot_params, expert_in, expert_out):
    images, tokens, width = context.shape
    rows = images * tokens
    owned, _, hidden = expert_in.shape
    slots = slot_params.shape[1]
    half = width // 2
    factor = logit_scale / math.sqrt(width)
    flat_ctx = context.reshape(rows, width)
    flat_cot = cotangent.reshape(rows, width)
    flat_res = residual.reshape(rows, width)
    dma = pltpu.SemaphoreType.DMA

    far = swap(proj_weight, "img", n_img, 2)
    perm = one_hot(
        np.arange(slots * 2 * images).reshape(slots, 2, images).transpose(1, 2, 0).reshape(-1)
    )
    proj_again, perm = lax.optimization_barrier((proj_weight, perm))
    near = swap(proj_again, "img", n_img, 1)
    deep = proj_weight.shape[0]
    block = (deep, width)
    left = (width // 2, rows)
    early = (1,) + expert_in.shape[1:]
    *lefts, near_copy, mixed, ctx, cot, early = call(
        functools.partial(prepare_kernel, n_img, n_exp),
        "prepare",
        16,
        [("hbm", x) for x in (flat_ctx, flat_res, flat_cot, proj_weight, expert_in)]
        + [("vmem", near)],
        [("hbm", left, bf16)] * 4
        + [("hbm", block, bf16), ("vmem", (rows, width), f32)]
        + [("vmem", (rows, width), bf16)] * 2
        + [("vmem", early, bf16)],
        [
            pltpu.VMEM((rows, width), bf16),
            pltpu.VMEM(block, bf16),
            pltpu.VMEM((width, rows), f32),
            pltpu.VMEM((4,) + left, bf16),
            dma((10,)),
        ],
    )
    params32 = slot_params.astype(f32).T
    slot_norm = jnp.sqrt(jnp.sum(params32 * params32, axis=1, keepdims=True) + epsilon)
    unit_t32 = params32 / slot_norm
    unit_t = unit_t32.astype(bf16)
    sources = n_img * n_exp
    far_img = n_img // 2
    count = sources * images
    shuffle = one_hot(
        np.arange(count * owned * 2)
        .reshape(sources, owned, 2, images)
        .transpose(1, 2, 0, 3)
        .reshape(-1)
    )
    far, mixed, unit_t, perm, shuffle = lax.optimization_barrier(
        (far, mixed, unit_t, perm, shuffle)
    )
    keep_left, send_left = lefts[:2], lefts[2:]
    far_near = swap(far, "img", n_img, 1)
    far_copy, mixed = call(
        functools.partial(partial_kernel, 2),
        "partial",
        6,
        [("vmem", ctx), ("vmem", mixed), ("vmem", far)],
        [("hbm", block, bf16), ("vmem", (rows, width), f32)],
        [dma((1,))],
    )
    stats = [((rows, width), bf16), ((rows, slots), f32)]
    message = slots * 2 * images
    far_near_copy, *kept_stats, out = call(
        functools.partial(forward_kernel, images, factor, 3),
        "forward",
        20,
        [
            ("vmem", ctx), ("vmem", mixed), ("vmem", cot), ("free", unit_t), ("free", perm),
            ("vmem", far_near),
        ],
        [("hbm", block, bf16)]
        + [("vmem", *s) for s in stats]
        + [("vmem", (message, width), bf16)],
        [dma((1,))],
    )

    got = lax.all_to_all(out.reshape(n_exp, -1, width), "exp", 0, 0, tiled=True)
    got = got.reshape(-1, width)
    got, first, second = lax.optimization_barrier((got, expert_in, expert_out))
    across = swap(got, "img", n_img, 2)
    first, second = call(
        fetch_kernel,
        "weights",
        4,
        [("hbm", first), ("hbm", second)],
        [("vmem", (owned - 1,) + first.shape[1:], bf16), ("vmem", second.shape, bf16)],
        [dma((2,))],
    )
    got, across, first, second = lax.optimization_barrier((got, across, first, second))
    near = swap(got, "img", n_img, 1)
    diagonal = swap(across, "img", n_img, 1)

    kept = [((owned * 2, count, width), bf16)] + [((owned, count, hidden), bf16)] * 2
    returned = (far_img * got.shape[0], width)
    slot_rows, act, grad_pre, keep, send = call(
        expert_kernel,
        "experts",
        16,
        [("vmem", x) for x in (got, near, across, diagonal)]
        + [("free", shuffle), ("vmem", early), ("vmem", first), ("vmem", second)],
        [("hbm", *s) for s in kept] + [("vmem", returned, bf16)] * 2,
        [
            *[pltpu.VMEM(*s) for s in kept],
            pltpu.VMEM((owned * 2, count, width), bf16),
            dma((3,)),
        ],
    )
    groups = [
        [(2 * x + c) * n_exp + e for x in range(far_img) for e in range(n_exp)] for c in range(2)
    ]
    near = swap(send, "img", n_img, 1)
    (back,) = call(
        pair_kernel,
        "pair",
        4,
        [("vmem", keep), ("vmem", near)],
        [("vmem", (far_img,) + got.shape, bf16)],
    )
    back = back.reshape(far_img * n_exp, -1, width)
    back = lax.all_to_all(
        back, ("img", "exp"), 0, 0, axis_index_groups=groups, tiled=True
    )

    cuts = 2
    grad_expert_in, grad_expert_out, left_p, cot = call(
        functools.partial(grads_kernel, cuts),
        "expert_grads",
        20,
        [("hbm", x) for x in (slot_rows, act, grad_pre, send_left[0], flat_cot)],
        [("hbm", expert_in.shape, bf16), ("hbm", expert_out.shape, bf16), ("vmem", left, bf16)]
        + [("vmem", (rows, width), bf16)],
        [
            *[pltpu.VMEM(*s) for s in kept],
            pltpu.VMEM(expert_in.shape, bf16),
            pltpu.VMEM(expert_out.shape, bf16),
            dma((5 + 2 * owned * cuts,)),
        ],
    )
    back, grad_expert_in, grad_expert_out, left_p, cot = lax.optimization_barrier(
        (back, grad_expert_in, grad_expert_out, left_p, cot)
    )

    n = width // 2
    grad, send_p, send_q, side, *keep_left = call(
        functools.partial(backward_kernel, images, factor),
        "backward",
        24,
        [("vmem", back.reshape(far_img, -1, width)), ("free", perm), ("free", unit_t)]
        + [("vmem", x) for x in (*kept_stats, cot, left_p)]
        + [("hbm", x) for x in (send_left[1], *keep_left)],
        [
            ("vmem", (rows, width), bf16),
            ("vmem", (n, half), bf16),
            ("vmem", (n + 4 * slots, half), bf16),
            ("vmem", (2 * slots, half), f32),
            ("vmem", left, bf16),
            ("vmem", left, bf16),
        ],
        [
            pltpu.VMEM(left, bf16),
            dma((3,)),
        ],
    )

    got_p = swap(send_p, "img", n_img, 1)
    got_q = swap(send_q, "img", n_img, 1)
    keep_p, keep_q = call(
        keep_kernel,
        "keep",
        4,
        [("vmem", x) for x in (*keep_left, grad)],
        [("vmem", (n, half), bf16)] * 2,
    )

    def after(n):
        rest = (("vmem", (n, half), bf16),) * 2 + (("vmem", (slots, half), f32),)
        return [*rest, ("vmem", (n, half), bf16), ("vmem", (n + 2 * slots, half), bf16)]

    n = n // 2
    part = ("vmem", (n, half), bf16)
    p, send_p = call(
        first_p_kernel, "first_p", 4, [("vmem", keep_p), ("vmem", got_p)], [part, part]
    )
    q, side, send_q = call(
        first_q_kernel,
        "first_q",
        4,
        [("vmem", x) for x in (keep_q, side, got_q)],
        [part, ("vmem", (slots, half), f32), ("vmem", (n + 2 * slots, half), bf16)],
    )
    got_p = swap(send_p, "img", n_img, 2)
    got_q = swap(send_q, "exp", n_exp, 1)
    projection = (proj_weight, near_copy, far_copy, far_near_copy)
    grad_context, grad_residual = call(
        context_kernel,
        "context",
        12,
        [("vmem", grad)] + [("hbm", x) for x in projection],
        [("hbm", (rows, width), bf16)] * 2,
        [
            pltpu.VMEM((n_img,) + block, bf16),
            pltpu.VMEM((n_img, rows, deep), bf16),
            dma((2 * n_img + 1,)),
        ],
    )
    got_p, got_q, grad_context, grad_residual = lax.optimization_barrier(
        (got_p, got_q, grad_context, grad_residual)
    )
    n = n // 2
    p, q, side, send_p, send_q = call(
        second_kernel, "second", 4, [("vmem", x) for x in (p, q, side, got_p, got_q)], after(n)
    )
    got_p = swap(send_p, "exp", n_exp, 1)
    got_q = swap(send_q, "img", n_img, 2)
    groups = n_exp // 2
    n = n // groups
    piece = slots // groups
    tail = -(-2 * piece // 8) * 8
    block = (2 * n + tail, half)
    keep, side, *sends = call(
        third_kernel,
        "third",
        4,
        [("vmem", x) for x in (p, q, side, got_p, got_q)],
        [("vmem", (2 * n, half), f32), ("vmem", (piece, half), f32)]
        + [("vmem", block, bf16)] * (groups - 1),
    )
    gots = [swap(s, "exp", n_exp, 2 * m) for m, s in enumerate(sends, 1)]
    (held,) = call(
        fourth_kernel,
        "fourth",
        4,
        [("vmem", x) for x in (keep, side, *gots)],
        [("vmem", block, bf16)],
    )
    held = [held] + [swap(held, "exp", n_exp, 2 * m) for m in range(1, groups)]
    others = [swap(x, "exp", n_exp, 1) for x in held]
    grad_proj, side = call(
        functools.partial(settle_kernel, piece),
        "settle",
        6,
        [("vmem", x) for x in held],
        [("hbm", (n_exp, n, width), f32), ("vmem", (n_exp, piece, half), f32)],
        [pltpu.VMEM((groups, n, width), f32), dma((groups,))],
    )
    grad_proj, grad_slots = call(
        functools.partial(last_kernel, piece),
        "last",
        6,
        [("vmem", x) for x in (side, *others)]
        + [("free", unit_t32), ("free", slot_norm), ("hbm", grad_proj)],
        [("hbm", (n_exp, n, width), f32), ("hbm", (slots, width), f32)],
        [
            pltpu.VMEM((n_exp, piece, half), f32),
            pltpu.VMEM((groups, n, width), f32),
            pltpu.VMEM((slots, width), f32),
            dma((groups + 1,)),
        ],
        {groups + 3: 0},
    )
    return (
        grad_context.reshape(images, tokens, width),
        grad_residual.reshape(images, tokens, width),
        grad_proj.reshape(-1, width),
        grad_slots.T,
        grad_expert_in,
        grad_expert_out,
    )


def solution(mesh):
    n_img, n_exp = mesh.shape["img"], mesh.shape["exp"]
    placed = (
        P(("img", "exp"), None, None),
        P(("img", "exp"), None, None),
        P(("img", "exp"), None, None),
        P("img", None),
        P(),
        P("exp", None, "img"),
        P("exp", "img", None),
    )
    return jax.shard_map(
        functools.partial(shards, n_img, n_exp),
        mesh=mesh,
        in_specs=placed,
        out_specs=(
            P(("img", "exp"), None, None),
            P(("img", "exp"), None, None),
            P("img", None),
            P(),
            P("exp", None, "img"),
            P("exp", "img", None),
        ),
        check_vma=False,
    )
```

```python
import functools
import math

import jax
import jax.numpy as jnp
import numpy as np
from jax import lax
from jax.experimental import pallas as pl
from jax.experimental.pallas import tpu as pltpu
from jax.sharding import PartitionSpec as P

logit_scale = 48.0
epsilon = 1e-06
f32 = jnp.float32
bf16 = jnp.bfloat16
spaces = {"vmem": pltpu.VMEM, "hbm": pltpu.HBM, "free": pltpu.VMEM}


def call(kernel, name, mib, inputs, outputs, scratch=(), aliases=()):
    def held(where, x):
        fixed = where in ("vmem", "hbm")
        return pltpu.with_memory_space_constraint(x, spaces[where]) if fixed else x

    return pl.pallas_call(
        kernel,
        in_specs=[pl.BlockSpec(memory_space=spaces[where]) for where, _ in inputs],
        out_specs=[pl.BlockSpec(memory_space=spaces[where]) for where, _, _ in outputs],
        out_shape=[spaces[where](s, t) for where, s, t in outputs],
        scratch_shapes=list(scratch),
        input_output_aliases=dict(aliases),
        compiler_params=pltpu.CompilerParams(vmem_limit_bytes=mib * 1024 * 1024),
        name=name,
    )(*[held(where, x) for where, x in inputs])


def fetch_kernel(*refs):
    n = len(refs) // 2
    mover = Mover(refs[-1])
    pairs = zip(refs[:n], refs[n : 2 * n], strict=True)
    tails = [(x.at[pl.ds(x.shape[0] - y.shape[0], y.shape[0])], y) for x, y in pairs]
    for copy in [mover.start(x, y) for x, y in tails]:
        copy.wait()


def swap(x, axis, size, bit):
    return lax.ppermute(x, axis, [(i, i ^ bit) for i in range(size)])


def tree(parts):
    while len(parts) > 1:
        parts = [parts[k] + parts[k + 1] for k in range(0, len(parts), 2)]
    return parts[0]


def dot(a, b):
    return jnp.dot(a, b, preferred_element_type=f32)


def dot_last(a, b):
    return lax.dot_general(a, b, (((1,), (1,)), ((), ())), preferred_element_type=f32)


def dot_first(a, b):
    return lax.dot_general(a, b, (((0,), (0,)), ((), ())), preferred_element_type=f32)


def one_hot(order):
    return (jnp.asarray(order, jnp.int32)[:, None] == jnp.arange(order.size)).astype(bf16)


def halves(x):
    n = x.shape[0] // 2
    return x[:n], x[n:]


def high_low(x):
    high = x.astype(bf16).astype(f32)
    return jnp.concatenate([high, (x - high).astype(bf16).astype(f32)], axis=0)


def joined(x):
    high, low = halves(x)
    return high + low


def gelu_both(pre):
    scale = math.sqrt(2.0 / math.pi)
    square = pre * pre
    bent = jnp.tanh(scale * (pre + 0.044715 * (square * pre)))
    cdf = 0.5 * (1.0 + bent)
    slope = 0.5 * (1.0 - bent * bent) * (scale * (1.0 + (3 * 0.044715) * square))
    return pre * cdf, cdf + pre * slope


class Mover:
    def __init__(self, sems):
        self.sems, self.used = sems, 0

    def start(self, source, target):
        copy = pltpu.make_async_copy(source, target, self.sems.at[self.used])
        self.used += 1
        copy.start()
        return copy


def prepare_kernel(n_img, n_exp, ctx_hbm, res_hbm, cot_hbm, own_hbm, first_hbm, near, *refs):
    lefts, near_out, mixed, ctx, cot, early = refs[:4], *refs[4:9]
    res, own, turned, kept, sems = refs[9:]
    mover = Mover(sems)
    get_ctx = mover.start(ctx_hbm, ctx)
    get_own = mover.start(own_hbm, own)
    get_res = mover.start(res_hbm, res)
    out = [mover.start(near, near_out), mover.start(cot_hbm, cot)]
    sub = turned.shape[0] // (n_img * n_exp)
    get_ctx.wait()
    turned[...] = ctx[...].astype(f32).T
    for core in range(2):
        for x in range(2):
            for y in range(2):
                block = []
                for z in range(n_exp // 2):
                    at = ((lax.axis_index("img") ^ (2 * x + core)) * n_exp + (lax.axis_index("exp") ^ (2 * z + y))) * sub
                    block.append(turned[pl.ds(pl.multiple_of(at, sub), sub), :])
                block = jnp.concatenate(block, axis=0).astype(bf16)
                n = block.shape[0]
                kept[2 * core, (2 * x + y) * n : (2 * x + y + 1) * n, :] = block
                kept[2 * core + 1, (2 * y + x) * n : (2 * y + x + 1) * n, :] = block
    out += [mover.start(kept.at[k], left) for k, left in enumerate(lefts)]
    get_own.wait()
    get_res.wait()
    deep = own.shape[0]
    first = pl.ds(pl.multiple_of(lax.axis_index("img") * deep, deep), deep)
    second = pl.ds(pl.multiple_of((lax.axis_index("img") ^ 1) * deep, deep), deep)
    mixed[...] = res[...].astype(f32) + dot(ctx[:, first], own[...]) + dot(ctx[:, second], near[...])
    out.append(mover.start(first_hbm.at[pl.ds(0, early.shape[0])], early))
    for copy in out:
        copy.wait()


def partial_kernel(taken, ctx, start, block, block_out, total, sems):
    deep = block.shape[0]
    columns = pl.ds(pl.multiple_of((lax.axis_index("img") ^ taken) * deep, deep), deep)
    out = Mover(sems).start(block, block_out)
    total[...] = start[...] + dot(ctx[:, columns], block[...])
    out.wait()


def inverse_of(stream32):
    return lax.rsqrt(jnp.mean(stream32 * stream32, axis=-1, keepdims=True) + epsilon)


def softmaxes(expo):
    dispatch32 = expo / jnp.sum(expo, axis=0, keepdims=True)
    return dispatch32, expo / jnp.sum(expo, axis=1, keepdims=True)


def forward_kernel(images, factor, taken, ctx, start, cot, unit, perm, block, *refs):
    block_out, stream_v, expo_v, slots_v, sems = refs
    mover = Mover(sems)
    deep = block.shape[0]
    tokens = cot.shape[0] // images
    columns = pl.ds(pl.multiple_of((lax.axis_index("img") ^ taken) * deep, deep), deep)
    out = [mover.start(block, block_out)]
    slot_in, grad_out = [], []
    for b in range(images):
        at = pl.ds(b * tokens, tokens)
        mixed = start[at, :] + dot(ctx[at, columns], block[...])
        stream = mixed.astype(bf16)
        stream_v[at, :] = stream
        stream32 = stream.astype(f32)
        inverse = inverse_of(stream32)
        normed = (stream32 * inverse).astype(bf16)
        expo = jnp.exp(factor * dot_last(normed, unit[...]))
        dispatch32, combine32 = softmaxes(expo)
        expo_v[at, :] = expo
        slot_in.append(dot_first(dispatch32.astype(bf16), normed).astype(bf16))
        grad_out.append(dot_first(combine32.astype(bf16), cot[at, :]).astype(bf16))
    parts = jnp.concatenate(slot_in + grad_out, axis=0)
    slots_v[...] = dot_first(perm[...], parts).astype(bf16)
    for copy in out:
        copy.wait()


def expert_kernel(own, near, across, diagonal, perm, early, first, second, *refs):
    rows_hbm, act_hbm, grad_hbm, keep, send = refs[:5]
    rows, act, grad_pre, held, sems = refs[5:]
    mover = Mover(sems)
    owned = second.shape[0]
    early_count = early.shape[0]
    got = jnp.concatenate([own[...], across[...], near[...], diagonal[...]], axis=0)
    rows[...] = dot(perm[...], got).astype(bf16).reshape(rows.shape)
    out = [mover.start(rows, rows_hbm)]
    for j in range(owned):
        first_w = early[j] if j < early_count else first[j - early_count]
        second_w = second[j]
        value, slope = gelu_both(dot(rows[2 * j], first_w))
        value = value.astype(bf16)
        act[j] = value
        grad = (dot_last(rows[2 * j + 1], second_w) * slope).astype(bf16)
        grad_pre[j] = grad
        held[2 * j] = dot(value, second_w).astype(bf16)
        held[2 * j + 1] = dot_last(grad, first_w).astype(bf16)
    out.append(mover.start(act, act_hbm))
    out.append(mover.start(grad_pre, grad_hbm))
    back = dot_first(perm[...], held[...].reshape(got.shape)).astype(bf16)
    keep[...], send[...] = halves(back)
    for copy in out:
        copy.wait()


def pair_kernel(keep, got, out):
    n = out.shape[1]
    for x in range(out.shape[0]):
        at = pl.ds(x * n, n)
        total = keep[at, :].astype(f32) + got[at, :].astype(f32)
        out[(lax.axis_index("img") >> 1) ^ x] = total.astype(bf16)


def grads_kernel(cuts, rows_hbm, act_hbm, grad_hbm, left_hbm, cot_hbm, *refs):
    first_hbm, second_hbm, left, cot = refs[:4]
    refs = refs[4:]
    rows, act, grad_pre, first, second, sems = refs
    mover = Mover(sems)
    sources = (rows_hbm, act_hbm, grad_hbm)
    gets = [mover.start(x, y) for x, y in zip(sources, refs[:3], strict=True)]
    out = [mover.start(left_hbm, left), mover.start(cot_hbm, cot)]
    for get in gets:
        get.wait()
    for j in range(first.shape[0]):
        pairs = ((second, second_hbm, act[j], rows[2 * j + 1]), (first, first_hbm, rows[2 * j], grad_pre[j]))
        for made, made_hbm, a, b in pairs:
            deep = made.shape[1] // cuts
            for k in range(cuts):
                at = slice(k * deep, (k + 1) * deep)
                made[j, at, :] = dot_first(a[:, at], b).astype(bf16)
                out.append(mover.start(made.at[j, at, :], made_hbm.at[j, at, :]))
    for copy in out:
        copy.wait()


def backward_kernel(images, factor, back, perm, unit_t, *refs):
    stream, expo, cot, left_p, left_q_hbm, *keep_hbm = refs[:7]
    grad_v, send_p, send_q, side_out, *keep_left = refs[7:13]
    left_q, sems = refs[13:]
    mover = Mover(sems)
    get = mover.start(left_q_hbm, left_q)
    gets = [mover.start(*pair) for pair in zip(keep_hbm, keep_left, strict=True)]
    tokens = cot.shape[0] // images
    slots = unit_t.shape[0]
    half = send_p.shape[1]
    total = tree([back[r].astype(f32) for r in range(back.shape[0])]).astype(bf16)
    parts = dot(perm[...], total).astype(bf16)
    unit_sum = 0.0
    for b in range(images):
        at = pl.ds(b * tokens, tokens)
        slot_out = parts[b * slots : (b + 1) * slots]
        grad_slot_in = parts[(images + b) * slots : (images + b + 1) * slots]
        upstream = cot[at, :]
        stream32 = stream[at, :].astype(f32)
        inv = inverse_of(stream32)
        normed32 = stream32 * inv
        normed = normed32.astype(bf16)
        dispatch32, combine32 = softmaxes(expo[at, :])
        grad_combine = dot_last(upstream, slot_out)
        grad_dispatch = dot_last(normed, grad_slot_in)
        logits = combine32 * (
            grad_combine - jnp.sum(combine32 * grad_combine, axis=1, keepdims=True)
        ) + dispatch32 * (
            grad_dispatch - jnp.sum(dispatch32 * grad_dispatch, axis=0, keepdims=True)
        )
        logits = logits.astype(bf16)
        grad_normed = dot(dispatch32.astype(bf16), grad_slot_in) + factor * dot(logits, unit_t[...])
        unit_sum = unit_sum + dot_first(logits, normed)
        grad = upstream.astype(f32) + inv * (
            grad_normed - normed32 * jnp.mean(normed32 * grad_normed, axis=-1, keepdims=True)
        )
        grad_v[at, :] = grad.astype(bf16)
    n = left_p.shape[0]
    send_p[...] = dot(left_p[...], grad_v[:, :half]).astype(bf16)
    get.wait()
    send_q[:n, :] = dot(left_q[...], grad_v[:, half:]).astype(bf16)
    unit_sum = factor * unit_sum
    side = high_low(jnp.concatenate([unit_sum[:, :half], unit_sum[:, half:]], axis=0))
    send_q[n:, :] = side.astype(bf16)
    for get in gets:
        get.wait()
    side_out[...] = joined(side)


def keep_kernel(left_p, left_q, grad, out_p, out_q):
    half = out_p.shape[1]
    out_p[...] = dot(left_p[...], grad[:, :half]).astype(bf16)
    out_q[...] = dot(left_q[...], grad[:, half:]).astype(bf16)


def chosen(bit, low, high):
    return jnp.where(bit == 0, low, high)


def first_p_kernel(keep, got, out, send):
    kept, sent = halves(keep[...].astype(f32) + got[...].astype(f32))
    out[...], send[...] = kept.astype(bf16), sent.astype(bf16)


def first_q_kernel(keep, side, got, out, side_out, send):
    n = keep.shape[0]
    got = got[...].astype(f32)
    kept, sent = halves(keep[...].astype(f32) + got[:n])
    low, high = halves(side[...] + joined(got[n:]))
    bit = lax.axis_index("exp") & 1
    side_out[...] = chosen(bit, low, high)
    out[...] = kept.astype(bf16)
    other = high_low(chosen(bit, high, low))
    send[...] = jnp.concatenate([sent, other], axis=0).astype(bf16)


def second_kernel(p_in, q_in, side, got_p, got_q, p_out, q_out, side_out, send_p, send_q):
    n = p_in.shape[0]
    got = got_q[...].astype(f32)
    p0, p1 = halves(p_in[...].astype(f32) + got_p[...].astype(f32))
    q0, q1 = halves(q_in[...].astype(f32) + got[:n])
    mine = high_low(side[...] + joined(got[n:]))
    side_out[...] = joined(mine)
    p_out[...] = p0.astype(bf16)
    q_out[...] = q0.astype(bf16)
    send_p[...] = p1.astype(bf16)
    send_q[...] = jnp.concatenate([q1, mine], axis=0).astype(bf16)


def side_rows(piece):
    piece = high_low(piece)
    short = -piece.shape[0] % 8
    if short:
        piece = jnp.concatenate([piece, jnp.zeros((short, piece.shape[1]), f32)], axis=0)
    return piece


def third_kernel(p_in, q_in, side, got_p, got_q, keep, side_out, *sends):
    n = p_in.shape[0]
    groups = len(sends) + 1
    got = got_q[...].astype(f32)
    p = p_in[...].astype(f32) + got_p[...].astype(f32)
    q = q_in[...].astype(f32) + got[:n]
    total = side[...] + joined(got[n:])
    deep = total.shape[0] // groups
    pieces = [total[m * deep : (m + 1) * deep] for m in range(groups)]
    bit = 1
    while bit < groups:
        flip = lax.axis_index("exp") & (2 * bit)
        pieces = [chosen(flip, pieces[m], pieces[m ^ bit]) for m in range(groups)]
        bit *= 2
    side_out[...] = pieces[0]
    n = n // groups
    keep[...] = jnp.concatenate([p[:n], q[:n]], axis=0)
    for m, send in enumerate(sends, 1):
        at = slice(m * n, (m + 1) * n)
        send[...] = jnp.concatenate([p[at], q[at], side_rows(pieces[m])], axis=0).astype(bf16)


def fourth_kernel(keep, side, *refs):
    gots, own = list(refs[:-1]), refs[-1]
    n, deep = keep.shape[0], side.shape[0]
    gots[0], gots[1] = gots[1], gots[0]
    gots = [g[...].astype(f32) for g in gots]
    total = tree([side[...]] + [joined(g[n : n + 2 * deep]) for g in gots])
    total = jnp.concatenate([tree([keep[...]] + [g[:n] for g in gots]), side_rows(total)], axis=0)
    own[...] = total.astype(bf16)


def context_kernel(grad, own_hbm, near_hbm, far_hbm, far_near_hbm, *refs):
    out_hbm, grad_hbm, blocks, out, sems = refs
    mover = Mover(sems)
    deep = blocks.shape[1]
    sources = (own_hbm, near_hbm, far_hbm, far_near_hbm)
    gets = [mover.start(source, blocks.at[r]) for r, source in enumerate(sources)]
    puts = [mover.start(grad, grad_hbm)]
    for r, get in enumerate(gets):
        get.wait()
        columns = pl.ds(pl.multiple_of((lax.axis_index("img") ^ r) * deep, deep), deep)
        out[r] = dot_last(grad[...], blocks[r]).astype(bf16)
        puts.append(mover.start(out.at[r], out_hbm.at[:, columns]))
    for put in puts:
        put.wait()


def settle(y, blocks, grad_hbm, side, grad, mover, deep):
    groups = len(blocks)
    n, half = grad.shape[1], blocks[0].shape[1]
    puts = []
    for z in range(groups):
        block = blocks[z][...].astype(f32)
        at = lax.axis_index("exp") ^ (2 * z + y)
        grad[z, :, :half] = block[:n]
        grad[z, :, half:] = block[n : 2 * n]
        puts.append(mover.start(grad.at[z], grad_hbm.at[at]))
        side[(at & 1) * groups + (at >> 1)] = joined(block[2 * n : 2 * n + 2 * deep])
    return puts


def settle_kernel(deep, *refs):
    blocks, (grad_hbm, side, grad, sems) = list(refs[:-4]), refs[-4:]
    blocks[1], blocks[2] = blocks[2], blocks[1]
    for put in settle(0, blocks, grad_hbm, side, grad, Mover(sems), deep):
        put.wait()


def last_kernel(deep, early, *refs):
    blocks, refs = refs[:-9], refs[-9:]
    unit_t, slot_norm, _, grad_hbm, slots_hbm, side, grad, slots_out, sems = refs
    mover = Mover(sems)
    side[...] = early[...]
    puts = settle(1, blocks, grad_hbm, side, grad, mover, deep)
    total = jnp.concatenate([side[k] for k in range(side.shape[0])], axis=0)
    total = jnp.concatenate(halves(total), axis=1)
    unit = unit_t[...]
    along = jnp.sum(unit * total, axis=1, keepdims=True)
    slots_out[...] = (total - unit * along) / slot_norm[...]
    puts.append(mover.start(slots_out, slots_hbm))
    for put in puts:
        put.wait()


def shards(n_img, n_exp, context, residual, cotangent, proj_weight, slot_params, expert_in, expert_out):
    images, tokens, width = context.shape
    rows = images * tokens
    owned, _, hidden = expert_in.shape
    slots = slot_params.shape[1]
    half = width // 2
    factor = logit_scale / math.sqrt(width)
    flat_ctx = context.reshape(rows, width)
    flat_cot = cotangent.reshape(rows, width)
    flat_res = residual.reshape(rows, width)
    dma = pltpu.SemaphoreType.DMA

    far = swap(proj_weight, "img", n_img, 2)
    perm = one_hot(
        np.arange(slots * 2 * images).reshape(slots, 2, images).transpose(1, 2, 0).reshape(-1)
    )
    proj_again, perm = lax.optimization_barrier((proj_weight, perm))
    near = swap(proj_again, "img", n_img, 1)
    deep = proj_weight.shape[0]
    block = (deep, width)
    left = (width // 2, rows)
    early = (1,) + expert_in.shape[1:]
    *lefts, near_copy, mixed, ctx, cot, early = call(
        functools.partial(prepare_kernel, n_img, n_exp),
        "prepare",
        16,
        [("hbm", x) for x in (flat_ctx, flat_res, flat_cot, proj_weight, expert_in)]
        + [("vmem", near)],
        [("hbm", left, bf16)] * 4
        + [("hbm", block, bf16), ("vmem", (rows, width), f32)]
        + [("vmem", (rows, width), bf16)] * 2
        + [("vmem", early, bf16)],
        [
            pltpu.VMEM((rows, width), bf16),
            pltpu.VMEM(block, bf16),
            pltpu.VMEM((width, rows), f32),
            pltpu.VMEM((4,) + left, bf16),
            dma((10,)),
        ],
    )
    params32 = slot_params.astype(f32).T
    slot_norm = jnp.sqrt(jnp.sum(params32 * params32, axis=1, keepdims=True) + epsilon)
    unit_t32 = params32 / slot_norm
    unit_t = unit_t32.astype(bf16)
    sources = n_img * n_exp
    far_img = n_img // 2
    count = sources * images
    shuffle = one_hot(
        np.arange(count * owned * 2)
        .reshape(sources, owned, 2, images)
        .transpose(1, 2, 0, 3)
        .reshape(-1)
    )
    far, mixed, unit_t, perm, shuffle = lax.optimization_barrier(
        (far, mixed, unit_t, perm, shuffle)
    )
    keep_left, send_left = lefts[:2], lefts[2:]
    far_near = swap(far, "img", n_img, 1)
    far_copy, mixed = call(
        functools.partial(partial_kernel, 2),
        "partial",
        6,
        [("vmem", ctx), ("vmem", mixed), ("vmem", far)],
        [("hbm", block, bf16), ("vmem", (rows, width), f32)],
        [dma((1,))],
    )
    stats = [((rows, width), bf16), ((rows, slots), f32)]
    message = slots * 2 * images
    far_near_copy, *kept_stats, out = call(
        functools.partial(forward_kernel, images, factor, 3),
        "forward",
        20,
        [
            ("vmem", ctx), ("vmem", mixed), ("vmem", cot), ("free", unit_t), ("free", perm),
            ("vmem", far_near),
        ],
        [("hbm", block, bf16)]
        + [("vmem", *s) for s in stats]
        + [("vmem", (message, width), bf16)],
        [dma((1,))],
    )

    got = lax.all_to_all(out.reshape(n_exp, -1, width), "exp", 0, 0, tiled=True)
    got = got.reshape(-1, width)
    got, first, second = lax.optimization_barrier((got, expert_in, expert_out))
    across = swap(got, "img", n_img, 2)
    first, second = call(
        fetch_kernel,
        "weights",
        4,
        [("hbm", first), ("hbm", second)],
        [("vmem", (owned - 1,) + first.shape[1:], bf16), ("vmem", second.shape, bf16)],
        [dma((2,))],
    )
    got, across, first, second = lax.optimization_barrier((got, across, first, second))
    near = swap(got, "img", n_img, 1)
    diagonal = swap(across, "img", n_img, 1)

    kept = [((owned * 2, count, width), bf16)] + [((owned, count, hidden), bf16)] * 2
    returned = (far_img * got.shape[0], width)
    slot_rows, act, grad_pre, keep, send = call(
        expert_kernel,
        "experts",
        16,
        [("vmem", x) for x in (got, near, across, diagonal)]
        + [("free", shuffle), ("vmem", early), ("vmem", first), ("vmem", second)],
        [("hbm", *s) for s in kept] + [("vmem", returned, bf16)] * 2,
        [
            *[pltpu.VMEM(*s) for s in kept],
            pltpu.VMEM((owned * 2, count, width), bf16),
            dma((3,)),
        ],
    )
    groups = [
        [(2 * x + c) * n_exp + e for x in range(far_img) for e in range(n_exp)] for c in range(2)
    ]
    near = swap(send, "img", n_img, 1)
    (back,) = call(
        pair_kernel,
        "pair",
        4,
        [("vmem", keep), ("vmem", near)],
        [("vmem", (far_img,) + got.shape, bf16)],
    )
    back = back.reshape(far_img * n_exp, -1, width)
    back = lax.all_to_all(
        back, ("img", "exp"), 0, 0, axis_index_groups=groups, tiled=True
    )

    cuts = 2
    grad_expert_in, grad_expert_out, left_p, cot = call(
        functools.partial(grads_kernel, cuts),
        "expert_grads",
        20,
        [("hbm", x) for x in (slot_rows, act, grad_pre, send_left[0], flat_cot)],
        [("hbm", expert_in.shape, bf16), ("hbm", expert_out.shape, bf16), ("vmem", left, bf16)]
        + [("vmem", (rows, width), bf16)],
        [
            *[pltpu.VMEM(*s) for s in kept],
            pltpu.VMEM(expert_in.shape, bf16),
            pltpu.VMEM(expert_out.shape, bf16),
            dma((5 + 2 * owned * cuts,)),
        ],
    )
    back, grad_expert_in, grad_expert_out, left_p, cot = lax.optimization_barrier(
        (back, grad_expert_in, grad_expert_out, left_p, cot)
    )

    n = width // 2
    grad, send_p, send_q, side, *keep_left = call(
        functools.partial(backward_kernel, images, factor),
        "backward",
        24,
        [("vmem", back.reshape(far_img, -1, width)), ("free", perm), ("free", unit_t)]
        + [("vmem", x) for x in (*kept_stats, cot, left_p)]
        + [("hbm", x) for x in (send_left[1], *keep_left)],
        [
            ("vmem", (rows, width), bf16),
            ("vmem", (n, half), bf16),
            ("vmem", (n + 4 * slots, half), bf16),
            ("vmem", (2 * slots, half), f32),
            ("vmem", left, bf16),
            ("vmem", left, bf16),
        ],
        [
            pltpu.VMEM(left, bf16),
            dma((3,)),
        ],
    )

    got_p = swap(send_p, "img", n_img, 1)
    got_q = swap(send_q, "img", n_img, 1)
    keep_p, keep_q = call(
        keep_kernel,
        "keep",
        4,
        [("vmem", x) for x in (*keep_left, grad)],
        [("vmem", (n, half), bf16)] * 2,
    )

    def after(n):
        rest = (("vmem", (n, half), bf16),) * 2 + (("vmem", (slots, half), f32),)
        return [*rest, ("vmem", (n, half), bf16), ("vmem", (n + 2 * slots, half), bf16)]

    n = n // 2
    part = ("vmem", (n, half), bf16)
    p, send_p = call(
        first_p_kernel, "first_p", 4, [("vmem", keep_p), ("vmem", got_p)], [part, part]
    )
    q, side, send_q = call(
        first_q_kernel,
        "first_q",
        4,
        [("vmem", x) for x in (keep_q, side, got_q)],
        [part, ("vmem", (slots, half), f32), ("vmem", (n + 2 * slots, half), bf16)],
    )
    got_p = swap(send_p, "img", n_img, 2)
    got_q = swap(send_q, "exp", n_exp, 1)
    projection = (proj_weight, near_copy, far_copy, far_near_copy)
    grad_context, grad_residual = call(
        context_kernel,
        "context",
        12,
        [("vmem", grad)] + [("hbm", x) for x in projection],
        [("hbm", (rows, width), bf16)] * 2,
        [
            pltpu.VMEM((n_img,) + block, bf16),
            pltpu.VMEM((n_img, rows, deep), bf16),
            dma((2 * n_img + 1,)),
        ],
    )
    got_p, got_q, grad_context, grad_residual = lax.optimization_barrier(
        (got_p, got_q, grad_context, grad_residual)
    )
    n = n // 2
    p, q, side, send_p, send_q = call(
        second_kernel, "second", 4, [("vmem", x) for x in (p, q, side, got_p, got_q)], after(n)
    )
    got_p = swap(send_p, "exp", n_exp, 1)
    got_q = swap(send_q, "img", n_img, 2)
    groups = n_exp // 2
    n = n // groups
    piece = slots // groups
    tail = -(-2 * piece // 8) * 8
    block = (2 * n + tail, half)
    keep, side, *sends = call(
        third_kernel,
        "third",
        4,
        [("vmem", x) for x in (p, q, side, got_p, got_q)],
        [("vmem", (2 * n, half), f32), ("vmem", (piece, half), f32)]
        + [("vmem", block, bf16)] * (groups - 1),
    )
    gots = [swap(s, "exp", n_exp, 2 * m) for m, s in enumerate(sends, 1)]
    (held,) = call(
        fourth_kernel,
        "fourth",
        4,
        [("vmem", x) for x in (keep, side, gots[1], gots[0], *gots[2:])],
        [("vmem", block, bf16)],
    )
    held = [held] + [swap(held, "exp", n_exp, 2 * m) for m in range(1, groups)]
    others = [swap(x, "exp", n_exp, 1) for x in held]
    grad_proj, side = call(
        functools.partial(settle_kernel, piece),
        "settle",
        6,
        [("vmem", x) for x in (held[0], held[2], held[1], *held[3:])],
        [("hbm", (n_exp, n, width), f32), ("vmem", (n_exp, piece, half), f32)],
        [pltpu.VMEM((groups, n, width), f32), dma((groups,))],
    )
    grad_proj, grad_slots = call(
        functools.partial(last_kernel, piece),
        "last",
        6,
        [("vmem", x) for x in (side, *others)]
        + [("free", unit_t32), ("free", slot_norm), ("hbm", grad_proj)],
        [("hbm", (n_exp, n, width), f32), ("hbm", (slots, width), f32)],
        [
            pltpu.VMEM((n_exp, piece, half), f32),
            pltpu.VMEM((groups, n, width), f32),
            pltpu.VMEM((slots, width), f32),
            dma((groups + 1,)),
        ],
        {groups + 3: 0},
    )
    return (
        grad_context.reshape(images, tokens, width),
        grad_residual.reshape(images, tokens, width),
        grad_proj.reshape(-1, width),
        grad_slots.T,
        grad_expert_in,
        grad_expert_out,
    )


def solution(mesh):
    n_img, n_exp = mesh.shape["img"], mesh.shape["exp"]
    placed = (
        P(("img", "exp"), None, None),
        P(("img", "exp"), None, None),
        P(("img", "exp"), None, None),
        P("img", None),
        P(),
        P("exp", None, "img"),
        P("exp", "img", None),
    )
    return jax.shard_map(
        functools.partial(shards, n_img, n_exp),
        mesh=mesh,
        in_specs=placed,
        out_specs=(
            P(("img", "exp"), None, None),
            P(("img", "exp"), None, None),
            P("img", None),
            P(),
            P("exp", None, "img"),
            P("exp", "img", None),
        ),
        check_vma=False,
    )
```

```python
import functools
import math

import jax
import jax.numpy as jnp
import numpy as np
from jax import lax
from jax.experimental import pallas as pl
from jax.experimental.pallas import tpu as pltpu
from jax.sharding import PartitionSpec as P

logit_scale = 48.0
epsilon = 1e-06
f32 = jnp.float32
bf16 = jnp.bfloat16
spaces = {"vmem": pltpu.VMEM, "hbm": pltpu.HBM, "free": pltpu.VMEM}


def call(kernel, name, mib, inputs, outputs, scratch=(), aliases=()):
    def held(where, x):
        fixed = where in ("vmem", "hbm")
        return pltpu.with_memory_space_constraint(x, spaces[where]) if fixed else x

    return pl.pallas_call(
        kernel,
        in_specs=[pl.BlockSpec(memory_space=spaces[where]) for where, _ in inputs],
        out_specs=[pl.BlockSpec(memory_space=spaces[where]) for where, _, _ in outputs],
        out_shape=[spaces[where](s, t) for where, s, t in outputs],
        scratch_shapes=list(scratch),
        input_output_aliases=dict(aliases),
        compiler_params=pltpu.CompilerParams(vmem_limit_bytes=mib * 1024 * 1024),
        name=name,
    )(*[held(where, x) for where, x in inputs])


def fetch_kernel(*refs):
    n = len(refs) // 2
    mover = Mover(refs[-1])
    pairs = zip(refs[:n], refs[n : 2 * n], strict=True)
    tails = [(x.at[pl.ds(x.shape[0] - y.shape[0], y.shape[0])], y) for x, y in pairs]
    for copy in [mover.start(x, y) for x, y in tails]:
        copy.wait()


def swap(x, axis, size, bit):
    return lax.ppermute(x, axis, [(i, i ^ bit) for i in range(size)])


def tree(parts):
    while len(parts) > 1:
        parts = [parts[k] + parts[k + 1] for k in range(0, len(parts), 2)]
    return parts[0]


def dot(a, b):
    return jnp.dot(a, b, preferred_element_type=f32)


def dot_last(a, b):
    return lax.dot_general(a, b, (((1,), (1,)), ((), ())), preferred_element_type=f32)


def dot_first(a, b):
    return lax.dot_general(a, b, (((0,), (0,)), ((), ())), preferred_element_type=f32)


def one_hot(order):
    return (jnp.asarray(order, jnp.int32)[:, None] == jnp.arange(order.size)).astype(bf16)


def halves(x):
    n = x.shape[0] // 2
    return x[:n], x[n:]


def high_low(x):
    high = x.astype(bf16).astype(f32)
    return jnp.concatenate([high, (x - high).astype(bf16).astype(f32)], axis=0)


def joined(x):
    high, low = halves(x)
    return high + low


def gelu_both(pre):
    scale = math.sqrt(2.0 / math.pi)
    square = pre * pre
    bent = jnp.tanh(scale * (pre + 0.044715 * (square * pre)))
    cdf = 0.5 * (1.0 + bent)
    slope = 0.5 * (1.0 - bent * bent) * (scale * (1.0 + (3 * 0.044715) * square))
    return pre * cdf, cdf + pre * slope


class Mover:
    def __init__(self, sems):
        self.sems, self.used = sems, 0

    def start(self, source, target):
        copy = pltpu.make_async_copy(source, target, self.sems.at[self.used])
        self.used += 1
        copy.start()
        return copy


def prepare_kernel(n_img, n_exp, ctx_hbm, res_hbm, cot_hbm, own_hbm, first_hbm, near, *refs):
    lefts, near_out, mixed, ctx, cot, early = refs[:4], *refs[4:9]
    res, own, turned, kept, sems = refs[9:]
    mover = Mover(sems)
    get_ctx = mover.start(ctx_hbm, ctx)
    get_own = mover.start(own_hbm, own)
    get_res = mover.start(res_hbm, res)
    out = [mover.start(near, near_out), mover.start(cot_hbm, cot)]
    sub = turned.shape[0] // (n_img * n_exp)
    get_ctx.wait()
    turned[...] = ctx[...].astype(f32).T
    for core in range(2):
        for x in range(2):
            for y in range(2):
                block = []
                for z in range(n_exp // 2):
                    at = ((lax.axis_index("img") ^ (2 * x + core)) * n_exp + (lax.axis_index("exp") ^ (2 * z + y))) * sub
                    block.append(turned[pl.ds(pl.multiple_of(at, sub), sub), :])
                block = jnp.concatenate(block, axis=0).astype(bf16)
                n = block.shape[0]
                kept[2 * core, (2 * x + y) * n : (2 * x + y + 1) * n, :] = block
                kept[2 * core + 1, (2 * y + x) * n : (2 * y + x + 1) * n, :] = block
    out += [mover.start(kept.at[k], left) for k, left in enumerate(lefts)]
    get_own.wait()
    get_res.wait()
    deep = own.shape[0]
    first = pl.ds(pl.multiple_of(lax.axis_index("img") * deep, deep), deep)
    second = pl.ds(pl.multiple_of((lax.axis_index("img") ^ 1) * deep, deep), deep)
    mixed[...] = res[...].astype(f32) + dot(ctx[:, first], own[...]) + dot(ctx[:, second], near[...])
    out.append(mover.start(first_hbm.at[pl.ds(0, early.shape[0])], early))
    for copy in out:
        copy.wait()


def partial_kernel(taken, ctx, start, block, block_out, total, sems):
    deep = block.shape[0]
    columns = pl.ds(pl.multiple_of((lax.axis_index("img") ^ taken) * deep, deep), deep)
    out = Mover(sems).start(block, block_out)
    total[...] = start[...] + dot(ctx[:, columns], block[...])
    out.wait()


def inverse_of(stream32):
    return lax.rsqrt(jnp.mean(stream32 * stream32, axis=-1, keepdims=True) + epsilon)


def softmaxes(expo):
    dispatch32 = expo / jnp.sum(expo, axis=0, keepdims=True)
    return dispatch32, expo / jnp.sum(expo, axis=1, keepdims=True)


def forward_kernel(images, factor, taken, ctx, start, cot, unit, perm, block, *refs):
    block_out, stream_v, expo_v, slots_v, sems = refs
    mover = Mover(sems)
    deep = block.shape[0]
    tokens = cot.shape[0] // images
    columns = pl.ds(pl.multiple_of((lax.axis_index("img") ^ taken) * deep, deep), deep)
    out = [mover.start(block, block_out)]
    slot_in, grad_out = [], []
    for b in range(images):
        at = pl.ds(b * tokens, tokens)
        mixed = start[at, :] + dot(ctx[at, columns], block[...])
        stream = mixed.astype(bf16)
        stream_v[at, :] = stream
        stream32 = stream.astype(f32)
        inverse = inverse_of(stream32)
        normed = (stream32 * inverse).astype(bf16)
        expo = jnp.exp(factor * dot_last(normed, unit[...]))
        dispatch32, combine32 = softmaxes(expo)
        expo_v[at, :] = expo
        slot_in.append(dot_first(dispatch32.astype(bf16), normed).astype(bf16))
        grad_out.append(dot_first(combine32.astype(bf16), cot[at, :]).astype(bf16))
    parts = jnp.concatenate(slot_in + grad_out, axis=0)
    slots_v[...] = dot_first(perm[...], parts).astype(bf16)
    for copy in out:
        copy.wait()


def expert_kernel(own, near, across, diagonal, perm, early, first, second, *refs):
    rows_hbm, act_hbm, grad_hbm, keep, send = refs[:5]
    rows, act, grad_pre, held, sems = refs[5:]
    mover = Mover(sems)
    owned = second.shape[0]
    early_count = early.shape[0]
    got = jnp.concatenate([own[...], across[...], near[...], diagonal[...]], axis=0)
    rows[...] = dot(perm[...], got).astype(bf16).reshape(rows.shape)
    out = [mover.start(rows, rows_hbm)]
    for j in range(owned):
        first_w = early[j] if j < early_count else first[j - early_count]
        second_w = second[j]
        value, slope = gelu_both(dot(rows[2 * j], first_w))
        value = value.astype(bf16)
        act[j] = value
        grad = (dot_last(rows[2 * j + 1], second_w) * slope).astype(bf16)
        grad_pre[j] = grad
        held[2 * j] = dot(value, second_w).astype(bf16)
        held[2 * j + 1] = dot_last(grad, first_w).astype(bf16)
    out.append(mover.start(act, act_hbm))
    out.append(mover.start(grad_pre, grad_hbm))
    back = dot_first(perm[...], held[...].reshape(got.shape)).astype(bf16)
    keep[...], send[...] = halves(back)
    for copy in out:
        copy.wait()


def pair_kernel(keep, got, out):
    n = out.shape[1]
    for x in range(out.shape[0]):
        at = pl.ds(x * n, n)
        total = keep[at, :].astype(f32) + got[at, :].astype(f32)
        out[(lax.axis_index("img") >> 1) ^ x] = total.astype(bf16)


def grads_kernel(cuts, rows_hbm, act_hbm, grad_hbm, left_hbm, cot_hbm, *refs):
    first_hbm, second_hbm, left, cot = refs[:4]
    refs = refs[4:]
    rows, act, grad_pre, first, second, sems = refs
    mover = Mover(sems)
    sources = (rows_hbm, act_hbm, grad_hbm)
    gets = [mover.start(x, y) for x, y in zip(sources, refs[:3], strict=True)]
    out = [mover.start(left_hbm, left), mover.start(cot_hbm, cot)]
    for get in gets:
        get.wait()
    for j in range(first.shape[0]):
        pairs = ((second, second_hbm, act[j], rows[2 * j + 1]), (first, first_hbm, rows[2 * j], grad_pre[j]))
        for made, made_hbm, a, b in pairs:
            deep = made.shape[1] // cuts
            for k in range(cuts):
                at = slice(k * deep, (k + 1) * deep)
                made[j, at, :] = dot_first(a[:, at], b).astype(bf16)
                out.append(mover.start(made.at[j, at, :], made_hbm.at[j, at, :]))
    for copy in out:
        copy.wait()


def backward_kernel(images, factor, back, perm, unit_t, *refs):
    stream, expo, cot, left_p, left_q_hbm, *keep_hbm = refs[:7]
    grad_v, send_p, send_q, side_out, *keep_left = refs[7:13]
    left_q, sems = refs[13:]
    mover = Mover(sems)
    get = mover.start(left_q_hbm, left_q)
    gets = [mover.start(*pair) for pair in zip(keep_hbm, keep_left, strict=True)]
    tokens = cot.shape[0] // images
    slots = unit_t.shape[0]
    half = send_p.shape[1]
    total = tree([back[r].astype(f32) for r in range(back.shape[0])]).astype(bf16)
    parts = dot(perm[...], total).astype(bf16)
    unit_sum = 0.0
    for b in range(images):
        at = pl.ds(b * tokens, tokens)
        slot_out = parts[b * slots : (b + 1) * slots]
        grad_slot_in = parts[(images + b) * slots : (images + b + 1) * slots]
        upstream = cot[at, :]
        stream32 = stream[at, :].astype(f32)
        inv = inverse_of(stream32)
        normed32 = stream32 * inv
        normed = normed32.astype(bf16)
        dispatch32, combine32 = softmaxes(expo[at, :])
        grad_combine = dot_last(upstream, slot_out)
        grad_dispatch = dot_last(normed, grad_slot_in)
        logits = combine32 * (
            grad_combine - jnp.sum(combine32 * grad_combine, axis=1, keepdims=True)
        ) + dispatch32 * (
            grad_dispatch - jnp.sum(dispatch32 * grad_dispatch, axis=0, keepdims=True)
        )
        logits = logits.astype(bf16)
        grad_normed = dot(dispatch32.astype(bf16), grad_slot_in) + factor * dot(logits, unit_t[...])
        unit_sum = unit_sum + dot_first(logits, normed)
        grad = upstream.astype(f32) + inv * (
            grad_normed - normed32 * jnp.mean(normed32 * grad_normed, axis=-1, keepdims=True)
        )
        grad_v[at, :] = grad.astype(bf16)
    n = left_p.shape[0]
    send_p[...] = dot(left_p[...], grad_v[:, :half]).astype(bf16)
    get.wait()
    send_q[:n, :] = dot(left_q[...], grad_v[:, half:]).astype(bf16)
    unit_sum = factor * unit_sum
    side = high_low(jnp.concatenate([unit_sum[:, :half], unit_sum[:, half:]], axis=0))
    send_q[n:, :] = side.astype(bf16)
    for get in gets:
        get.wait()
    side_out[...] = joined(side)


def keep_kernel(left_p, left_q, grad, out_p, out_q):
    half = out_p.shape[1]
    out_p[...] = dot(left_p[...], grad[:, :half]).astype(bf16)
    out_q[...] = dot(left_q[...], grad[:, half:]).astype(bf16)


def chosen(bit, low, high):
    return jnp.where(bit == 0, low, high)


def first_p_kernel(keep, got, out, send):
    kept, sent = halves(keep[...].astype(f32) + got[...].astype(f32))
    out[...], send[...] = kept.astype(bf16), sent.astype(bf16)


def first_q_kernel(keep, side, got, out, side_out, send):
    n = keep.shape[0]
    got = got[...].astype(f32)
    kept, sent = halves(keep[...].astype(f32) + got[:n])
    low, high = halves(side[...] + joined(got[n:]))
    bit = lax.axis_index("exp") & 1
    side_out[...] = chosen(bit, low, high)
    out[...] = kept.astype(bf16)
    other = high_low(chosen(bit, high, low))
    send[...] = jnp.concatenate([sent, other], axis=0).astype(bf16)


def second_kernel(p_in, q_in, side, got_p, got_q, p_out, q_out, side_out, send_p, send_q):
    n = p_in.shape[0]
    got = got_q[...].astype(f32)
    p0, p1 = halves(p_in[...].astype(f32) + got_p[...].astype(f32))
    q0, q1 = halves(q_in[...].astype(f32) + got[:n])
    mine = high_low(side[...] + joined(got[n:]))
    side_out[...] = joined(mine)
    p_out[...] = p0.astype(bf16)
    q_out[...] = q0.astype(bf16)
    send_p[...] = p1.astype(bf16)
    send_q[...] = jnp.concatenate([q1, mine], axis=0).astype(bf16)


def side_rows(piece):
    piece = high_low(piece)
    short = -piece.shape[0] % 8
    if short:
        piece = jnp.concatenate([piece, jnp.zeros((short, piece.shape[1]), f32)], axis=0)
    return piece


def third_kernel(p_in, q_in, side, got_p, got_q, keep, side_out, *sends):
    n = p_in.shape[0]
    groups = len(sends) + 1
    got = got_q[...].astype(f32)
    p = p_in[...].astype(f32) + got_p[...].astype(f32)
    q = q_in[...].astype(f32) + got[:n]
    total = side[...] + joined(got[n:])
    deep = total.shape[0] // groups
    pieces = [total[m * deep : (m + 1) * deep] for m in range(groups)]
    bit = 1
    while bit < groups:
        flip = lax.axis_index("exp") & (2 * bit)
        pieces = [chosen(flip, pieces[m], pieces[m ^ bit]) for m in range(groups)]
        bit *= 2
    side_out[...] = pieces[0]
    n = n // groups
    keep[...] = jnp.concatenate([p[:n], q[:n]], axis=0)
    for m, send in enumerate(sends, 1):
        at = slice(m * n, (m + 1) * n)
        send[...] = jnp.concatenate([p[at], q[at], side_rows(pieces[m])], axis=0).astype(bf16)


def fourth_kernel(keep, side, *refs):
    gots, own = list(refs[:-1]), refs[-1]
    n, deep = keep.shape[0], side.shape[0]
    gots[0], gots[1] = gots[1], gots[0]
    gots = [g[...].astype(f32) for g in gots]
    total = tree([side[...]] + [joined(g[n : n + 2 * deep]) for g in gots])
    total = jnp.concatenate([tree([keep[...]] + [g[:n] for g in gots]), side_rows(total)], axis=0)
    own[...] = total.astype(bf16)


def context_kernel(grad, own_hbm, near_hbm, far_hbm, far_near_hbm, *refs):
    out_hbm, grad_hbm, blocks, out, sems = refs
    mover = Mover(sems)
    deep = blocks.shape[1]
    sources = (own_hbm, near_hbm, far_hbm, far_near_hbm)
    gets = [mover.start(source, blocks.at[r]) for r, source in enumerate(sources)]
    puts = [mover.start(grad, grad_hbm)]
    for r, get in enumerate(gets):
        get.wait()
        columns = pl.ds(pl.multiple_of((lax.axis_index("img") ^ r) * deep, deep), deep)
        out[r] = dot_last(grad[...], blocks[r]).astype(bf16)
        puts.append(mover.start(out.at[r], out_hbm.at[:, columns]))
    for put in puts:
        put.wait()


def settle(y, blocks, grad_hbm, side, grad, mover, deep):
    groups = len(blocks)
    n, half = grad.shape[1], blocks[0].shape[1]
    puts = []
    for z in range(groups):
        block = blocks[z][...].astype(f32)
        at = lax.axis_index("exp") ^ (2 * z + y)
        grad[z, :, :half] = block[:n]
        grad[z, :, half:] = block[n : 2 * n]
        puts.append(mover.start(grad.at[z], grad_hbm.at[at]))
        side[(at & 1) * groups + (at >> 1)] = joined(block[2 * n : 2 * n + 2 * deep])
    return puts


def settle_kernel(deep, *refs):
    blocks, (grad_hbm, side, grad, sems) = list(refs[:-4]), refs[-4:]
    blocks[1], blocks[2] = blocks[2], blocks[1]
    for put in settle(0, blocks, grad_hbm, side, grad, Mover(sems), deep):
        put.wait()


def last_kernel(deep, early, *refs):
    blocks, refs = list(refs[:-9]), refs[-9:]
    blocks[1], blocks[2] = blocks[2], blocks[1]
    unit_t, slot_norm, _, grad_hbm, slots_hbm, side, grad, slots_out, sems = refs
    mover = Mover(sems)
    side[...] = early[...]
    puts = settle(1, blocks, grad_hbm, side, grad, mover, deep)
    total = jnp.concatenate([side[k] for k in range(side.shape[0])], axis=0)
    total = jnp.concatenate(halves(total), axis=1)
    unit = unit_t[...]
    along = jnp.sum(unit * total, axis=1, keepdims=True)
    slots_out[...] = (total - unit * along) / slot_norm[...]
    puts.append(mover.start(slots_out, slots_hbm))
    for put in puts:
        put.wait()


def shards(n_img, n_exp, context, residual, cotangent, proj_weight, slot_params, expert_in, expert_out):
    images, tokens, width = context.shape
    rows = images * tokens
    owned, _, hidden = expert_in.shape
    slots = slot_params.shape[1]
    half = width // 2
    factor = logit_scale / math.sqrt(width)
    flat_ctx = context.reshape(rows, width)
    flat_cot = cotangent.reshape(rows, width)
    flat_res = residual.reshape(rows, width)
    dma = pltpu.SemaphoreType.DMA

    far = swap(proj_weight, "img", n_img, 2)
    perm = one_hot(
        np.arange(slots * 2 * images).reshape(slots, 2, images).transpose(1, 2, 0).reshape(-1)
    )
    proj_again, perm = lax.optimization_barrier((proj_weight, perm))
    near = swap(proj_again, "img", n_img, 1)
    deep = proj_weight.shape[0]
    block = (deep, width)
    left = (width // 2, rows)
    early = (1,) + expert_in.shape[1:]
    *lefts, near_copy, mixed, ctx, cot, early = call(
        functools.partial(prepare_kernel, n_img, n_exp),
        "prepare",
        16,
        [("hbm", x) for x in (flat_ctx, flat_res, flat_cot, proj_weight, expert_in)]
        + [("vmem", near)],
        [("hbm", left, bf16)] * 4
        + [("hbm", block, bf16), ("vmem", (rows, width), f32)]
        + [("vmem", (rows, width), bf16)] * 2
        + [("vmem", early, bf16)],
        [
            pltpu.VMEM((rows, width), bf16),
            pltpu.VMEM(block, bf16),
            pltpu.VMEM((width, rows), f32),
            pltpu.VMEM((4,) + left, bf16),
            dma((10,)),
        ],
    )
    params32 = slot_params.astype(f32).T
    slot_norm = jnp.sqrt(jnp.sum(params32 * params32, axis=1, keepdims=True) + epsilon)
    unit_t32 = params32 / slot_norm
    unit_t = unit_t32.astype(bf16)
    sources = n_img * n_exp
    far_img = n_img // 2
    count = sources * images
    shuffle = one_hot(
        np.arange(count * owned * 2)
        .reshape(sources, owned, 2, images)
        .transpose(1, 2, 0, 3)
        .reshape(-1)
    )
    far, mixed, unit_t, perm, shuffle = lax.optimization_barrier(
        (far, mixed, unit_t, perm, shuffle)
    )
    keep_left, send_left = lefts[:2], lefts[2:]
    far_near = swap(far, "img", n_img, 1)
    far_copy, mixed = call(
        functools.partial(partial_kernel, 2),
        "partial",
        6,
        [("vmem", ctx), ("vmem", mixed), ("vmem", far)],
        [("hbm", block, bf16), ("vmem", (rows, width), f32)],
        [dma((1,))],
    )
    stats = [((rows, width), bf16), ((rows, slots), f32)]
    message = slots * 2 * images
    far_near_copy, *kept_stats, out = call(
        functools.partial(forward_kernel, images, factor, 3),
        "forward",
        20,
        [
            ("vmem", ctx), ("vmem", mixed), ("vmem", cot), ("free", unit_t), ("free", perm),
            ("vmem", far_near),
        ],
        [("hbm", block, bf16)]
        + [("vmem", *s) for s in stats]
        + [("vmem", (message, width), bf16)],
        [dma((1,))],
    )

    got = lax.all_to_all(out.reshape(n_exp, -1, width), "exp", 0, 0, tiled=True)
    got = got.reshape(-1, width)
    got, first, second = lax.optimization_barrier((got, expert_in, expert_out))
    across = swap(got, "img", n_img, 2)
    first, second = call(
        fetch_kernel,
        "weights",
        4,
        [("hbm", first), ("hbm", second)],
        [("vmem", (owned - 1,) + first.shape[1:], bf16), ("vmem", second.shape, bf16)],
        [dma((2,))],
    )
    got, across, first, second = lax.optimization_barrier((got, across, first, second))
    near = swap(got, "img", n_img, 1)
    diagonal = swap(across, "img", n_img, 1)

    kept = [((owned * 2, count, width), bf16)] + [((owned, count, hidden), bf16)] * 2
    returned = (far_img * got.shape[0], width)
    slot_rows, act, grad_pre, keep, send = call(
        expert_kernel,
        "experts",
        16,
        [("vmem", x) for x in (got, near, across, diagonal)]
        + [("free", shuffle), ("vmem", early), ("vmem", first), ("vmem", second)],
        [("hbm", *s) for s in kept] + [("vmem", returned, bf16)] * 2,
        [
            *[pltpu.VMEM(*s) for s in kept],
            pltpu.VMEM((owned * 2, count, width), bf16),
            dma((3,)),
        ],
    )
    groups = [
        [(2 * x + c) * n_exp + e for x in range(far_img) for e in range(n_exp)] for c in range(2)
    ]
    near = swap(send, "img", n_img, 1)
    (back,) = call(
        pair_kernel,
        "pair",
        4,
        [("vmem", keep), ("vmem", near)],
        [("vmem", (far_img,) + got.shape, bf16)],
    )
    back = back.reshape(far_img * n_exp, -1, width)
    back = lax.all_to_all(
        back, ("img", "exp"), 0, 0, axis_index_groups=groups, tiled=True
    )

    cuts = 2
    grad_expert_in, grad_expert_out, left_p, cot = call(
        functools.partial(grads_kernel, cuts),
        "expert_grads",
        20,
        [("hbm", x) for x in (slot_rows, act, grad_pre, send_left[0], flat_cot)],
        [("hbm", expert_in.shape, bf16), ("hbm", expert_out.shape, bf16), ("vmem", left, bf16)]
        + [("vmem", (rows, width), bf16)],
        [
            *[pltpu.VMEM(*s) for s in kept],
            pltpu.VMEM(expert_in.shape, bf16),
            pltpu.VMEM(expert_out.shape, bf16),
            dma((5 + 2 * owned * cuts,)),
        ],
    )
    back, grad_expert_in, grad_expert_out, left_p, cot = lax.optimization_barrier(
        (back, grad_expert_in, grad_expert_out, left_p, cot)
    )

    n = width // 2
    grad, send_p, send_q, side, *keep_left = call(
        functools.partial(backward_kernel, images, factor),
        "backward",
        24,
        [("vmem", back.reshape(far_img, -1, width)), ("free", perm), ("free", unit_t)]
        + [("vmem", x) for x in (*kept_stats, cot, left_p)]
        + [("hbm", x) for x in (send_left[1], *keep_left)],
        [
            ("vmem", (rows, width), bf16),
            ("vmem", (n, half), bf16),
            ("vmem", (n + 4 * slots, half), bf16),
            ("vmem", (2 * slots, half), f32),
            ("vmem", left, bf16),
            ("vmem", left, bf16),
        ],
        [
            pltpu.VMEM(left, bf16),
            dma((3,)),
        ],
    )

    got_p = swap(send_p, "img", n_img, 1)
    got_q = swap(send_q, "img", n_img, 1)
    keep_p, keep_q = call(
        keep_kernel,
        "keep",
        4,
        [("vmem", x) for x in (*keep_left, grad)],
        [("vmem", (n, half), bf16)] * 2,
    )

    def after(n):
        rest = (("vmem", (n, half), bf16),) * 2 + (("vmem", (slots, half), f32),)
        return [*rest, ("vmem", (n, half), bf16), ("vmem", (n + 2 * slots, half), bf16)]

    n = n // 2
    part = ("vmem", (n, half), bf16)
    p, send_p = call(
        first_p_kernel, "first_p", 4, [("vmem", keep_p), ("vmem", got_p)], [part, part]
    )
    q, side, send_q = call(
        first_q_kernel,
        "first_q",
        4,
        [("vmem", x) for x in (keep_q, side, got_q)],
        [part, ("vmem", (slots, half), f32), ("vmem", (n + 2 * slots, half), bf16)],
    )
    got_p = swap(send_p, "img", n_img, 2)
    got_q = swap(send_q, "exp", n_exp, 1)
    projection = (proj_weight, near_copy, far_copy, far_near_copy)
    grad_context, grad_residual = call(
        context_kernel,
        "context",
        12,
        [("vmem", grad)] + [("hbm", x) for x in projection],
        [("hbm", (rows, width), bf16)] * 2,
        [
            pltpu.VMEM((n_img,) + block, bf16),
            pltpu.VMEM((n_img, rows, deep), bf16),
            dma((2 * n_img + 1,)),
        ],
    )
    got_p, got_q, grad_context, grad_residual = lax.optimization_barrier(
        (got_p, got_q, grad_context, grad_residual)
    )
    n = n // 2
    p, q, side, send_p, send_q = call(
        second_kernel, "second", 4, [("vmem", x) for x in (p, q, side, got_p, got_q)], after(n)
    )
    got_p = swap(send_p, "exp", n_exp, 1)
    got_q = swap(send_q, "img", n_img, 2)
    groups = n_exp // 2
    n = n // groups
    piece = slots // groups
    tail = -(-2 * piece // 8) * 8
    block = (2 * n + tail, half)
    keep, side, *sends = call(
        third_kernel,
        "third",
        4,
        [("vmem", x) for x in (p, q, side, got_p, got_q)],
        [("vmem", (2 * n, half), f32), ("vmem", (piece, half), f32)]
        + [("vmem", block, bf16)] * (groups - 1),
    )
    gots = [swap(s, "exp", n_exp, 2 * m) for m, s in enumerate(sends, 1)]
    (held,) = call(
        fourth_kernel,
        "fourth",
        4,
        [("vmem", x) for x in (keep, side, gots[1], gots[0], *gots[2:])],
        [("vmem", block, bf16)],
    )
    held = [held] + [swap(held, "exp", n_exp, 2 * m) for m in range(1, groups)]
    others = [swap(x, "exp", n_exp, 1) for x in held]
    grad_proj, side = call(
        functools.partial(settle_kernel, piece),
        "settle",
        6,
        [("vmem", x) for x in (held[0], held[2], held[1], *held[3:])],
        [("hbm", (n_exp, n, width), f32), ("vmem", (n_exp, piece, half), f32)],
        [pltpu.VMEM((groups, n, width), f32), dma((groups,))],
    )
    grad_proj, grad_slots = call(
        functools.partial(last_kernel, piece),
        "last",
        6,
        [("vmem", x) for x in (side, others[0], others[2], others[1], *others[3:])]
        + [("free", unit_t32), ("free", slot_norm), ("hbm", grad_proj)],
        [("hbm", (n_exp, n, width), f32), ("hbm", (slots, width), f32)],
        [
            pltpu.VMEM((n_exp, piece, half), f32),
            pltpu.VMEM((groups, n, width), f32),
            pltpu.VMEM((slots, width), f32),
            dma((groups + 1,)),
        ],
        {groups + 3: 0},
    )
    return (
        grad_context.reshape(images, tokens, width),
        grad_residual.reshape(images, tokens, width),
        grad_proj.reshape(-1, width),
        grad_slots.T,
        grad_expert_in,
        grad_expert_out,
    )


def solution(mesh):
    n_img, n_exp = mesh.shape["img"], mesh.shape["exp"]
    placed = (
        P(("img", "exp"), None, None),
        P(("img", "exp"), None, None),
        P(("img", "exp"), None, None),
        P("img", None),
        P(),
        P("exp", None, "img"),
        P("exp", "img", None),
    )
    return jax.shard_map(
        functools.partial(shards, n_img, n_exp),
        mesh=mesh,
        in_specs=placed,
        out_specs=(
            P(("img", "exp"), None, None),
            P(("img", "exp"), None, None),
            P("img", None),
            P(),
            P("exp", None, "img"),
            P("exp", "img", None),
        ),
        check_vma=False,
    )
```
